32 devices in a mesh: dp: 4 (over x, core), expert: 8 (over z, y).
Axes of the slice: x: 2, y: 2, z: 4, core: 2. Of those that a mesh axis runs over, the one named last changes fastest.
Arguments:
- tokens: bfloat16 [768, 4096], P(('dp', 'expert')), may hold values from -6 to 6
- expert_ids: int32 [768, 8], P(('dp', 'expert')), may hold values from 0 to 15, all different within a row; in each aligned block of 24 rows (0 to 23, 24 to 47, ...) at most 24 rows name the same one
- route_weight: float32 [768, 8], P(('dp', 'expert')), may hold values from 0.05 to 0.5
- slot_of: int32 [16, 2], replicated, may hold values from 0 to 31, as said below
- swap_flag: int32 [32], P(('dp', 'expert')), may hold values from 0 to 1, as said below
- w_gate: bfloat16 [32, 4096, 512], P(('dp', 'expert')), may hold values from -0.09375 to 0.09375
- w_up: bfloat16 [32, 4096, 512], P(('dp', 'expert')), may hold values from -0.09375 to 0.09375
- w_down: bfloat16 [32, 512, 4096], P(('dp', 'expert')), may hold values from -0.1875 to 0.1875
Outputs:
- moe_out: bfloat16 [768, 4096], P(('dp', 'expert'))
The draws below stay inside these ranges and needn't reach their ends.
Inputs may be any that keep to these rules, and one draw needn't show every extreme that they name: `expert_ids`: in each aligned block of 24 rows (the rows of one device) no expert is chosen by more than 24 rows, and some expert is chosen by exactly 24 rows in some block. `slot_of`: every slot number appears exactly once. `swap_flag`: slot s = d * 8 + x pairs with the slot of dp index d XOR 1 and the same x; both slots of a pair carry the same flag.
All inputs are finite; a program needn't handle non-finite values.
Results may differ from the reference program's by a relative error of at most 0.0058.
Values may be sent and summed in bfloat16 or wider, within the bound.
No kernel may reach another device: no remote copies, remote signals or barrier semaphores. Data moves between devices by JAX's collectives and lax.ppermute only.
A program may use at most 128 MiB of HBM per device.

```python
import math
import jax
import jax.numpy as jnp
import numpy as np
from jax import lax

D = 4096
FFW = 1024
TOP = 8
T_DEV = 24
DP_RANKS = 4
EXPERT_RANKS = 8
SLOTS = 32
EXPERTS = 16
HALF = 512
CAP = 24
TOKENS = 768


def draw_slot_of(key, part):
    return jax.random.permutation(key, SLOTS).astype(jnp.int32).reshape(EXPERTS, 2)


def draw_swap_flag(key, part):
    pair_flags = jax.random.randint(key, (DP_RANKS // 2, 1, EXPERT_RANKS), 0, 2, dtype=jnp.int32)
    return jnp.broadcast_to(pair_flags, (DP_RANKS // 2, 2, EXPERT_RANKS)).reshape(SLOTS)


def steps_of(own_key, extent, split, low, largest):
    gain = 1.0
    for axis_at, blocks in split:
        steps = jax.random.uniform(jax.random.fold_in(jax.random.fold_in(own_key, 6), axis_at), (blocks,), jnp.float32, low / len(split), largest / len(split))
        gain = gain * jnp.repeat(jnp.exp(steps), extent[axis_at] // blocks).reshape((-1,) + (1,) * (len(extent) - 1 - axis_at))
    return gain


def routed_block(rng, own, number, rows, number_of, top, most, skew):
    ranking = jax.random.permutation(rng, number_of)
    crowded, common = shares(number_of, rows * top, most, skew, True), shares(number_of, rows * top, most, skew, False)
    places = jnp.arange(number_of)

    def named(lengths, rotation):
        used = int((lengths > 0).sum())
        fixed = max(1, used // 4)
        passed = fixed + (places - fixed + rotation * (used - fixed)) % max(1, number_of - fixed)
        return jnp.zeros((number_of,), jnp.int32).at[ranking[jnp.where(places < fixed, places, passed)]].set(jnp.asarray(lengths, jnp.int32))

    lengths = jnp.where(number % 4 == 0, named(crowded, number // 4), named(common, number - number // 4 - 1))
    mixed = jax.random.permutation(jax.random.fold_in(own, 3), number_of)
    donor, sink = mixed[0:number_of // 2 * 2:2], mixed[1:number_of // 2 * 2:2]
    room = jnp.minimum(lengths[donor] - 1, most - lengths[sink]) // 2
    room = jnp.where((donor == ranking[0]) | (sink == ranking[0]) | (lengths[sink] == 0), 0, jnp.maximum(room, 0))
    passed = jax.random.randint(jax.random.fold_in(own, 4), (number_of // 2,), 0, 1 << 20) % (room + 1)
    lengths = lengths.at[donor].add(-passed).at[sink].add(passed)
    items = jnp.searchsorted(jnp.cumsum(lengths), jnp.arange(rows * top), side="right").astype(jnp.int32)
    table = items.reshape(top, rows).T
    table = table[jax.random.permutation(jax.random.fold_in(own, 1), rows)]
    rotation = jax.random.randint(jax.random.fold_in(own, 2), (rows, 1), 0, top)
    return jnp.take_along_axis(table, (jnp.arange(top)[None, :] + rotation) % top, axis=1)


def shares(amount, total, bound, slope, full):
    weights = [(1 << 20) // math.isqrt(rank ** slope) + 1 for rank in range(1, amount + 1)]
    largest = bound if full else min(bound, max(-(-total // amount), total * weights[0] // sum(weights)))
    least = 1 if total - largest >= amount - 1 else 0
    counts, surplus = [largest] + [least] * (amount - 1), total - largest - least * (amount - 1)
    while surplus > 0:
        movable = [i for i in range(1, amount) if counts[i] < largest] or [i for i in range(1, amount) if counts[i] < bound]
        whole, budget = sum([weights[i] for i in movable]), surplus
        for i in movable:
            addition = min(bound - counts[i], max(1, budget * weights[i] // whole), surplus)
            counts[i] = counts[i] + addition
            surplus = surplus - addition
    return np.array(counts)


def scatter_about(key, shape, scale, bound, split=(), held_as=jnp.bfloat16):
    drawn = jax.random.normal(key, shape, jnp.float32) * scale
    if len(split) > 0:
        drawn = steps_of(key, shape, split, -0.22, 0.18) * drawn
    return jnp.clip(drawn, min=-bound, max=bound).astype(held_as)


def setup_inputs(seed: int = 0) -> dict:
    arg_keys = jax.random.split(jax.random.key(seed), 9)
    tokens = scatter_about(arg_keys[0], (TOKENS, D), 1.0, 6.0, ((0, 32),))
    expert_ids_keys = jax.random.split(jax.random.fold_in(arg_keys[1], 1), TOKENS // T_DEV)
    expert_ids_turns = jax.random.permutation(jax.random.fold_in(arg_keys[1], 3), TOKENS // T_DEV)
    expert_ids = jax.vmap(lambda own, number: routed_block(jax.random.fold_in(arg_keys[1], 2), own, number, T_DEV, EXPERTS, TOP, CAP, 2))(expert_ids_keys, expert_ids_turns).reshape((TOKENS, TOP))
    route_weight = jnp.clip(jnp.exp(math.log(0.5) - 2.3025851 * jax.random.uniform(arg_keys[2], (TOKENS, TOP), jnp.float32) ** steps_of(arg_keys[2], (TOKENS, TOP), ((0, 32),), -0.2, 0.2)), 0.05, 0.5)
    slot_of = draw_slot_of(jax.random.fold_in(arg_keys[8], 71), 0)
    swap_flag = draw_swap_flag(jax.random.fold_in(arg_keys[8], 71), 0)
    w_gate = scatter_about(arg_keys[5], (SLOTS, D, HALF), D ** -0.5, 0.09375, ((0, 32),))
    w_up = scatter_about(arg_keys[6], (SLOTS, D, HALF), D ** -0.5, 0.09375, ((0, 32),))
    w_down = scatter_about(arg_keys[7], (SLOTS, HALF, D), FFW ** -0.5, 0.1875, ((0, 32),))
    return dict(tokens=tokens, expert_ids=expert_ids, route_weight=route_weight, slot_of=slot_of, swap_flag=swap_flag, w_gate=w_gate, w_up=w_up, w_down=w_down)


def reference(tokens, expert_ids, route_weight, slot_of, swap_flag, w_gate, w_up, w_down):
    pair_count = TOKENS * TOP
    flat_ids = expert_ids.reshape(pair_count)
    flat_weight = route_weight.reshape(pair_count)
    parity = (slot_of // EXPERT_RANKS) % 2
    source_slot = (slot_of + swap_flag[slot_of] * EXPERT_RANKS * (1 - 2 * parity)).astype(jnp.int32)
    most_rows = SLOTS * CAP

    def serve_half(totals, column):
        expert = column // 2
        half_idx = column % 2
        chosen = flat_ids == expert
        pair_ids = jnp.nonzero(chosen, size=most_rows, fill_value=pair_count)[0].astype(jnp.int32)
        is_live = pair_ids < pair_count
        safe_ids = jnp.minimum(pair_ids, pair_count - 1).astype(jnp.int32)
        token_row = (safe_ids // TOP).astype(jnp.int32)
        weight_slot = source_slot[expert, half_idx]
        picked = tokens[token_row]
        gate_sum = jnp.dot(picked, w_gate[weight_slot], preferred_element_type=jnp.float32)
        up_sum = jnp.dot(picked, w_up[weight_slot], preferred_element_type=jnp.float32)
        hidden = (jax.nn.silu(gate_sum) * up_sum).astype(jnp.bfloat16)
        partial_out = jnp.dot(hidden, w_down[weight_slot], preferred_element_type=jnp.float32)
        partial_out = lax.optimization_barrier(partial_out.astype(jnp.bfloat16)).astype(jnp.float32)
        pair_scale = jnp.where(is_live, flat_weight[safe_ids], jnp.zeros_like(flat_weight[safe_ids]))
        return totals.at[token_row].add(partial_out * pair_scale[:, None]), None

    totals, unused = lax.scan(serve_half, jnp.zeros((TOKENS, D), jnp.float32), jnp.arange(2 * EXPERTS, dtype=jnp.int32))
    return totals.astype(jnp.bfloat16)
```

```python
import jax
import jax.numpy as jnp
from jax import lax
from jax.sharding import PartitionSpec as P

AXES = ("dp", "expert")


def partner(value, axis, distance):
    mask = 2**distance
    pairs = [(source, source ^ mask) for source in range(lax.axis_size(axis))]
    return lax.ppermute(value, axis, pairs)


def exchange(value):
    return lax.all_to_all(
        lax.all_to_all(value, "dp", split_axis=0, concat_axis=0, tiled=True),
        "expert",
        split_axis=1,
        concat_axis=1,
        tiled=True,
    )


def sparse(tokens, expert_ids, route_weight, slot_of, swap_flag, w_gate, w_up, w_down):
    dp_count = lax.axis_size("dp")
    ex_count = lax.axis_size("expert")
    slot_count = dp_count * ex_count
    tok_rows, model_width = tokens.shape
    top_count = expert_ids.shape[1]
    experts = slot_of.shape[0]
    capacity = 2 * tok_rows * top_count // experts
    moved_shards = partner((w_gate, w_up, w_down), "dp", 0)
    taking = swap_flag[0] == 1
    gate_w = jnp.where(taking, moved_shards[0][0], w_gate[0])
    up_w = jnp.where(taking, moved_shards[1][0], w_up[0])
    down_w = jnp.where(taking, moved_shards[2][0], w_down[0])
    pair_count = tok_rows * top_count
    flat_ids = expert_ids.reshape(pair_count)
    onehot = (flat_ids[:, None] == jnp.arange(experts, dtype=jnp.int32)).astype(jnp.int32)
    order_rank = jnp.sum((jnp.cumsum(onehot, axis=0) - onehot) * onehot, axis=1)
    dest_slot = jnp.sum(onehot[:, :, None] * slot_of[None, :, :], axis=1)
    position = dest_slot * capacity + order_rank[:, None]
    pair_ids = jnp.broadcast_to(jnp.arange(pair_count, dtype=jnp.int32)[:, None], (pair_count, 2))
    owner = (
        jnp.full((slot_count * capacity,), -1, jnp.int32)
        .at[position.reshape(-1)]
        .set(pair_ids.reshape(-1))
    )
    token_row = jnp.maximum(owner, 0) // top_count
    outbox = jnp.where((owner >= 0)[:, None], tokens[token_row], jnp.zeros((), tokens.dtype))
    outbox = outbox.reshape(dp_count, ex_count, capacity, model_width)
    arrived = exchange(outbox).reshape(slot_count * capacity, model_width)
    gate_sum = jnp.dot(arrived, gate_w, preferred_element_type=jnp.float32)
    up_sum = jnp.dot(arrived, up_w, preferred_element_type=jnp.float32)
    hidden = (jax.nn.silu(gate_sum) * up_sum).astype(jnp.bfloat16)
    partial_out = jnp.dot(hidden, down_w, preferred_element_type=jnp.float32).astype(jnp.bfloat16)
    partial_out = partial_out.reshape(dp_count, ex_count, capacity, model_width)
    returned = exchange(partial_out).reshape(slot_count * capacity, model_width)
    picked = returned[position].astype(jnp.float32)
    scaled = jnp.sum(picked, axis=1) * route_weight.reshape(pair_count)[:, None]
    return jnp.sum(scaled.reshape(tok_rows, top_count, model_width), axis=1).astype(jnp.bfloat16)


def served_expert(slot_of, swap_flag):
    d = lax.axis_index("dp")
    x = lax.axis_index("expert")
    serving = jnp.where(swap_flag[0] == 1, d ^ 1, d) * lax.axis_size("expert") + x
    numbers = jnp.arange(slot_of.shape[0], dtype=jnp.int32)[:, None]
    return jnp.sum(jnp.where(slot_of == serving, numbers, 0))


def dense(tokens, expert_ids, route_weight, slot_of, swap_flag, w_gate, w_up, w_down):
    mine = served_expert(slot_of, swap_flag)
    all_ids = lax.all_gather(expert_ids, AXES, tiled=True)
    all_weights = lax.all_gather(route_weight, AXES, tiled=True)
    scale = jnp.sum(jnp.where(all_ids == mine, all_weights, 0.0), axis=1)
    arrived = lax.all_gather(tokens, AXES, tiled=True)
    gate_sum = jnp.dot(arrived, w_gate[0], preferred_element_type=jnp.float32)
    up_sum = jnp.dot(arrived, w_up[0], preferred_element_type=jnp.float32)
    hidden = (jax.nn.silu(gate_sum) * up_sum).astype(jnp.bfloat16)
    partial_out = jnp.dot(hidden, w_down[0], preferred_element_type=jnp.float32)
    partial_out = (partial_out * scale[:, None]).astype(jnp.bfloat16)
    return lax.psum_scatter(partial_out, AXES, scatter_dimension=0, tiled=True)


def on_device(tokens, expert_ids, *rest):
    slot_of = rest[1]
    capacity = 2 * tokens.shape[0] * expert_ids.shape[1] // slot_of.shape[0]
    serve = dense if capacity >= tokens.shape[0] else sparse
    return serve(tokens, expert_ids, *rest)


def solution(mesh):
    return jax.shard_map(
        on_device,
        mesh=mesh,
        in_specs=(
            P(AXES, None),
            P(AXES, None),
            P(AXES, None),
            P(),
            P(AXES),
            P(AXES, None, None),
            P(AXES, None, None),
            P(AXES, None, None),
        ),
        out_specs=P(AXES, None),
        check_vma=False,
    )
```

```python
import jax
import jax.numpy as jnp
from jax import lax
from jax.sharding import PartitionSpec as P

AXES = ("dp", "expert")
LANES = 128


def partner(value, axis, distance):
    mask = 2**distance
    pairs = [(source, source ^ mask) for source in range(lax.axis_size(axis))]
    return lax.ppermute(value, axis, pairs)


def exchange(value):
    return lax.all_to_all(
        lax.all_to_all(value, "dp", split_axis=0, concat_axis=0, tiled=True),
        "expert",
        split_axis=1,
        concat_axis=1,
        tiled=True,
    )


def sparse(tokens, expert_ids, route_weight, slot_of, swap_flag, w_gate, w_up, w_down):
    dp_count = lax.axis_size("dp")
    ex_count = lax.axis_size("expert")
    slot_count = dp_count * ex_count
    tok_rows, model_width = tokens.shape
    top_count = expert_ids.shape[1]
    experts = slot_of.shape[0]
    capacity = 2 * tok_rows * top_count // experts
    moved_shards = partner((w_gate, w_up, w_down), "dp", 0)
    taking = swap_flag[0] == 1
    gate_w = jnp.where(taking, moved_shards[0][0], w_gate[0])
    up_w = jnp.where(taking, moved_shards[1][0], w_up[0])
    down_w = jnp.where(taking, moved_shards[2][0], w_down[0])
    pair_count = tok_rows * top_count
    flat_ids = expert_ids.reshape(pair_count)
    onehot = (flat_ids[:, None] == jnp.arange(experts, dtype=jnp.int32)).astype(jnp.int32)
    order_rank = jnp.sum((jnp.cumsum(onehot, axis=0) - onehot) * onehot, axis=1)
    dest_slot = jnp.sum(onehot[:, :, None] * slot_of[None, :, :], axis=1)
    position = dest_slot * capacity + order_rank[:, None]
    pair_ids = jnp.broadcast_to(jnp.arange(pair_count, dtype=jnp.int32)[:, None], (pair_count, 2))
    owner = (
        jnp.full((slot_count * capacity,), -1, jnp.int32)
        .at[position.reshape(-1)]
        .set(pair_ids.reshape(-1))
    )
    token_row = jnp.maximum(owner, 0) // top_count
    outbox = jnp.where((owner >= 0)[:, None], tokens[token_row], jnp.zeros((), tokens.dtype))
    outbox = outbox.reshape(dp_count, ex_count, capacity, model_width)
    arrived = exchange(outbox).reshape(slot_count * capacity, model_width)
    gate_sum = jnp.dot(arrived, gate_w, preferred_element_type=jnp.float32)
    up_sum = jnp.dot(arrived, up_w, preferred_element_type=jnp.float32)
    hidden = (jax.nn.silu(gate_sum) * up_sum).astype(jnp.bfloat16)
    partial_out = jnp.dot(hidden, down_w, preferred_element_type=jnp.float32).astype(jnp.bfloat16)
    partial_out = partial_out.reshape(dp_count, ex_count, capacity, model_width)
    returned = exchange(partial_out).reshape(slot_count * capacity, model_width)
    picked = returned[position].astype(jnp.float32)
    scaled = jnp.sum(picked, axis=1) * route_weight.reshape(pair_count)[:, None]
    return jnp.sum(scaled.reshape(tok_rows, top_count, model_width), axis=1).astype(jnp.bfloat16)


def served_expert(slot_of, swap_flag):
    d = lax.axis_index("dp")
    x = lax.axis_index("expert")
    serving = jnp.where(swap_flag[0] == 1, d ^ 1, d) * lax.axis_size("expert") + x
    numbers = jnp.arange(slot_of.shape[0], dtype=jnp.int32)[:, None]
    return jnp.sum(jnp.where(slot_of == serving, numbers, 0))


def permute(value, move):
    ex_count = lax.axis_size("expert")
    pairs = []
    for source in range(lax.axis_size("dp") * ex_count):
        d, e = divmod(source, ex_count)
        d, e = move(d, e)
        pairs.append((source, d * ex_count + e))
    return lax.ppermute(value, AXES, pairs)


def to_sibling(d, e):
    return d ^ 1, e


def over_first(d, e):
    return (d ^ 2, e) if d % 2 else (d, e ^ 1)


def over_second(d, e):
    return (d, e ^ 1) if d % 2 else (d ^ 2, e)


def along_line(distance):
    ex_count = lax.axis_size("expert")
    return lambda d, e: (d, (e + 2 * distance) % ex_count)


def packed(tokens, expert_ids, route_weight):
    top_count = expert_ids.shape[1]
    parts = []
    rest = route_weight
    for _ in range(3):
        part = lax.reduce_precision(rest, exponent_bits=8, mantissa_bits=7)
        parts.append(part.astype(jnp.bfloat16))
        rest = rest - part
    ids = expert_ids.astype(jnp.bfloat16)
    extra = jnp.concatenate([ids] + parts, axis=1)
    extra = jnp.pad(extra, ((0, 0), (0, LANES - 4 * top_count)))
    return jnp.concatenate([tokens, extra], axis=1)


def scale_of(extra, mine, top_count):
    ids = extra[:, :top_count].astype(jnp.float32)
    values = extra[:, top_count : 4 * top_count].astype(jnp.float32)
    weights = values[:, :top_count] + values[:, top_count : 2 * top_count] + values[:, 2 * top_count :]
    return jnp.sum(jnp.where(ids == mine.astype(jnp.float32), weights, 0.0), axis=1, keepdims=True)


def serve_rows(rows, mine, top_count, w_gate, w_up, w_down):
    width = w_gate.shape[0]
    arrived = rows[:, :width]
    gate_sum = jnp.dot(arrived, w_gate, preferred_element_type=jnp.float32)
    up_sum = jnp.dot(arrived, w_up, preferred_element_type=jnp.float32)
    hidden = (jax.nn.silu(gate_sum) * up_sum).astype(jnp.bfloat16)
    partial_out = jnp.dot(hidden, w_down, preferred_element_type=jnp.float32)
    return (partial_out * scale_of(rows[:, width:], mine, top_count)).astype(jnp.bfloat16)


def total(*terms):
    return sum(term.astype(jnp.float32) for term in terms).astype(jnp.bfloat16)


def dense(tokens, expert_ids, route_weight, slot_of, swap_flag, w_gate, w_up, w_down):
    tok_rows, width = tokens.shape
    top_count = expert_ids.shape[1]
    line_count = lax.axis_size("expert") // 2
    mine = served_expert(slot_of, swap_flag)
    own = packed(tokens, expert_ids, route_weight)
    line = jnp.concatenate([own] + [permute(own, along_line(k)) for k in range(1, line_count)])
    first = permute(line, over_first)
    sib_line = permute(line, to_sibling)
    early = jnp.concatenate([line, first])
    late = permute(early, over_second)
    sib_first = permute(first, to_sibling)
    sib_late = permute(late, to_sibling)

    args = (mine, top_count, w_gate[0], w_up[0], w_down[0])
    half = early.shape[0]
    out_early = serve_rows(jnp.concatenate([early, sib_line, sib_first]), *args)
    out_late = serve_rows(jnp.concatenate([late, sib_late]), *args)
    got_early = permute(out_early[half:], to_sibling)
    got_late = permute(out_late[half:], to_sibling)
    late_sum = total(out_late[:half], got_late)
    got = permute(late_sum, over_second)
    early_sum = total(out_early[:half], got_early, got)
    half = line.shape[0]
    got = permute(early_sum[half:], over_first)
    line_sum = total(early_sum[:half], got)
    terms = [line_sum[:tok_rows]]
    for k in range(1, line_count):
        terms.append(permute(line_sum[k * tok_rows : (k + 1) * tok_rows], along_line(-k)))
    return total(*terms)


def on_device(tokens, expert_ids, *rest):
    slot_of = rest[1]
    capacity = 2 * tokens.shape[0] * expert_ids.shape[1] // slot_of.shape[0]
    serve = dense if capacity >= tokens.shape[0] else sparse
    return serve(tokens, expert_ids, *rest)


def solution(mesh):
    return jax.shard_map(
        on_device,
        mesh=mesh,
        in_specs=(
            P(AXES, None),
            P(AXES, None),
            P(AXES, None),
            P(),
            P(AXES),
            P(AXES, None, None),
            P(AXES, None, None),
            P(AXES, None, None),
        ),
        out_specs=P(AXES, None),
        check_vma=False,
    )
```

```python
import jax
import jax.numpy as jnp
from jax import lax
from jax.sharding import PartitionSpec as P

AXES = ("dp", "expert")
LANES = 128


def partner(value, axis, distance):
    mask = 2**distance
    pairs = [(source, source ^ mask) for source in range(lax.axis_size(axis))]
    return lax.ppermute(value, axis, pairs)


def exchange(value):
    return lax.all_to_all(
        lax.all_to_all(value, "dp", split_axis=0, concat_axis=0, tiled=True),
        "expert",
        split_axis=1,
        concat_axis=1,
        tiled=True,
    )


def sparse(tokens, expert_ids, route_weight, slot_of, swap_flag, w_gate, w_up, w_down):
    dp_count = lax.axis_size("dp")
    ex_count = lax.axis_size("expert")
    slot_count = dp_count * ex_count
    tok_rows, model_width = tokens.shape
    top_count = expert_ids.shape[1]
    experts = slot_of.shape[0]
    capacity = 2 * tok_rows * top_count // experts
    moved_shards = partner((w_gate, w_up, w_down), "dp", 0)
    taking = swap_flag[0] == 1
    gate_w = jnp.where(taking, moved_shards[0][0], w_gate[0])
    up_w = jnp.where(taking, moved_shards[1][0], w_up[0])
    down_w = jnp.where(taking, moved_shards[2][0], w_down[0])
    pair_count = tok_rows * top_count
    flat_ids = expert_ids.reshape(pair_count)
    onehot = (flat_ids[:, None] == jnp.arange(experts, dtype=jnp.int32)).astype(jnp.int32)
    order_rank = jnp.sum((jnp.cumsum(onehot, axis=0) - onehot) * onehot, axis=1)
    dest_slot = jnp.sum(onehot[:, :, None] * slot_of[None, :, :], axis=1)
    position = dest_slot * capacity + order_rank[:, None]
    pair_ids = jnp.broadcast_to(jnp.arange(pair_count, dtype=jnp.int32)[:, None], (pair_count, 2))
    owner = (
        jnp.full((slot_count * capacity,), -1, jnp.int32)
        .at[position.reshape(-1)]
        .set(pair_ids.reshape(-1))
    )
    token_row = jnp.maximum(owner, 0) // top_count
    outbox = jnp.where((owner >= 0)[:, None], tokens[token_row], jnp.zeros((), tokens.dtype))
    outbox = outbox.reshape(dp_count, ex_count, capacity, model_width)
    arrived = exchange(outbox).reshape(slot_count * capacity, model_width)
    gate_sum = jnp.dot(arrived, gate_w, preferred_element_type=jnp.float32)
    up_sum = jnp.dot(arrived, up_w, preferred_element_type=jnp.float32)
    hidden = (jax.nn.silu(gate_sum) * up_sum).astype(jnp.bfloat16)
    partial_out = jnp.dot(hidden, down_w, preferred_element_type=jnp.float32).astype(jnp.bfloat16)
    partial_out = partial_out.reshape(dp_count, ex_count, capacity, model_width)
    returned = exchange(partial_out).reshape(slot_count * capacity, model_width)
    picked = returned[position].astype(jnp.float32)
    scaled = jnp.sum(picked, axis=1) * route_weight.reshape(pair_count)[:, None]
    return jnp.sum(scaled.reshape(tok_rows, top_count, model_width), axis=1).astype(jnp.bfloat16)


def served_expert(slot_of, swap_flag):
    d = lax.axis_index("dp")
    x = lax.axis_index("expert")
    serving = jnp.where(swap_flag[0] == 1, d ^ 1, d) * lax.axis_size("expert") + x
    numbers = jnp.arange(slot_of.shape[0], dtype=jnp.int32)[:, None]
    return jnp.sum(jnp.where(slot_of == serving, numbers, 0))


def to_sibling(d, e):
    return d ^ 1, e


def over_first(d, e):
    return (d ^ 2, e) if d % 2 else (d, e ^ 1)


def over_second(d, e):
    return (d, e ^ 1) if d % 2 else (d ^ 2, e)


def along_line(distance):
    ex_count = lax.axis_size("expert")
    return lambda d, e: (d, (e + 2 * distance) % ex_count)


def packed(tokens, expert_ids, route_weight):
    top_count = expert_ids.shape[1]
    parts = []
    rest = route_weight
    for _ in range(3):
        part = lax.reduce_precision(rest, exponent_bits=8, mantissa_bits=7)
        parts.append(part.astype(jnp.bfloat16))
        rest = rest - part
    ids = expert_ids.astype(jnp.bfloat16)
    extra = jnp.concatenate([ids] + parts, axis=1)
    extra = jnp.pad(extra, ((0, 0), (0, LANES - 4 * top_count)))
    return jnp.concatenate([tokens, extra], axis=1)


def scale_of(extra, mine, top_count):
    ids = extra[:, :top_count].astype(jnp.float32)
    values = extra[:, top_count : 4 * top_count].astype(jnp.float32)
    weights = values[:, :top_count] + values[:, top_count : 2 * top_count] + values[:, 2 * top_count :]
    return jnp.sum(jnp.where(ids == mine.astype(jnp.float32), weights, 0.0), axis=1, keepdims=True)


def serve_rows(rows, mine, top_count, w_gate, w_up, w_down):
    width = w_gate.shape[0]
    arrived = rows[:, :width]
    gate_sum = jnp.dot(arrived, w_gate, preferred_element_type=jnp.float32)
    up_sum = jnp.dot(arrived, w_up, preferred_element_type=jnp.float32)
    hidden = (jax.nn.silu(gate_sum) * up_sum).astype(jnp.bfloat16)
    partial_out = jnp.dot(hidden, w_down, preferred_element_type=jnp.float32)
    return (partial_out * scale_of(rows[:, width:], mine, top_count)).astype(jnp.bfloat16)


def groups_of(*moves):
    ex_count = lax.axis_size("expert")
    found = set()
    for source in range(lax.axis_size("dp") * ex_count):
        d, e = divmod(source, ex_count)
        found.add(tuple(sorted({source} | {a * ex_count + b for a, b in (move(d, e) for move in moves)})))
    return [list(group) for group in sorted(found)]


def dense(tokens, expert_ids, route_weight, slot_of, swap_flag, w_gate, w_up, w_down):
    top_count = expert_ids.shape[1]
    line_count = lax.axis_size("expert") // 2
    mine = served_expert(slot_of, swap_flag)
    rows = packed(tokens, expert_ids, route_weight)
    stages = [
        groups_of(*[along_line(k) for k in range(1, line_count)]),
        groups_of(over_first),
        groups_of(over_second),
        groups_of(to_sibling),
    ]
    for groups in stages:
        rows = lax.all_gather(rows, AXES, axis_index_groups=groups, tiled=True)
    out = serve_rows(rows, mine, top_count, w_gate[0], w_up[0], w_down[0])
    for groups in stages[::-1]:
        out = lax.psum_scatter(out, AXES, scatter_dimension=0, axis_index_groups=groups, tiled=True)
    return out


def on_device(tokens, expert_ids, *rest):
    slot_of = rest[1]
    capacity = 2 * tokens.shape[0] * expert_ids.shape[1] // slot_of.shape[0]
    serve = dense if capacity >= tokens.shape[0] else sparse
    return serve(tokens, expert_ids, *rest)


def solution(mesh):
    return jax.shard_map(
        on_device,
        mesh=mesh,
        in_specs=(
            P(AXES, None),
            P(AXES, None),
            P(AXES, None),
            P(),
            P(AXES),
            P(AXES, None, None),
            P(AXES, None, None),
            P(AXES, None, None),
        ),
        out_specs=P(AXES, None),
        check_vma=False,
    )
```

```python
import functools

import jax
import jax.numpy as jnp
from jax import lax
from jax.experimental import pallas as pl
from jax.experimental.pallas import tpu as pltpu
from jax.sharding import PartitionSpec as P

AXES = ("dp", "expert")
LANES = 128
PARTS = 4
ROWS_AT_ONCE = 8


def partner(value, axis, distance):
    mask = 2**distance
    pairs = [(source, source ^ mask) for source in range(lax.axis_size(axis))]
    return lax.ppermute(value, axis, pairs)


def exchange(value):
    return lax.all_to_all(
        lax.all_to_all(value, "dp", split_axis=0, concat_axis=0, tiled=True),
        "expert",
        split_axis=1,
        concat_axis=1,
        tiled=True,
    )


def sparse(tokens, expert_ids, route_weight, slot_of, swap_flag, w_gate, w_up, w_down):
    dp_count = lax.axis_size("dp")
    ex_count = lax.axis_size("expert")
    slot_count = dp_count * ex_count
    tok_rows, model_width = tokens.shape
    top_count = expert_ids.shape[1]
    experts = slot_of.shape[0]
    capacity = 2 * tok_rows * top_count // experts
    moved_shards = partner((w_gate, w_up, w_down), "dp", 0)
    taking = swap_flag[0] == 1
    gate_w = jnp.where(taking, moved_shards[0][0], w_gate[0])
    up_w = jnp.where(taking, moved_shards[1][0], w_up[0])
    down_w = jnp.where(taking, moved_shards[2][0], w_down[0])
    pair_count = tok_rows * top_count
    flat_ids = expert_ids.reshape(pair_count)
    onehot = (flat_ids[:, None] == jnp.arange(experts, dtype=jnp.int32)).astype(jnp.int32)
    order_rank = jnp.sum((jnp.cumsum(onehot, axis=0) - onehot) * onehot, axis=1)
    dest_slot = jnp.sum(onehot[:, :, None] * slot_of[None, :, :], axis=1)
    position = dest_slot * capacity + order_rank[:, None]
    pair_ids = jnp.broadcast_to(jnp.arange(pair_count, dtype=jnp.int32)[:, None], (pair_count, 2))
    owner = (
        jnp.full((slot_count * capacity,), -1, jnp.int32)
        .at[position.reshape(-1)]
        .set(pair_ids.reshape(-1))
    )
    token_row = jnp.maximum(owner, 0) // top_count
    outbox = jnp.where((owner >= 0)[:, None], tokens[token_row], jnp.zeros((), tokens.dtype))
    outbox = outbox.reshape(dp_count, ex_count, capacity, model_width)
    arrived = exchange(outbox).reshape(slot_count * capacity, model_width)
    gate_sum = jnp.dot(arrived, gate_w, preferred_element_type=jnp.float32)
    up_sum = jnp.dot(arrived, up_w, preferred_element_type=jnp.float32)
    hidden = (jax.nn.silu(gate_sum) * up_sum).astype(jnp.bfloat16)
    partial_out = jnp.dot(hidden, down_w, preferred_element_type=jnp.float32).astype(jnp.bfloat16)
    partial_out = partial_out.reshape(dp_count, ex_count, capacity, model_width)
    returned = exchange(partial_out).reshape(slot_count * capacity, model_width)
    picked = returned[position].astype(jnp.float32)
    scaled = jnp.sum(picked, axis=1) * route_weight.reshape(pair_count)[:, None]
    return jnp.sum(scaled.reshape(tok_rows, top_count, model_width), axis=1).astype(jnp.bfloat16)


def served_expert(slot_of, swap_flag):
    d = lax.axis_index("dp")
    x = lax.axis_index("expert")
    serving = jnp.where(swap_flag[0] == 1, d ^ 1, d) * lax.axis_size("expert") + x
    numbers = jnp.arange(slot_of.shape[0], dtype=jnp.int32)[:, None]
    return jnp.sum(jnp.where(slot_of == serving, numbers, 0))


def permute(value, move):
    ex_count = lax.axis_size("expert")
    pairs = []
    for source in range(lax.axis_size("dp") * ex_count):
        d, e = move(*divmod(source, ex_count))
        pairs.append((source, d * ex_count + e))
    return lax.ppermute(value, AXES, pairs)


def to_sibling(d, e):
    return d ^ 1, e


def over_first(d, e):
    return (d ^ 2, e) if d % 2 else (d, e ^ 1)


def over_second(d, e):
    return (d, e ^ 1) if d % 2 else (d ^ 2, e)


def along_line(distance):
    return lambda d, e: (d, e ^ (2 * distance))


def choices(expert_ids, route_weight):
    parts = [expert_ids.astype(jnp.bfloat16)]
    rest = route_weight
    for _ in range(3):
        part = lax.reduce_precision(rest, exponent_bits=8, mantissa_bits=7)
        parts.append(part.astype(jnp.bfloat16))
        rest = rest - part
    extra = jnp.concatenate(parts, axis=1)
    return jnp.pad(extra, ((0, 0), (0, -extra.shape[1] % LANES)))


def scale_of(extra, mine, top_count):
    extra = extra.astype(jnp.float32)
    ids, hi, mid, lo = (extra[:, k * top_count : (k + 1) * top_count] for k in range(4))
    return jnp.sum(jnp.where(ids == mine, hi + mid + lo, 0.0), axis=1, keepdims=True)


def serve_kernel(
    top_count, mine, own, sib, w_gate, w_up, w_down, out_own, out_sib, x, gate, up, down, y, in_sem, out_sem
):
    rows, packed_width = own.shape
    width, hidden_width = w_gate.shape
    depth = width // PARTS
    loads = [
        pltpu.make_async_copy(own, x.at[:rows], in_sem.at[0]),
        pltpu.make_async_copy(sib, x.at[rows:], in_sem.at[1]),
    ]
    for k in range(PARTS):
        part = pl.ds(k * depth, depth)
        loads.append(pltpu.make_async_copy(w_gate.at[part], gate.at[part], in_sem.at[2 + 2 * k]))
        loads.append(pltpu.make_async_copy(w_up.at[part], up.at[part], in_sem.at[3 + 2 * k]))
    load_down = pltpu.make_async_copy(w_down, down, in_sem.at[2 + 2 * PARTS])
    for load in loads:
        load.start()
    load_down.start()
    loads[0].wait()
    loads[1].wait()
    gate_sum = jnp.zeros((2 * rows, hidden_width), jnp.float32)
    up_sum = jnp.zeros((2 * rows, hidden_width), jnp.float32)
    for k in range(PARTS):
        part = pl.ds(k * depth, depth)
        loads[2 + 2 * k].wait()
        gate_sum += jnp.dot(x[:, part], gate[part], preferred_element_type=jnp.float32)
        loads[3 + 2 * k].wait()
        up_sum += jnp.dot(x[:, part], up[part], preferred_element_type=jnp.float32)
    hidden = (gate_sum / (1.0 + jnp.exp(-gate_sum)) * up_sum).astype(jnp.bfloat16)
    scale = scale_of(x[:, width:], mine[0].astype(jnp.float32), top_count)
    load_down.wait()
    stores = []
    for k in range(PARTS):
        part = pl.ds(k * depth, depth)
        served = jnp.dot(hidden, down[:, part], preferred_element_type=jnp.float32)
        y[:, part] = (served * scale).astype(jnp.bfloat16)
        stores.append(pltpu.make_async_copy(y.at[rows:, part], out_sib.at[:, part], out_sem.at[2 * k]))
        stores.append(pltpu.make_async_copy(y.at[:rows, part], out_own.at[:, part], out_sem.at[2 * k + 1]))
        stores[-2].start()
        stores[-1].start()
    for store in stores:
        store.wait()


def serve_rows(own, sib, mine, top_count, w_gate, w_up, w_down):
    rows, packed_width = own.shape
    width, hidden_width = w_gate.shape
    anywhere = pl.BlockSpec(memory_space=pl.ANY)
    out = jax.ShapeDtypeStruct((rows, width), jnp.bfloat16)
    moved = 2 * (4 * rows * width + 3 * width * hidden_width)
    return pl.pallas_call(
        functools.partial(serve_kernel, top_count),
        out_shape=(out, out),
        in_specs=[pl.BlockSpec(memory_space=pltpu.SMEM)] + [anywhere] * 5,
        out_specs=(anywhere, anywhere),
        scratch_shapes=[
            pltpu.VMEM((2 * rows, packed_width), jnp.bfloat16),
            pltpu.VMEM((width, hidden_width), jnp.bfloat16),
            pltpu.VMEM((width, hidden_width), jnp.bfloat16),
            pltpu.VMEM((hidden_width, width), jnp.bfloat16),
            pltpu.VMEM((2 * rows, width), jnp.bfloat16),
            pltpu.SemaphoreType.DMA((3 + 2 * PARTS,)),
            pltpu.SemaphoreType.DMA((2 * PARTS,)),
        ],
        compiler_params=pltpu.CompilerParams(vmem_limit_bytes=40 * 2**20),
        cost_estimate=pl.CostEstimate(
            flops=12 * rows * width * hidden_width, bytes_accessed=moved, transcendentals=2 * rows * hidden_width
        ),
        name="serve_rows",
    )(mine.reshape(1), own, sib, w_gate, w_up, w_down)


def total(*terms):
    return sum(term.astype(jnp.float32) for term in terms).astype(jnp.bfloat16)


def gather_and_serve(own, moves, serve):
    rows = own.shape[0]
    held = own
    for move in moves:
        held = jnp.concatenate([held, permute(held, move)])
    out, out_sib = serve(held, permute(held, to_sibling))
    terms = [out, permute(out_sib, to_sibling)]
    for move in moves[::-1]:
        half = terms[-1].shape[0] // 2
        sent = total(*[term[half : 2 * half] for term in terms])
        terms.append(permute(sent, move))
    return total(*[term[:rows] for term in terms])


def dense(tokens, expert_ids, route_weight, slot_of, swap_flag, w_gate, w_up, w_down):
    tok_rows = tokens.shape[0]
    top_count = expert_ids.shape[1]
    mine = served_expert(slot_of, swap_flag)
    line_bits = (lax.axis_size("expert") // 2).bit_length() - 1
    moves = [along_line(2**bit) for bit in range(line_bits)][::-1] + [over_first, over_second]
    step = ROWS_AT_ONCE if tok_rows % ROWS_AT_ONCE == 0 else tok_rows
    extra = choices(expert_ids, route_weight)
    outs = []
    for at in range(0, tok_rows, step):
        own = jnp.concatenate([tokens[at : at + step], extra[at : at + step]], axis=1)
        serve = lambda held, sib: serve_rows(held, sib, mine, top_count, w_gate[0], w_up[0], w_down[0])
        outs.append(gather_and_serve(own, moves, serve))
    return jnp.concatenate(outs)


def on_device(tokens, expert_ids, *rest):
    slot_of = rest[1]
    ex_count = lax.axis_size("expert")
    capacity = 2 * tokens.shape[0] * expert_ids.shape[1] // slot_of.shape[0]
    paired = lax.axis_size("dp") == 4 and ex_count >= 2 and ex_count & (ex_count - 1) == 0
    serve = dense if capacity >= tokens.shape[0] and paired else sparse
    return serve(tokens, expert_ids, *rest)


def solution(mesh):
    return jax.shard_map(
        on_device,
        mesh=mesh,
        in_specs=(
            P(AXES, None),
            P(AXES, None),
            P(AXES, None),
            P(),
            P(AXES),
            P(AXES, None, None),
            P(AXES, None, None),
            P(AXES, None, None),
        ),
        out_specs=P(AXES, None),
        check_vma=False,
    )
```

```python
import functools

import jax
import jax.numpy as jnp
from jax import lax
from jax.experimental import pallas as pl
from jax.experimental.pallas import tpu as pltpu
from jax.sharding import PartitionSpec as P

AXES = ("dp", "expert")
LANES = 128
PARTS = 4
ROWS_AT_ONCE = 8


def partner(value, axis, distance):
    mask = 2**distance
    pairs = [(source, source ^ mask) for source in range(lax.axis_size(axis))]
    return lax.ppermute(value, axis, pairs)


def exchange(value):
    return lax.all_to_all(
        lax.all_to_all(value, "dp", split_axis=0, concat_axis=0, tiled=True),
        "expert",
        split_axis=1,
        concat_axis=1,
        tiled=True,
    )


def sparse(tokens, expert_ids, route_weight, slot_of, swap_flag, w_gate, w_up, w_down):
    dp_count = lax.axis_size("dp")
    ex_count = lax.axis_size("expert")
    slot_count = dp_count * ex_count
    tok_rows, model_width = tokens.shape
    top_count = expert_ids.shape[1]
    experts = slot_of.shape[0]
    capacity = 2 * tok_rows * top_count // experts
    moved_shards = partner((w_gate, w_up, w_down), "dp", 0)
    taking = swap_flag[0] == 1
    gate_w = jnp.where(taking, moved_shards[0][0], w_gate[0])
    up_w = jnp.where(taking, moved_shards[1][0], w_up[0])
    down_w = jnp.where(taking, moved_shards[2][0], w_down[0])
    pair_count = tok_rows * top_count
    flat_ids = expert_ids.reshape(pair_count)
    onehot = (flat_ids[:, None] == jnp.arange(experts, dtype=jnp.int32)).astype(jnp.int32)
    order_rank = jnp.sum((jnp.cumsum(onehot, axis=0) - onehot) * onehot, axis=1)
    dest_slot = jnp.sum(onehot[:, :, None] * slot_of[None, :, :], axis=1)
    position = dest_slot * capacity + order_rank[:, None]
    pair_ids = jnp.broadcast_to(jnp.arange(pair_count, dtype=jnp.int32)[:, None], (pair_count, 2))
    owner = (
        jnp.full((slot_count * capacity,), -1, jnp.int32)
        .at[position.reshape(-1)]
        .set(pair_ids.reshape(-1))
    )
    token_row = jnp.maximum(owner, 0) // top_count
    outbox = jnp.where((owner >= 0)[:, None], tokens[token_row], jnp.zeros((), tokens.dtype))
    outbox = outbox.reshape(dp_count, ex_count, capacity, model_width)
    arrived = exchange(outbox).reshape(slot_count * capacity, model_width)
    gate_sum = jnp.dot(arrived, gate_w, preferred_element_type=jnp.float32)
    up_sum = jnp.dot(arrived, up_w, preferred_element_type=jnp.float32)
    hidden = (jax.nn.silu(gate_sum) * up_sum).astype(jnp.bfloat16)
    partial_out = jnp.dot(hidden, down_w, preferred_element_type=jnp.float32).astype(jnp.bfloat16)
    partial_out = partial_out.reshape(dp_count, ex_count, capacity, model_width)
    returned = exchange(partial_out).reshape(slot_count * capacity, model_width)
    picked = returned[position].astype(jnp.float32)
    scaled = jnp.sum(picked, axis=1) * route_weight.reshape(pair_count)[:, None]
    return jnp.sum(scaled.reshape(tok_rows, top_count, model_width), axis=1).astype(jnp.bfloat16)


def served_expert(slot_of, swap_flag):
    d = lax.axis_index("dp")
    x = lax.axis_index("expert")
    serving = jnp.where(swap_flag[0] == 1, d ^ 1, d) * lax.axis_size("expert") + x
    numbers = jnp.arange(slot_of.shape[0], dtype=jnp.int32)[:, None]
    return jnp.sum(jnp.where(slot_of == serving, numbers, 0))


def permute(value, move):
    ex_count = lax.axis_size("expert")
    pairs = []
    for source in range(lax.axis_size("dp") * ex_count):
        d, e = move(*divmod(source, ex_count))
        pairs.append((source, d * ex_count + e))
    return lax.ppermute(value, AXES, pairs)


def to_sibling(d, e):
    return d ^ 1, e


def over_first(d, e):
    return (d ^ 2, e) if d % 2 else (d, e ^ 1)


def over_second(d, e):
    return (d, e ^ 1) if d % 2 else (d ^ 2, e)


def along_line(distance):
    return lambda d, e: (d, e ^ (2 * distance))


def choices(expert_ids, route_weight):
    parts = [expert_ids.astype(jnp.bfloat16)]
    rest = route_weight
    for _ in range(3):
        part = lax.reduce_precision(rest, exponent_bits=8, mantissa_bits=7)
        parts.append(part.astype(jnp.bfloat16))
        rest = rest - part
    extra = jnp.concatenate(parts, axis=1)
    return jnp.pad(extra, ((0, 0), (0, -extra.shape[1] % LANES)))


def scale_of(extra, mine, top_count):
    extra = extra.astype(jnp.float32)
    ids, hi, mid, lo = (extra[:, k * top_count : (k + 1) * top_count] for k in range(4))
    return jnp.sum(jnp.where(ids == mine, hi + mid + lo, 0.0), axis=1, keepdims=True)


def serve_kernel(
    top_count, mine, own, sib, w_gate, w_up, w_down, out_own, out_sib, x, gate, up, down, y, in_sem, out_sem
):
    rows, packed_width = own.shape
    width, hidden_width = w_gate.shape
    depth = width // PARTS
    loads = [
        pltpu.make_async_copy(own, x.at[:rows], in_sem.at[0]),
        pltpu.make_async_copy(sib, x.at[rows:], in_sem.at[1]),
    ]
    for k in range(PARTS):
        part = pl.ds(k * depth, depth)
        loads.append(pltpu.make_async_copy(w_gate.at[part], gate.at[part], in_sem.at[2 + 2 * k]))
        loads.append(pltpu.make_async_copy(w_up.at[part], up.at[part], in_sem.at[3 + 2 * k]))
    load_down = pltpu.make_async_copy(w_down, down, in_sem.at[2 + 2 * PARTS])
    for load in loads:
        load.start()
    load_down.start()
    loads[0].wait()
    loads[1].wait()
    gate_sum = jnp.zeros((2 * rows, hidden_width), jnp.float32)
    up_sum = jnp.zeros((2 * rows, hidden_width), jnp.float32)
    for k in range(PARTS):
        part = pl.ds(k * depth, depth)
        loads[2 + 2 * k].wait()
        gate_sum += jnp.dot(x[:, part], gate[part], preferred_element_type=jnp.float32)
        loads[3 + 2 * k].wait()
        up_sum += jnp.dot(x[:, part], up[part], preferred_element_type=jnp.float32)
    hidden = (gate_sum / (1.0 + jnp.exp(-gate_sum)) * up_sum).astype(jnp.bfloat16)
    scale = scale_of(x[:, width:], mine[0].astype(jnp.float32), top_count)
    load_down.wait()
    stores = []
    for k in range(PARTS):
        part = pl.ds(k * depth, depth)
        served = jnp.dot(hidden, down[:, part], preferred_element_type=jnp.float32)
        y[:, part] = (served * scale).astype(jnp.bfloat16)
        stores.append(pltpu.make_async_copy(y.at[rows:, part], out_sib.at[:, part], out_sem.at[2 * k]))
        stores.append(pltpu.make_async_copy(y.at[:rows, part], out_own.at[:, part], out_sem.at[2 * k + 1]))
        stores[-2].start()
        stores[-1].start()
    for store in stores:
        store.wait()


def serve_rows(own, sib, mine, top_count, w_gate, w_up, w_down):
    rows, packed_width = own.shape
    width, hidden_width = w_gate.shape
    anywhere = pl.BlockSpec(memory_space=pl.ANY)
    out = jax.ShapeDtypeStruct((rows, width), jnp.bfloat16)
    moved = 2 * (4 * rows * width + 3 * width * hidden_width)
    return pl.pallas_call(
        functools.partial(serve_kernel, top_count),
        out_shape=(out, out),
        in_specs=[pl.BlockSpec(memory_space=pltpu.SMEM)] + [anywhere] * 5,
        out_specs=(anywhere, anywhere),
        scratch_shapes=[
            pltpu.VMEM((2 * rows, packed_width), jnp.bfloat16),
            pltpu.VMEM((width, hidden_width), jnp.bfloat16),
            pltpu.VMEM((width, hidden_width), jnp.bfloat16),
            pltpu.VMEM((hidden_width, width), jnp.bfloat16),
            pltpu.VMEM((2 * rows, width), jnp.bfloat16),
            pltpu.SemaphoreType.DMA((3 + 2 * PARTS,)),
            pltpu.SemaphoreType.DMA((2 * PARTS,)),
        ],
        compiler_params=pltpu.CompilerParams(vmem_limit_bytes=40 * 2**20),
        cost_estimate=pl.CostEstimate(
            flops=12 * rows * width * hidden_width, bytes_accessed=moved, transcendentals=2 * rows * hidden_width
        ),
        name="serve_rows",
    )(mine.reshape(1), own, sib, w_gate, w_up, w_down)


def total(*terms):
    return sum(term.astype(jnp.float32) for term in terms).astype(jnp.bfloat16)


def gather_and_serve(own, moves, serve, after):
    rows = own.shape[0]
    held = own
    marks = []
    if after is not None:
        held, _ = lax.optimization_barrier((held, after))
    for move in moves:
        got = permute(held, move)
        marks.append(got)
        held = jnp.concatenate([held, got])
    out, out_sib = serve(held, permute(held, to_sibling))
    terms = [out, permute(out_sib, to_sibling)]
    for move in moves[::-1]:
        half = terms[-1].shape[0] // 2
        sent = total(*[term[half : 2 * half] for term in terms])
        terms.append(permute(sent, move))
    return total(*[term[:rows] for term in terms]), marks[2]


def dense(tokens, expert_ids, route_weight, slot_of, swap_flag, w_gate, w_up, w_down):
    tok_rows = tokens.shape[0]
    top_count = expert_ids.shape[1]
    mine = served_expert(slot_of, swap_flag)
    line_bits = (lax.axis_size("expert") // 2).bit_length() - 1
    moves = [along_line(2**bit) for bit in range(line_bits)][::-1] + [over_first, over_second]
    step = ROWS_AT_ONCE if tok_rows % ROWS_AT_ONCE == 0 else tok_rows
    extra = choices(expert_ids, route_weight)
    outs = []
    after = None
    for at in range(0, tok_rows, step):
        own = jnp.concatenate([tokens[at : at + step], extra[at : at + step]], axis=1)
        serve = lambda held, sib: serve_rows(held, sib, mine, top_count, w_gate[0], w_up[0], w_down[0])
        out, after = gather_and_serve(own, moves, serve, after)
        outs.append(out)
    return jnp.concatenate(outs)


def on_device(tokens, expert_ids, *rest):
    slot_of = rest[1]
    ex_count = lax.axis_size("expert")
    capacity = 2 * tokens.shape[0] * expert_ids.shape[1] // slot_of.shape[0]
    paired = lax.axis_size("dp") == 4 and ex_count >= 2 and ex_count & (ex_count - 1) == 0
    serve = dense if capacity >= tokens.shape[0] and paired else sparse
    return serve(tokens, expert_ids, *rest)


def solution(mesh):
    return jax.shard_map(
        on_device,
        mesh=mesh,
        in_specs=(
            P(AXES, None),
            P(AXES, None),
            P(AXES, None),
            P(),
            P(AXES),
            P(AXES, None, None),
            P(AXES, None, None),
            P(AXES, None, None),
        ),
        out_specs=P(AXES, None),
        check_vma=False,
    )
```

```python
import functools

import jax
import jax.numpy as jnp
from jax import lax
from jax.experimental import pallas as pl
from jax.experimental.pallas import tpu as pltpu
from jax.sharding import PartitionSpec as P

AXES = ("dp", "expert")
LANES = 128
PARTS = 4
ROWS_AT_ONCE = 8
ORDER = [0, 1, 0, 1, 0, 2, 1, 0, 2, 1, 0, 2, 0, 1, 2, 0, 1, 1, 2, 0, 1, 2, 2, 0, 2, 0, 1, 2, 0, 1, 2, 1, 2, 0, 1, 2]


def partner(value, axis, distance):
    mask = 2**distance
    pairs = [(source, source ^ mask) for source in range(lax.axis_size(axis))]
    return lax.ppermute(value, axis, pairs)


def exchange(value):
    return lax.all_to_all(
        lax.all_to_all(value, "dp", split_axis=0, concat_axis=0, tiled=True),
        "expert",
        split_axis=1,
        concat_axis=1,
        tiled=True,
    )


def sparse(tokens, expert_ids, route_weight, slot_of, swap_flag, w_gate, w_up, w_down):
    dp_count = lax.axis_size("dp")
    ex_count = lax.axis_size("expert")
    slot_count = dp_count * ex_count
    tok_rows, model_width = tokens.shape
    top_count = expert_ids.shape[1]
    experts = slot_of.shape[0]
    capacity = 2 * tok_rows * top_count // experts
    moved_shards = partner((w_gate, w_up, w_down), "dp", 0)
    taking = swap_flag[0] == 1
    gate_w = jnp.where(taking, moved_shards[0][0], w_gate[0])
    up_w = jnp.where(taking, moved_shards[1][0], w_up[0])
    down_w = jnp.where(taking, moved_shards[2][0], w_down[0])
    pair_count = tok_rows * top_count
    flat_ids = expert_ids.reshape(pair_count)
    onehot = (flat_ids[:, None] == jnp.arange(experts, dtype=jnp.int32)).astype(jnp.int32)
    order_rank = jnp.sum((jnp.cumsum(onehot, axis=0) - onehot) * onehot, axis=1)
    dest_slot = jnp.sum(onehot[:, :, None] * slot_of[None, :, :], axis=1)
    position = dest_slot * capacity + order_rank[:, None]
    pair_ids = jnp.broadcast_to(jnp.arange(pair_count, dtype=jnp.int32)[:, None], (pair_count, 2))
    owner = (
        jnp.full((slot_count * capacity,), -1, jnp.int32)
        .at[position.reshape(-1)]
        .set(pair_ids.reshape(-1))
    )
    token_row = jnp.maximum(owner, 0) // top_count
    outbox = jnp.where((owner >= 0)[:, None], tokens[token_row], jnp.zeros((), tokens.dtype))
    outbox = outbox.reshape(dp_count, ex_count, capacity, model_width)
    arrived = exchange(outbox).reshape(slot_count * capacity, model_width)
    gate_sum = jnp.dot(arrived, gate_w, preferred_element_type=jnp.float32)
    up_sum = jnp.dot(arrived, up_w, preferred_element_type=jnp.float32)
    hidden = (jax.nn.silu(gate_sum) * up_sum).astype(jnp.bfloat16)
    partial_out = jnp.dot(hidden, down_w, preferred_element_type=jnp.float32).astype(jnp.bfloat16)
    partial_out = partial_out.reshape(dp_count, ex_count, capacity, model_width)
    returned = exchange(partial_out).reshape(slot_count * capacity, model_width)
    picked = returned[position].astype(jnp.float32)
    scaled = jnp.sum(picked, axis=1) * route_weight.reshape(pair_count)[:, None]
    return jnp.sum(scaled.reshape(tok_rows, top_count, model_width), axis=1).astype(jnp.bfloat16)


def served_expert(slot_of, swap_flag):
    d = lax.axis_index("dp")
    x = lax.axis_index("expert")
    serving = jnp.where(swap_flag[0] == 1, d ^ 1, d) * lax.axis_size("expert") + x
    numbers = jnp.arange(slot_of.shape[0], dtype=jnp.int32)[:, None]
    return jnp.sum(jnp.where(slot_of == serving, numbers, 0))


def permute(value, move):
    ex_count = lax.axis_size("expert")
    pairs = []
    for source in range(lax.axis_size("dp") * ex_count):
        d, e = move(*divmod(source, ex_count))
        pairs.append((source, d * ex_count + e))
    return lax.ppermute(value, AXES, pairs)


def to_sibling(d, e):
    return d ^ 1, e


def over_first(d, e):
    return (d ^ 2, e) if d % 2 else (d, e ^ 1)


def over_second(d, e):
    return (d, e ^ 1) if d % 2 else (d ^ 2, e)


def along_line(distance):
    return lambda d, e: (d, e ^ (2 * distance))


def choices(expert_ids, route_weight):
    parts = [expert_ids.astype(jnp.bfloat16)]
    rest = route_weight
    for _ in range(3):
        part = lax.reduce_precision(rest, exponent_bits=8, mantissa_bits=7)
        parts.append(part.astype(jnp.bfloat16))
        rest = rest - part
    extra = jnp.concatenate(parts, axis=1)
    return jnp.pad(extra, ((0, 0), (0, -extra.shape[1] % LANES)))


def scale_of(extra, mine, top_count):
    extra = extra.astype(jnp.float32)
    ids, hi, mid, lo = (extra[:, k * top_count : (k + 1) * top_count] for k in range(4))
    return jnp.sum(jnp.where(ids == mine, hi + mid + lo, 0.0), axis=1, keepdims=True)


def serve_kernel(
    top_count, mine, own, sib, w_gate, w_up, w_down, out_own, out_sib, x, gate, up, down, y, in_sem, out_sem
):
    rows, packed_width = own.shape
    width, hidden_width = w_gate.shape
    depth = width // PARTS
    loads = [
        pltpu.make_async_copy(own, x.at[:rows], in_sem.at[0]),
        pltpu.make_async_copy(sib, x.at[rows:], in_sem.at[1]),
    ]
    for k in range(PARTS):
        part = pl.ds(k * depth, depth)
        loads.append(pltpu.make_async_copy(w_gate.at[part], gate.at[part], in_sem.at[2 + 2 * k]))
        loads.append(pltpu.make_async_copy(w_up.at[part], up.at[part], in_sem.at[3 + 2 * k]))
    load_down = pltpu.make_async_copy(w_down, down, in_sem.at[2 + 2 * PARTS])
    for load in loads:
        load.start()
    load_down.start()
    loads[0].wait()
    loads[1].wait()
    gate_sum = jnp.zeros((2 * rows, hidden_width), jnp.float32)
    up_sum = jnp.zeros((2 * rows, hidden_width), jnp.float32)
    for k in range(PARTS):
        part = pl.ds(k * depth, depth)
        loads[2 + 2 * k].wait()
        gate_sum += jnp.dot(x[:, part], gate[part], preferred_element_type=jnp.float32)
        loads[3 + 2 * k].wait()
        up_sum += jnp.dot(x[:, part], up[part], preferred_element_type=jnp.float32)
    hidden = (gate_sum / (1.0 + jnp.exp(-gate_sum)) * up_sum).astype(jnp.bfloat16)
    scale = scale_of(x[:, width:], mine[0].astype(jnp.float32), top_count)
    load_down.wait()
    stores = []
    for k in range(PARTS):
        part = pl.ds(k * depth, depth)
        served = jnp.dot(hidden, down[:, part], preferred_element_type=jnp.float32)
        y[:, part] = (served * scale).astype(jnp.bfloat16)
        stores.append(pltpu.make_async_copy(y.at[rows:, part], out_sib.at[:, part], out_sem.at[2 * k]))
        stores.append(pltpu.make_async_copy(y.at[:rows, part], out_own.at[:, part], out_sem.at[2 * k + 1]))
        stores[-2].start()
        stores[-1].start()
    for store in stores:
        store.wait()


def serve_rows(own, sib, mine, top_count, w_gate, w_up, w_down):
    rows, packed_width = own.shape
    width, hidden_width = w_gate.shape
    anywhere = pl.BlockSpec(memory_space=pl.ANY)
    out = jax.ShapeDtypeStruct((rows, width), jnp.bfloat16)
    moved = 2 * (4 * rows * width + 3 * width * hidden_width)
    return pl.pallas_call(
        functools.partial(serve_kernel, top_count),
        out_shape=(out, out),
        in_specs=[pl.BlockSpec(memory_space=pltpu.SMEM)] + [anywhere] * 5,
        out_specs=(anywhere, anywhere),
        scratch_shapes=[
            pltpu.VMEM((2 * rows, packed_width), jnp.bfloat16),
            pltpu.VMEM((width, hidden_width), jnp.bfloat16),
            pltpu.VMEM((width, hidden_width), jnp.bfloat16),
            pltpu.VMEM((hidden_width, width), jnp.bfloat16),
            pltpu.VMEM((2 * rows, width), jnp.bfloat16),
            pltpu.SemaphoreType.DMA((3 + 2 * PARTS,)),
            pltpu.SemaphoreType.DMA((2 * PARTS,)),
        ],
        compiler_params=pltpu.CompilerParams(vmem_limit_bytes=40 * 2**20),
        cost_estimate=pl.CostEstimate(
            flops=12 * rows * width * hidden_width, bytes_accessed=moved, transcendentals=2 * rows * hidden_width
        ),
        name="serve_rows",
    )(mine.reshape(1), own, sib, w_gate, w_up, w_down)


def total(*terms):
    return sum(term.astype(jnp.float32) for term in terms).astype(jnp.bfloat16)


def chunk_steps(own, moves, serve):
    rows = own.shape[0]
    (held,) = yield (own,)
    for move in moves:
        (got,) = yield (permute(held, move),)
        held = jnp.concatenate([held, got])
    (sib,) = yield (permute(held, to_sibling),)
    out, out_sib = yield serve(held, sib)
    terms = [out]
    (got,) = yield (permute(out_sib, to_sibling),)
    for move in moves[::-1]:
        terms.append(got)
        half = got.shape[0] // 2
        sent = total(*[term[half : 2 * half] for term in terms])
        (got,) = yield (permute(sent, move),)
    terms.append(got)
    return total(*[term[:rows] for term in terms])


def in_order(chunks, order):
    waits = [next(chunk) for chunk in chunks]
    results = [None] * len(chunks)
    before = ()
    for number in order:
        count = len(waits[number])
        ready = lax.optimization_barrier(waits[number] + before)[:count]
        before = waits[number]
        try:
            waits[number] = chunks[number].send(ready)
        except StopIteration as end:
            results[number] = end.value
    return results


def step_order(chunk_count, step_count):
    if chunk_count == 3 and step_count == len(ORDER) // 3:
        return ORDER
    return [number for _ in range(step_count) for number in range(chunk_count)]


def dense(tokens, expert_ids, route_weight, slot_of, swap_flag, w_gate, w_up, w_down):
    tok_rows = tokens.shape[0]
    top_count = expert_ids.shape[1]
    mine = served_expert(slot_of, swap_flag)
    line_bits = (lax.axis_size("expert") // 2).bit_length() - 1
    moves = [along_line(2**bit) for bit in range(line_bits)][::-1] + [over_first, over_second]
    step = ROWS_AT_ONCE if tok_rows % ROWS_AT_ONCE == 0 else tok_rows
    extra = choices(expert_ids, route_weight)
    chunks = []
    for at in range(0, tok_rows, step):
        own = jnp.concatenate([tokens[at : at + step], extra[at : at + step]], axis=1)
        serve = lambda held, sib: serve_rows(held, sib, mine, top_count, w_gate[0], w_up[0], w_down[0])
        chunks.append(chunk_steps(own, moves, serve))
    return jnp.concatenate(in_order(chunks, step_order(len(chunks), 2 * len(moves) + 4)))


def on_device(tokens, expert_ids, *rest):
    slot_of = rest[1]
    ex_count = lax.axis_size("expert")
    capacity = 2 * tokens.shape[0] * expert_ids.shape[1] // slot_of.shape[0]
    paired = lax.axis_size("dp") == 4 and ex_count >= 2 and ex_count & (ex_count - 1) == 0
    serve = dense if capacity >= tokens.shape[0] and paired else sparse
    return serve(tokens, expert_ids, *rest)


def solution(mesh):
    return jax.shard_map(
        on_device,
        mesh=mesh,
        in_specs=(
            P(AXES, None),
            P(AXES, None),
            P(AXES, None),
            P(),
            P(AXES),
            P(AXES, None, None),
            P(AXES, None, None),
            P(AXES, None, None),
        ),
        out_specs=P(AXES, None),
        check_vma=False,
    )
```

```python
import functools

import jax
import jax.numpy as jnp
from jax import lax
from jax.experimental import pallas as pl
from jax.experimental.pallas import tpu as pltpu
from jax.sharding import PartitionSpec as P

AXES = ("dp", "expert")
LANES = 128
PARTS = 4
VMEM_MIB = 8
ROWS_AT_ONCE = 8
GUARDS = []


def partner(value, axis, distance):
    mask = 2**distance
    pairs = [(source, source ^ mask) for source in range(lax.axis_size(axis))]
    return lax.ppermute(value, axis, pairs)


def exchange(value):
    return lax.all_to_all(
        lax.all_to_all(value, "dp", split_axis=0, concat_axis=0, tiled=True),
        "expert",
        split_axis=1,
        concat_axis=1,
        tiled=True,
    )


def sparse(tokens, expert_ids, route_weight, slot_of, swap_flag, w_gate, w_up, w_down):
    dp_count = lax.axis_size("dp")
    ex_count = lax.axis_size("expert")
    slot_count = dp_count * ex_count
    tok_rows, model_width = tokens.shape
    top_count = expert_ids.shape[1]
    experts = slot_of.shape[0]
    capacity = 2 * tok_rows * top_count // experts
    moved_shards = partner((w_gate, w_up, w_down), "dp", 0)
    taking = swap_flag[0] == 1
    gate_w = jnp.where(taking, moved_shards[0][0], w_gate[0])
    up_w = jnp.where(taking, moved_shards[1][0], w_up[0])
    down_w = jnp.where(taking, moved_shards[2][0], w_down[0])
    pair_count = tok_rows * top_count
    flat_ids = expert_ids.reshape(pair_count)
    onehot = (flat_ids[:, None] == jnp.arange(experts, dtype=jnp.int32)).astype(jnp.int32)
    order_rank = jnp.sum((jnp.cumsum(onehot, axis=0) - onehot) * onehot, axis=1)
    dest_slot = jnp.sum(onehot[:, :, None] * slot_of[None, :, :], axis=1)
    position = dest_slot * capacity + order_rank[:, None]
    pair_ids = jnp.broadcast_to(jnp.arange(pair_count, dtype=jnp.int32)[:, None], (pair_count, 2))
    owner = (
        jnp.full((slot_count * capacity,), -1, jnp.int32)
        .at[position.reshape(-1)]
        .set(pair_ids.reshape(-1))
    )
    token_row = jnp.maximum(owner, 0) // top_count
    outbox = jnp.where((owner >= 0)[:, None], tokens[token_row], jnp.zeros((), tokens.dtype))
    outbox = outbox.reshape(dp_count, ex_count, capacity, model_width)
    arrived = exchange(outbox).reshape(slot_count * capacity, model_width)
    gate_sum = jnp.dot(arrived, gate_w, preferred_element_type=jnp.float32)
    up_sum = jnp.dot(arrived, up_w, preferred_element_type=jnp.float32)
    hidden = (jax.nn.silu(gate_sum) * up_sum).astype(jnp.bfloat16)
    partial_out = jnp.dot(hidden, down_w, preferred_element_type=jnp.float32).astype(jnp.bfloat16)
    partial_out = partial_out.reshape(dp_count, ex_count, capacity, model_width)
    returned = exchange(partial_out).reshape(slot_count * capacity, model_width)
    picked = returned[position].astype(jnp.float32)
    scaled = jnp.sum(picked, axis=1) * route_weight.reshape(pair_count)[:, None]
    return jnp.sum(scaled.reshape(tok_rows, top_count, model_width), axis=1).astype(jnp.bfloat16)


def served_expert(slot_of, swap_flag):
    d = lax.axis_index("dp")
    x = lax.axis_index("expert")
    serving = jnp.where(swap_flag[0] == 1, d ^ 1, d) * lax.axis_size("expert") + x
    numbers = jnp.arange(slot_of.shape[0], dtype=jnp.int32)[:, None]
    return jnp.sum(jnp.where(slot_of == serving, numbers, 0))


def permute(value, move):
    ex_count = lax.axis_size("expert")
    pairs = []
    for source in range(lax.axis_size("dp") * ex_count):
        d, e = move(*divmod(source, ex_count))
        pairs.append((source, d * ex_count + e))
    return lax.ppermute(value, AXES, pairs)


def to_sibling(d, e):
    return d ^ 1, e


def over_first(d, e):
    return (d ^ 2, e) if d % 2 else (d, e ^ 1)


def over_second(d, e):
    return (d, e ^ 1) if d % 2 else (d ^ 2, e)


def along_line(distance):
    return lambda d, e: (d, e ^ (2 * distance))


def choices(expert_ids, route_weight):
    parts = [expert_ids.astype(jnp.bfloat16)]
    rest = route_weight
    for _ in range(3):
        part = lax.reduce_precision(rest, exponent_bits=8, mantissa_bits=7)
        parts.append(part.astype(jnp.bfloat16))
        rest = rest - part
    extra = jnp.concatenate(parts, axis=1)
    return jnp.pad(extra, ((0, 0), (0, -extra.shape[1] % LANES)))


def scale_of(extra, mine, top_count):
    extra = extra.astype(jnp.float32)
    ids, hi, mid, lo = (extra[:, k * top_count : (k + 1) * top_count] for k in range(4))
    return jnp.sum(jnp.where(ids == mine, hi + mid + lo, 0.0), axis=1, keepdims=True)


def serve_kernel(top_count, mine, own, sib, w_gate, w_up, w_down, out_own, out_sib):
    rows = own.shape[0]
    width, hidden_width = w_gate.shape
    depth = width // PARTS
    gate_sum = jnp.zeros((2 * rows, hidden_width), jnp.float32)
    up_sum = jnp.zeros((2 * rows, hidden_width), jnp.float32)
    for k in range(PARTS):
        part = pl.ds(k * depth, depth)
        x = jnp.concatenate([own[:, part], sib[:, part]])
        gate_sum += jnp.dot(x, w_gate[part], preferred_element_type=jnp.float32)
        up_sum += jnp.dot(x, w_up[part], preferred_element_type=jnp.float32)
    hidden = (gate_sum / (1.0 + jnp.exp(-gate_sum)) * up_sum).astype(jnp.bfloat16)
    extra = jnp.concatenate([own[:, width:], sib[:, width:]])
    scale = scale_of(extra, mine[0].astype(jnp.float32), top_count)
    for k in range(PARTS):
        part = pl.ds(k * depth, depth)
        served = jnp.dot(hidden, w_down[:, part], preferred_element_type=jnp.float32) * scale
        out_own[:, part] = served[:rows].astype(jnp.bfloat16)
        out_sib[:, part] = served[rows:].astype(jnp.bfloat16)


def serve_rows(own, sib, mine, top_count, w_gate, w_up, w_down):
    rows, packed_width = own.shape
    width, hidden_width = w_gate.shape
    whole = pl.BlockSpec(memory_space=pltpu.VMEM)
    out = jax.ShapeDtypeStruct((rows, width), jnp.bfloat16)
    moved = 2 * (4 * rows * width + 3 * width * hidden_width)
    return pl.pallas_call(
        functools.partial(serve_kernel, top_count),
        out_shape=(out, out),
        in_specs=[pl.BlockSpec(memory_space=pltpu.SMEM)] + [whole] * 5,
        out_specs=(whole, whole),
        compiler_params=pltpu.CompilerParams(vmem_limit_bytes=VMEM_MIB * 2**20),
        cost_estimate=pl.CostEstimate(
            flops=12 * rows * width * hidden_width, bytes_accessed=moved, transcendentals=2 * rows * hidden_width
        ),
        name="serve_rows",
    )(mine.reshape(1), own, sib, w_gate, w_up, w_down)


def total(*terms):
    return sum(term.astype(jnp.float32) for term in terms).astype(jnp.bfloat16)


def chunk_steps(own, moves, serve):
    rows = own.shape[0]
    (held,) = yield (own,)
    for move in moves:
        (got,) = yield (permute(held, move),)
        held = jnp.concatenate([held, got])
    (sib,) = yield (permute(held, to_sibling),)
    out, out_sib = serve(held, sib)
    (got,) = yield (permute(out_sib, to_sibling),)
    terms = [out]
    for move in moves[::-1]:
        terms.append(got)
        half = got.shape[0] // 2
        sent = total(*[term[half : 2 * half] for term in terms])
        (got,) = yield (permute(sent, move),)
    terms.append(got)
    return total(*[term[:rows] for term in terms])


def run_steps(chunks, guards):
    waits = [[next(chunk)[0]] for chunk in chunks]
    results = [None] * len(chunks)
    while any(result is None for result in results):
        for i, chunk in enumerate(chunks):
            at = len(waits[i]) - 1
            asked = [(j, t) for k, s, j, t in guards if (k, s) == (i, at)]
            if results[i] is not None or any(len(waits[j]) <= t for j, t in asked):
                continue
            ready = tuple(waits[i][-1:])
            if asked:
                ready = lax.optimization_barrier(ready + tuple(waits[j][t] for j, t in asked))[:1]
            try:
                waits[i].append(chunk.send(ready)[0])
            except StopIteration as end:
                results[i] = end.value
    return results


def dense(tokens, expert_ids, route_weight, slot_of, swap_flag, w_gate, w_up, w_down):
    tok_rows = tokens.shape[0]
    top_count = expert_ids.shape[1]
    mine = served_expert(slot_of, swap_flag)
    line_bits = (lax.axis_size("expert") // 2).bit_length() - 1
    moves = [along_line(2**bit) for bit in range(line_bits)][::-1] + [over_first, over_second]
    step = ROWS_AT_ONCE if tok_rows % ROWS_AT_ONCE == 0 else tok_rows
    extra = choices(expert_ids, route_weight)
    chunks = []
    for at in range(0, tok_rows, step):
        own = jnp.concatenate([tokens[at : at + step], extra[at : at + step]], axis=1)
        serve = lambda held, sib: serve_rows(held, sib, mine, top_count, w_gate[0], w_up[0], w_down[0])
        chunks.append(chunk_steps(own, moves, serve))
    guards = GUARDS if len(chunks) == 3 and len(moves) == 4 else []
    return jnp.concatenate(run_steps(chunks, guards))


def on_device(tokens, expert_ids, *rest):
    slot_of = rest[1]
    ex_count = lax.axis_size("expert")
    capacity = 2 * tokens.shape[0] * expert_ids.shape[1] // slot_of.shape[0]
    paired = lax.axis_size("dp") == 4 and ex_count >= 2 and ex_count & (ex_count - 1) == 0
    serve = dense if capacity >= tokens.shape[0] and paired else sparse
    return serve(tokens, expert_ids, *rest)


def solution(mesh):
    return jax.shard_map(
        on_device,
        mesh=mesh,
        in_specs=(
            P(AXES, None),
            P(AXES, None),
            P(AXES, None),
            P(),
            P(AXES),
            P(AXES, None, None),
            P(AXES, None, None),
            P(AXES, None, None),
        ),
        out_specs=P(AXES, None),
        check_vma=False,
    )
```

```python
import functools

import jax
import jax.numpy as jnp
from jax import lax
from jax.experimental import pallas as pl
from jax.experimental.pallas import tpu as pltpu
from jax.sharding import PartitionSpec as P

AXES = ("dp", "expert")
LANES = 128
PARTS = 4
VMEM_MIB = 12
ROWS_AT_ONCE = 8
GUARDS = []


def partner(value, axis, distance):
    mask = 2**distance
    pairs = [(source, source ^ mask) for source in range(lax.axis_size(axis))]
    return lax.ppermute(value, axis, pairs)


def exchange(value):
    return lax.all_to_all(
        lax.all_to_all(value, "dp", split_axis=0, concat_axis=0, tiled=True),
        "expert",
        split_axis=1,
        concat_axis=1,
        tiled=True,
    )


def sparse(tokens, expert_ids, route_weight, slot_of, swap_flag, w_gate, w_up, w_down):
    dp_count = lax.axis_size("dp")
    ex_count = lax.axis_size("expert")
    slot_count = dp_count * ex_count
    tok_rows, model_width = tokens.shape
    top_count = expert_ids.shape[1]
    experts = slot_of.shape[0]
    capacity = 2 * tok_rows * top_count // experts
    moved_shards = partner((w_gate, w_up, w_down), "dp", 0)
    taking = swap_flag[0] == 1
    gate_w = jnp.where(taking, moved_shards[0][0], w_gate[0])
    up_w = jnp.where(taking, moved_shards[1][0], w_up[0])
    down_w = jnp.where(taking, moved_shards[2][0], w_down[0])
    pair_count = tok_rows * top_count
    flat_ids = expert_ids.reshape(pair_count)
    onehot = (flat_ids[:, None] == jnp.arange(experts, dtype=jnp.int32)).astype(jnp.int32)
    order_rank = jnp.sum((jnp.cumsum(onehot, axis=0) - onehot) * onehot, axis=1)
    dest_slot = jnp.sum(onehot[:, :, None] * slot_of[None, :, :], axis=1)
    position = dest_slot * capacity + order_rank[:, None]
    pair_ids = jnp.broadcast_to(jnp.arange(pair_count, dtype=jnp.int32)[:, None], (pair_count, 2))
    owner = (
        jnp.full((slot_count * capacity,), -1, jnp.int32)
        .at[position.reshape(-1)]
        .set(pair_ids.reshape(-1))
    )
    token_row = jnp.maximum(owner, 0) // top_count
    outbox = jnp.where((owner >= 0)[:, None], tokens[token_row], jnp.zeros((), tokens.dtype))
    outbox = outbox.reshape(dp_count, ex_count, capacity, model_width)
    arrived = exchange(outbox).reshape(slot_count * capacity, model_width)
    gate_sum = jnp.dot(arrived, gate_w, preferred_element_type=jnp.float32)
    up_sum = jnp.dot(arrived, up_w, preferred_element_type=jnp.float32)
    hidden = (jax.nn.silu(gate_sum) * up_sum).astype(jnp.bfloat16)
    partial_out = jnp.dot(hidden, down_w, preferred_element_type=jnp.float32).astype(jnp.bfloat16)
    partial_out = partial_out.reshape(dp_count, ex_count, capacity, model_width)
    returned = exchange(partial_out).reshape(slot_count * capacity, model_width)
    picked = returned[position].astype(jnp.float32)
    scaled = jnp.sum(picked, axis=1) * route_weight.reshape(pair_count)[:, None]
    return jnp.sum(scaled.reshape(tok_rows, top_count, model_width), axis=1).astype(jnp.bfloat16)


def served_expert(slot_of, swap_flag):
    d = lax.axis_index("dp")
    x = lax.axis_index("expert")
    serving = jnp.where(swap_flag[0] == 1, d ^ 1, d) * lax.axis_size("expert") + x
    numbers = jnp.arange(slot_of.shape[0], dtype=jnp.int32)[:, None]
    return jnp.sum(jnp.where(slot_of == serving, numbers, 0))


def permute(value, move):
    ex_count = lax.axis_size("expert")
    pairs = []
    for source in range(lax.axis_size("dp") * ex_count):
        d, e = move(*divmod(source, ex_count))
        pairs.append((source, d * ex_count + e))
    return lax.ppermute(value, AXES, pairs)


def to_sibling(d, e):
    return d ^ 1, e


def over_first(d, e):
    return (d ^ 2, e) if d % 2 else (d, e ^ 1)


def over_second(d, e):
    return (d, e ^ 1) if d % 2 else (d ^ 2, e)


def along_line(distance):
    return lambda d, e: (d, e ^ (2 * distance))


def choices(expert_ids, route_weight):
    parts = [expert_ids.astype(jnp.bfloat16)]
    rest = route_weight
    for _ in range(3):
        part = lax.reduce_precision(rest, exponent_bits=8, mantissa_bits=7)
        parts.append(part.astype(jnp.bfloat16))
        rest = rest - part
    extra = jnp.concatenate(parts, axis=1)
    return jnp.pad(extra, ((0, 0), (0, -extra.shape[1] % LANES)))


def pack_kernel(tokens, extra, *outs):
    at = 0
    for out in outs:
        rows, packed_width = out.shape
        out[...] = jnp.concatenate([tokens[at : at + rows], extra[at : at + rows]], axis=1)
        at += rows


def packed(tokens, extra, rows):
    tok_rows, width = tokens.shape
    whole = pl.BlockSpec(memory_space=pltpu.VMEM)
    out = jax.ShapeDtypeStruct((rows, width + extra.shape[1]), tokens.dtype)
    return pl.pallas_call(
        pack_kernel,
        out_shape=(out,) * (tok_rows // rows),
        in_specs=[whole, whole],
        out_specs=(whole,) * (tok_rows // rows),
        name="pack_rows",
    )(tokens, extra)


def scale_of(extra, mine, top_count):
    extra = extra.astype(jnp.float32)
    ids, hi, mid, lo = (extra[:, k * top_count : (k + 1) * top_count] for k in range(4))
    return jnp.sum(jnp.where(ids == mine, hi + mid + lo, 0.0), axis=1, keepdims=True)


def serve_kernel(top_count, mine, own, sib, w_gate, w_up, w_down, out_own, out_sib, down, sem):
    load = pltpu.make_async_copy(w_down, down, sem)
    load.start()
    rows = own.shape[0]
    width, hidden_width = w_gate.shape
    depth = width // PARTS
    gate_sum = jnp.zeros((2 * rows, hidden_width), jnp.float32)
    up_sum = jnp.zeros((2 * rows, hidden_width), jnp.float32)
    for k in range(PARTS):
        part = pl.ds(k * depth, depth)
        x = jnp.concatenate([own[:, part], sib[:, part]])
        gate_sum += jnp.dot(x, w_gate[part], preferred_element_type=jnp.float32)
        up_sum += jnp.dot(x, w_up[part], preferred_element_type=jnp.float32)
    hidden = (gate_sum / (1.0 + jnp.exp(-gate_sum)) * up_sum).astype(jnp.bfloat16)
    extra = jnp.concatenate([own[:, width:], sib[:, width:]])
    scale = scale_of(extra, mine[0].astype(jnp.float32), top_count)
    load.wait()
    for k in range(PARTS):
        part = pl.ds(k * depth, depth)
        served = jnp.dot(hidden, down[:, part], preferred_element_type=jnp.float32) * scale
        out_own[:, part] = served[:rows].astype(jnp.bfloat16)
        out_sib[:, part] = served[rows:].astype(jnp.bfloat16)


def serve_rows(own, sib, mine, top_count, w_gate, w_up, w_down):
    rows, packed_width = own.shape
    width, hidden_width = w_gate.shape
    whole = pl.BlockSpec(memory_space=pltpu.VMEM)
    out = jax.ShapeDtypeStruct((rows, width), jnp.bfloat16)
    moved = 2 * (4 * rows * width + 3 * width * hidden_width)
    return pl.pallas_call(
        functools.partial(serve_kernel, top_count),
        out_shape=(out, out),
        in_specs=[pl.BlockSpec(memory_space=pltpu.SMEM)] + [whole] * 4 + [pl.BlockSpec(memory_space=pltpu.HBM)],
        out_specs=(whole, whole),
        scratch_shapes=[pltpu.VMEM((hidden_width, width), jnp.bfloat16), pltpu.SemaphoreType.DMA],
        compiler_params=pltpu.CompilerParams(vmem_limit_bytes=VMEM_MIB * 2**20),
        cost_estimate=pl.CostEstimate(
            flops=12 * rows * width * hidden_width, bytes_accessed=moved, transcendentals=2 * rows * hidden_width
        ),
        name="serve_rows",
    )(mine.reshape(1), own, sib, w_gate, w_up, w_down)


def total(*terms):
    return sum(term.astype(jnp.float32) for term in terms).astype(jnp.bfloat16)


def chunk_steps(own, moves, serve):
    rows = own.shape[0]
    (held,) = yield (own,)
    for move in moves:
        (got,) = yield (permute(held, move),)
        held = jnp.concatenate([held, got])
    (sib,) = yield (permute(held, to_sibling),)
    out, out_sib = serve(held, sib)
    (out_sib,) = yield (out_sib,)
    (got,) = yield (permute(out_sib, to_sibling),)
    terms = [out]
    for move in moves[::-1]:
        terms.append(got)
        half = got.shape[0] // 2
        sent = total(*[term[half : 2 * half] for term in terms])
        (got,) = yield (permute(sent, move),)
    terms.append(got)
    return total(*[term[:rows] for term in terms])


def run_steps(chunks, guards):
    waits = [[next(chunk)[0]] for chunk in chunks]
    results = [None] * len(chunks)
    while any(result is None for result in results):
        for i, chunk in enumerate(chunks):
            at = len(waits[i]) - 1
            asked = [(j, t) for k, s, j, t in guards if (k, s) == (i, at)]
            if results[i] is not None or any(len(waits[j]) <= t for j, t in asked):
                continue
            ready = tuple(waits[i][-1:])
            if asked:
                ready = lax.optimization_barrier(ready + tuple(waits[j][t] for j, t in asked))[:1]
            try:
                waits[i].append(chunk.send(ready)[0])
            except StopIteration as end:
                results[i] = end.value
    return results


def dense(tokens, expert_ids, route_weight, slot_of, swap_flag, w_gate, w_up, w_down):
    tok_rows = tokens.shape[0]
    top_count = expert_ids.shape[1]
    mine = served_expert(slot_of, swap_flag)
    line_bits = (lax.axis_size("expert") // 2).bit_length() - 1
    moves = [along_line(2**bit) for bit in range(line_bits)][::-1] + [over_first, over_second]
    step = ROWS_AT_ONCE if tok_rows % ROWS_AT_ONCE == 0 else tok_rows
    extra = choices(expert_ids, route_weight)
    serve = lambda held, sib: serve_rows(held, sib, mine, top_count, w_gate[0], w_up[0], w_down[0])
    chunks = [chunk_steps(own, moves, serve) for own in packed(tokens, extra, step)]
    guards = GUARDS if len(chunks) == 3 and len(moves) == 4 else []
    return jnp.concatenate(run_steps(chunks, guards))


def on_device(tokens, expert_ids, *rest):
    slot_of = rest[1]
    ex_count = lax.axis_size("expert")
    capacity = 2 * tokens.shape[0] * expert_ids.shape[1] // slot_of.shape[0]
    paired = lax.axis_size("dp") == 4 and ex_count >= 2 and ex_count & (ex_count - 1) == 0
    serve = dense if capacity >= tokens.shape[0] and paired else sparse
    return serve(tokens, expert_ids, *rest)


def solution(mesh):
    return jax.shard_map(
        on_device,
        mesh=mesh,
        in_specs=(
            P(AXES, None),
            P(AXES, None),
            P(AXES, None),
            P(),
            P(AXES),
            P(AXES, None, None),
            P(AXES, None, None),
            P(AXES, None, None),
        ),
        out_specs=P(AXES, None),
        check_vma=False,
    )
```

```python
import functools

import jax
import jax.numpy as jnp
from jax import lax
from jax.experimental import pallas as pl
from jax.experimental.pallas import tpu as pltpu
from jax.sharding import PartitionSpec as P

AXES = ("dp", "expert")
LANES = 128
PARTS = 4
VMEM_MIB = 12
ROWS_AT_ONCE = 8
GUARDS = []


def partner(value, axis, distance):
    mask = 2**distance
    pairs = [(source, source ^ mask) for source in range(lax.axis_size(axis))]
    return lax.ppermute(value, axis, pairs)


def exchange(value):
    return lax.all_to_all(
        lax.all_to_all(value, "dp", split_axis=0, concat_axis=0, tiled=True),
        "expert",
        split_axis=1,
        concat_axis=1,
        tiled=True,
    )


def sparse(tokens, expert_ids, route_weight, slot_of, swap_flag, w_gate, w_up, w_down):
    dp_count = lax.axis_size("dp")
    ex_count = lax.axis_size("expert")
    slot_count = dp_count * ex_count
    tok_rows, model_width = tokens.shape
    top_count = expert_ids.shape[1]
    experts = slot_of.shape[0]
    capacity = 2 * tok_rows * top_count // experts
    moved_shards = partner((w_gate, w_up, w_down), "dp", 0)
    taking = swap_flag[0] == 1
    gate_w = jnp.where(taking, moved_shards[0][0], w_gate[0])
    up_w = jnp.where(taking, moved_shards[1][0], w_up[0])
    down_w = jnp.where(taking, moved_shards[2][0], w_down[0])
    pair_count = tok_rows * top_count
    flat_ids = expert_ids.reshape(pair_count)
    onehot = (flat_ids[:, None] == jnp.arange(experts, dtype=jnp.int32)).astype(jnp.int32)
    order_rank = jnp.sum((jnp.cumsum(onehot, axis=0) - onehot) * onehot, axis=1)
    dest_slot = jnp.sum(onehot[:, :, None] * slot_of[None, :, :], axis=1)
    position = dest_slot * capacity + order_rank[:, None]
    pair_ids = jnp.broadcast_to(jnp.arange(pair_count, dtype=jnp.int32)[:, None], (pair_count, 2))
    owner = (
        jnp.full((slot_count * capacity,), -1, jnp.int32)
        .at[position.reshape(-1)]
        .set(pair_ids.reshape(-1))
    )
    token_row = jnp.maximum(owner, 0) // top_count
    outbox = jnp.where((owner >= 0)[:, None], tokens[token_row], jnp.zeros((), tokens.dtype))
    outbox = outbox.reshape(dp_count, ex_count, capacity, model_width)
    arrived = exchange(outbox).reshape(slot_count * capacity, model_width)
    gate_sum = jnp.dot(arrived, gate_w, preferred_element_type=jnp.float32)
    up_sum = jnp.dot(arrived, up_w, preferred_element_type=jnp.float32)
    hidden = (jax.nn.silu(gate_sum) * up_sum).astype(jnp.bfloat16)
    partial_out = jnp.dot(hidden, down_w, preferred_element_type=jnp.float32).astype(jnp.bfloat16)
    partial_out = partial_out.reshape(dp_count, ex_count, capacity, model_width)
    returned = exchange(partial_out).reshape(slot_count * capacity, model_width)
    picked = returned[position].astype(jnp.float32)
    scaled = jnp.sum(picked, axis=1) * route_weight.reshape(pair_count)[:, None]
    return jnp.sum(scaled.reshape(tok_rows, top_count, model_width), axis=1).astype(jnp.bfloat16)


def served_expert(slot_of, swap_flag):
    d = lax.axis_index("dp")
    x = lax.axis_index("expert")
    serving = jnp.where(swap_flag[0] == 1, d ^ 1, d) * lax.axis_size("expert") + x
    numbers = jnp.arange(slot_of.shape[0], dtype=jnp.int32)[:, None]
    return jnp.sum(jnp.where(slot_of == serving, numbers, 0))


def permute(value, move):
    ex_count = lax.axis_size("expert")
    pairs = []
    for source in range(lax.axis_size("dp") * ex_count):
        d, e = move(*divmod(source, ex_count))
        pairs.append((source, d * ex_count + e))
    return lax.ppermute(value, AXES, pairs)


def to_sibling(d, e):
    return d ^ 1, e


def over_first(d, e):
    return (d ^ 2, e) if d % 2 else (d, e ^ 1)


def over_second(d, e):
    return (d, e ^ 1) if d % 2 else (d ^ 2, e)


def along_line(distance):
    return lambda d, e: (d, e ^ (2 * distance))


def choices(expert_ids, route_weight):
    parts = [expert_ids.astype(jnp.bfloat16)]
    rest = route_weight
    for _ in range(3):
        part = lax.reduce_precision(rest, exponent_bits=8, mantissa_bits=7)
        parts.append(part.astype(jnp.bfloat16))
        rest = rest - part
    extra = jnp.concatenate(parts, axis=1)
    return jnp.pad(extra, ((0, 0), (0, -extra.shape[1] % LANES)))


def pack_kernel(tokens, extra, *outs):
    at = 0
    for out in outs:
        rows, packed_width = out.shape
        out[...] = jnp.concatenate([tokens[at : at + rows], extra[at : at + rows]], axis=1)
        at += rows


def packed(tokens, extra, rows):
    tok_rows, width = tokens.shape
    whole = pl.BlockSpec(memory_space=pltpu.VMEM)
    out = pltpu.VMEM((rows, width + extra.shape[1]), tokens.dtype)
    return pl.pallas_call(
        pack_kernel,
        out_shape=(out,) * (tok_rows // rows),
        in_specs=[whole, whole],
        out_specs=(whole,) * (tok_rows // rows),
        name="pack_rows",
    )(tokens, extra)


def scale_of(extra, mine, top_count):
    extra = extra.astype(jnp.float32)
    ids, hi, mid, lo = (extra[:, k * top_count : (k + 1) * top_count] for k in range(4))
    return jnp.sum(jnp.where(ids == mine, hi + mid + lo, 0.0), axis=1, keepdims=True)


def serve_kernel(top_count, mine, own, sib, w_gate, w_up, w_down, out_own, out_sib, down, sem):
    load = pltpu.make_async_copy(w_down, down, sem)
    load.start()
    rows = own.shape[0]
    width, hidden_width = w_gate.shape
    depth = width // PARTS
    gate_sum = jnp.zeros((2 * rows, hidden_width), jnp.float32)
    up_sum = jnp.zeros((2 * rows, hidden_width), jnp.float32)
    for k in range(PARTS):
        part = pl.ds(k * depth, depth)
        x = jnp.concatenate([own[:, part], sib[:, part]])
        gate_sum += jnp.dot(x, w_gate[part], preferred_element_type=jnp.float32)
        up_sum += jnp.dot(x, w_up[part], preferred_element_type=jnp.float32)
    hidden = (gate_sum / (1.0 + jnp.exp(-gate_sum)) * up_sum).astype(jnp.bfloat16)
    extra = jnp.concatenate([own[:, width:], sib[:, width:]])
    scale = scale_of(extra, mine[0].astype(jnp.float32), top_count)
    load.wait()
    for k in range(PARTS):
        part = pl.ds(k * depth, depth)
        served = jnp.dot(hidden, down[:, part], preferred_element_type=jnp.float32) * scale
        out_own[:, part] = served[:rows].astype(jnp.bfloat16)
        out_sib[:, part] = served[rows:].astype(jnp.bfloat16)


def serve_rows(own, sib, mine, top_count, w_gate, w_up, w_down):
    rows, packed_width = own.shape
    width, hidden_width = w_gate.shape
    whole = pl.BlockSpec(memory_space=pltpu.VMEM)
    out = jax.ShapeDtypeStruct((rows, width), jnp.bfloat16)
    moved = 2 * (4 * rows * width + 3 * width * hidden_width)
    return pl.pallas_call(
        functools.partial(serve_kernel, top_count),
        out_shape=(out, out),
        in_specs=[pl.BlockSpec(memory_space=pltpu.SMEM)] + [whole] * 4 + [pl.BlockSpec(memory_space=pltpu.HBM)],
        out_specs=(whole, whole),
        scratch_shapes=[pltpu.VMEM((hidden_width, width), jnp.bfloat16), pltpu.SemaphoreType.DMA],
        compiler_params=pltpu.CompilerParams(vmem_limit_bytes=VMEM_MIB * 2**20),
        cost_estimate=pl.CostEstimate(
            flops=12 * rows * width * hidden_width, bytes_accessed=moved, transcendentals=2 * rows * hidden_width
        ),
        name="serve_rows",
    )(mine.reshape(1), own, sib, w_gate, w_up, pltpu.with_memory_space_constraint(w_down, pltpu.HBM))


def total(*terms):
    return sum(term.astype(jnp.float32) for term in terms).astype(jnp.bfloat16)


def chunk_steps(own, moves, serve):
    rows = own.shape[0]
    (held,) = yield (own,)
    for move in moves:
        (got,) = yield (permute(held, move),)
        held = jnp.concatenate([held, got])
    (sib,) = yield (permute(held, to_sibling),)
    out, out_sib = serve(held, sib)
    (out_sib,) = yield (out_sib,)
    (got,) = yield (permute(out_sib, to_sibling),)
    terms = [out]
    for move in moves[::-1]:
        terms.append(got)
        half = got.shape[0] // 2
        sent = total(*[term[half : 2 * half] for term in terms])
        (got,) = yield (permute(sent, move),)
    terms.append(got)
    return total(*[term[:rows] for term in terms])


def run_steps(chunks, guards):
    waits = [[next(chunk)[0]] for chunk in chunks]
    results = [None] * len(chunks)
    while any(result is None for result in results):
        for i, chunk in enumerate(chunks):
            at = len(waits[i]) - 1
            asked = [(j, t) for k, s, j, t in guards if (k, s) == (i, at)]
            if results[i] is not None or any(len(waits[j]) <= t for j, t in asked):
                continue
            ready = tuple(waits[i][-1:])
            if asked:
                ready = lax.optimization_barrier(ready + tuple(waits[j][t] for j, t in asked))[:1]
            try:
                waits[i].append(chunk.send(ready)[0])
            except StopIteration as end:
                results[i] = end.value
    return results


def dense(tokens, expert_ids, route_weight, slot_of, swap_flag, w_gate, w_up, w_down):
    tok_rows = tokens.shape[0]
    top_count = expert_ids.shape[1]
    mine = served_expert(slot_of, swap_flag)
    line_bits = (lax.axis_size("expert") // 2).bit_length() - 1
    along = [along_line(2**bit) for bit in range(line_bits)][::-1]
    across = [over_first, over_second]
    routes = [along[:1] + across + along[1:], along + across, along + across]
    step = ROWS_AT_ONCE if tok_rows % ROWS_AT_ONCE == 0 else tok_rows
    extra = choices(expert_ids, route_weight)
    serve = lambda held, sib: serve_rows(held, sib, mine, top_count, w_gate[0], w_up[0], w_down[0])
    owns = packed(tokens, extra, step)
    chunks = [chunk_steps(own, routes[i % len(routes)], serve) for i, own in enumerate(owns)]
    guards = GUARDS if len(chunks) == 3 and line_bits == 2 else []
    return jnp.concatenate(run_steps(chunks, guards))


def on_device(tokens, expert_ids, *rest):
    slot_of = rest[1]
    ex_count = lax.axis_size("expert")
    capacity = 2 * tokens.shape[0] * expert_ids.shape[1] // slot_of.shape[0]
    paired = lax.axis_size("dp") == 4 and ex_count >= 2 and ex_count & (ex_count - 1) == 0
    serve = dense if capacity >= tokens.shape[0] and paired else sparse
    return serve(tokens, expert_ids, *rest)


def solution(mesh):
    return jax.shard_map(
        on_device,
        mesh=mesh,
        in_specs=(
            P(AXES, None),
            P(AXES, None),
            P(AXES, None),
            P(),
            P(AXES),
            P(AXES, None, None),
            P(AXES, None, None),
            P(AXES, None, None),
        ),
        out_specs=P(AXES, None),
        check_vma=False,
    )
```

```python
import functools

import jax
import jax.numpy as jnp
from jax import lax
from jax.experimental import pallas as pl
from jax.experimental.pallas import tpu as pltpu
from jax.sharding import PartitionSpec as P

AXES = ("dp", "expert")
LANES = 128
PARTS = 4
VMEM_MIB = 8
ROWS_AT_ONCE = 8
GUARDS = []


def partner(value, axis, distance):
    mask = 2**distance
    pairs = [(source, source ^ mask) for source in range(lax.axis_size(axis))]
    return lax.ppermute(value, axis, pairs)


def exchange(value):
    return lax.all_to_all(
        lax.all_to_all(value, "dp", split_axis=0, concat_axis=0, tiled=True),
        "expert",
        split_axis=1,
        concat_axis=1,
        tiled=True,
    )


def sparse(tokens, expert_ids, route_weight, slot_of, swap_flag, w_gate, w_up, w_down):
    dp_count = lax.axis_size("dp")
    ex_count = lax.axis_size("expert")
    slot_count = dp_count * ex_count
    tok_rows, model_width = tokens.shape
    top_count = expert_ids.shape[1]
    experts = slot_of.shape[0]
    capacity = 2 * tok_rows * top_count // experts
    moved_shards = partner((w_gate, w_up, w_down), "dp", 0)
    taking = swap_flag[0] == 1
    gate_w = jnp.where(taking, moved_shards[0][0], w_gate[0])
    up_w = jnp.where(taking, moved_shards[1][0], w_up[0])
    down_w = jnp.where(taking, moved_shards[2][0], w_down[0])
    pair_count = tok_rows * top_count
    flat_ids = expert_ids.reshape(pair_count)
    onehot = (flat_ids[:, None] == jnp.arange(experts, dtype=jnp.int32)).astype(jnp.int32)
    order_rank = jnp.sum((jnp.cumsum(onehot, axis=0) - onehot) * onehot, axis=1)
    dest_slot = jnp.sum(onehot[:, :, None] * slot_of[None, :, :], axis=1)
    position = dest_slot * capacity + order_rank[:, None]
    pair_ids = jnp.broadcast_to(jnp.arange(pair_count, dtype=jnp.int32)[:, None], (pair_count, 2))
    owner = (
        jnp.full((slot_count * capacity,), -1, jnp.int32)
        .at[position.reshape(-1)]
        .set(pair_ids.reshape(-1))
    )
    token_row = jnp.maximum(owner, 0) // top_count
    outbox = jnp.where((owner >= 0)[:, None], tokens[token_row], jnp.zeros((), tokens.dtype))
    outbox = outbox.reshape(dp_count, ex_count, capacity, model_width)
    arrived = exchange(outbox).reshape(slot_count * capacity, model_width)
    gate_sum = jnp.dot(arrived, gate_w, preferred_element_type=jnp.float32)
    up_sum = jnp.dot(arrived, up_w, preferred_element_type=jnp.float32)
    hidden = (jax.nn.silu(gate_sum) * up_sum).astype(jnp.bfloat16)
    partial_out = jnp.dot(hidden, down_w, preferred_element_type=jnp.float32).astype(jnp.bfloat16)
    partial_out = partial_out.reshape(dp_count, ex_count, capacity, model_width)
    returned = exchange(partial_out).reshape(slot_count * capacity, model_width)
    picked = returned[position].astype(jnp.float32)
    scaled = jnp.sum(picked, axis=1) * route_weight.reshape(pair_count)[:, None]
    return jnp.sum(scaled.reshape(tok_rows, top_count, model_width), axis=1).astype(jnp.bfloat16)


def permute(value, move):
    ex_count = lax.axis_size("expert")
    pairs = []
    for source in range(lax.axis_size("dp") * ex_count):
        d, e = move(*divmod(source, ex_count))
        pairs.append((source, d * ex_count + e))
    return lax.ppermute(value, AXES, pairs)


def to_sibling(d, e):
    return d ^ 1, e


def over_first(d, e):
    return (d ^ 2, e) if d % 2 else (d, e ^ 1)


def over_second(d, e):
    return (d, e ^ 1) if d % 2 else (d ^ 2, e)


def along_line(distance):
    return lambda d, e: (d, e ^ (2 * distance))


def pack_kernel(slots, flag, tokens, ids, weights, mine, *outs_and_square):
    *outs, square = outs_and_square
    d = lax.axis_index("dp")
    serving = jnp.where(flag[0] == 1, d ^ 1, d) * lax.axis_size("expert") + lax.axis_index("expert")
    expert = jnp.int32(0)
    for half in range(slots.shape[0]):
        for number in range(slots.shape[1]):
            expert += jnp.where(slots[half, number] == serving, number, 0)
    mine[0] = expert
    top_count, tok_rows = ids.shape
    square[...] = jnp.zeros_like(square)
    square[:top_count, :tok_rows] = ids[...].astype(jnp.float32)
    rest = weights[...]
    for k in range(1, 4):
        part = rest.astype(jnp.bfloat16).astype(jnp.float32)
        square[k * top_count : (k + 1) * top_count, :tok_rows] = part
        rest = rest - part
    extra = square[...].T.astype(jnp.bfloat16)
    at = 0
    for out in outs:
        rows, packed_width = out.shape
        out[...] = jnp.concatenate([tokens[at : at + rows], extra[at : at + rows]], axis=1)
        at += rows


def packed(tokens, expert_ids, route_weight, slot_of, swap_flag, rows):
    tok_rows, width = tokens.shape
    side = -(-max(tok_rows, 4 * expert_ids.shape[1]) // LANES) * LANES
    scalars = pl.BlockSpec(memory_space=pltpu.SMEM)
    whole = pl.BlockSpec(memory_space=pltpu.VMEM)
    count = tok_rows // rows
    mine, *owns = pl.pallas_call(
        pack_kernel,
        out_shape=(jax.ShapeDtypeStruct((1,), jnp.int32),) + (pltpu.VMEM((rows, width + side), tokens.dtype),) * count,
        in_specs=[scalars] * 2 + [whole] * 3,
        out_specs=(scalars,) + (whole,) * count,
        scratch_shapes=[pltpu.VMEM((side, side), jnp.float32)],
        name="pack_rows",
    )(slot_of.T, swap_flag, tokens, expert_ids.T, route_weight.T)
    return mine, owns


def scale_of(extra, mine, top_count):
    extra = extra.astype(jnp.float32)
    ids, hi, mid, lo = (extra[:, k * top_count : (k + 1) * top_count] for k in range(4))
    return jnp.sum(jnp.where(ids == mine, hi + mid + lo, 0.0), axis=1, keepdims=True)


def serve_kernel(top_count, mine, own, sib, w_gate, w_up, w_down, out_own, out_sib):
    rows = own.shape[0]
    width, hidden_width = w_gate.shape
    depth = width // PARTS
    gate_sum = jnp.zeros((2 * rows, hidden_width), jnp.float32)
    up_sum = jnp.zeros((2 * rows, hidden_width), jnp.float32)
    for k in range(PARTS):
        part = pl.ds(k * depth, depth)
        x = jnp.concatenate([own[:, part], sib[:, part]])
        gate_sum += jnp.dot(x, w_gate[part], preferred_element_type=jnp.float32)
        up_sum += jnp.dot(x, w_up[part], preferred_element_type=jnp.float32)
    hidden = (gate_sum / (1.0 + jnp.exp(-gate_sum)) * up_sum).astype(jnp.bfloat16)
    extra = jnp.concatenate([own[:, width:], sib[:, width:]])
    scale = scale_of(extra, mine[0].astype(jnp.float32), top_count)
    for k in range(PARTS):
        part = pl.ds(k * depth, depth)
        served = jnp.dot(hidden, w_down[:, part], preferred_element_type=jnp.float32) * scale
        out_own[:, part] = served[:rows].astype(jnp.bfloat16)
        out_sib[:, part] = served[rows:].astype(jnp.bfloat16)


def serve_rows(own, sib, mine, top_count, w_gate, w_up, w_down):
    rows, packed_width = own.shape
    width, hidden_width = w_gate.shape
    whole = pl.BlockSpec(memory_space=pltpu.VMEM)
    out = jax.ShapeDtypeStruct((rows, width), jnp.bfloat16)
    moved = 2 * (4 * rows * width + 3 * width * hidden_width)
    return pl.pallas_call(
        functools.partial(serve_kernel, top_count),
        out_shape=(out, out),
        in_specs=[pl.BlockSpec(memory_space=pltpu.SMEM)] + [whole] * 5,
        out_specs=(whole, whole),
        compiler_params=pltpu.CompilerParams(vmem_limit_bytes=VMEM_MIB * 2**20),
        cost_estimate=pl.CostEstimate(
            flops=12 * rows * width * hidden_width, bytes_accessed=moved, transcendentals=2 * rows * hidden_width
        ),
        name="serve_rows",
    )(mine, own, sib, w_gate, w_up, w_down)


def total(*terms):
    return sum(term.astype(jnp.float32) for term in terms).astype(jnp.bfloat16)


def chunk_steps(own, moves, serve):
    rows = own.shape[0]
    (held,) = yield (own,)
    for move in moves:
        (got,) = yield (permute(held, move),)
        held = jnp.concatenate([held, got])
    (sib,) = yield (permute(held, to_sibling),)
    out, out_sib = serve(held, sib)
    (out_sib,) = yield (out_sib,)
    (got,) = yield (permute(out_sib, to_sibling),)
    terms = [out]
    for move in moves[::-1]:
        terms.append(got)
        half = got.shape[0] // 2
        sent = total(*[term[half : 2 * half] for term in terms])
        (got,) = yield (permute(sent, move),)
    terms.append(got)
    return total(*[term[:rows] for term in terms])


def run_steps(chunks, guards):
    waits = [[next(chunk)[0]] for chunk in chunks]
    results = [None] * len(chunks)
    while any(result is None for result in results):
        for i, chunk in enumerate(chunks):
            at = len(waits[i]) - 1
            asked = [(j, t) for k, s, j, t in guards if (k, s) == (i, at)]
            if results[i] is not None or any(len(waits[j]) <= t for j, t in asked):
                continue
            ready = tuple(waits[i][-1:])
            if asked:
                ready = lax.optimization_barrier(ready + tuple(waits[j][t] for j, t in asked))[:1]
            try:
                waits[i].append(chunk.send(ready)[0])
            except StopIteration as end:
                results[i] = end.value
    return results


def dense(tokens, expert_ids, route_weight, slot_of, swap_flag, w_gate, w_up, w_down):
    tok_rows = tokens.shape[0]
    top_count = expert_ids.shape[1]
    line_bits = (lax.axis_size("expert") // 2).bit_length() - 1
    along = [along_line(2**bit) for bit in range(line_bits)][::-1]
    across = [over_first, over_second]
    routes = [along + across, along[:1] + across + along[1:]]
    step = ROWS_AT_ONCE if tok_rows % ROWS_AT_ONCE == 0 else tok_rows
    mine, owns = packed(tokens, expert_ids, route_weight, slot_of, swap_flag, step)
    serve = lambda held, sib: serve_rows(held, sib, mine, top_count, w_gate[0], w_up[0], w_down[0])
    chunks = [chunk_steps(own, routes[i % len(routes)], serve) for i, own in enumerate(owns)]
    guards = GUARDS if len(chunks) == 3 and line_bits == 2 else []
    return jnp.concatenate(run_steps(chunks, guards))


def on_device(tokens, expert_ids, *rest):
    slot_of = rest[1]
    ex_count = lax.axis_size("expert")
    capacity = 2 * tokens.shape[0] * expert_ids.shape[1] // slot_of.shape[0]
    paired = lax.axis_size("dp") == 4 and ex_count >= 2 and ex_count & (ex_count - 1) == 0
    serve = dense if capacity >= tokens.shape[0] and paired else sparse
    return serve(tokens, expert_ids, *rest)


def solution(mesh):
    return jax.shard_map(
        on_device,
        mesh=mesh,
        in_specs=(
            P(AXES, None),
            P(AXES, None),
            P(AXES, None),
            P(),
            P(AXES),
            P(AXES, None, None),
            P(AXES, None, None),
            P(AXES, None, None),
        ),
        out_specs=P(AXES, None),
        check_vma=False,
    )
```

```python
import functools

import jax
import jax.numpy as jnp
from jax import lax
from jax.experimental import pallas as pl
from jax.experimental.pallas import tpu as pltpu
from jax.sharding import PartitionSpec as P

AXES = ("dp", "expert")
LANES = 128
PARTS = 4
VMEM_MIB = 8
ROWS_AT_ONCE = 8


def partner(value, axis, distance):
    mask = 2**distance
    pairs = [(source, source ^ mask) for source in range(lax.axis_size(axis))]
    return lax.ppermute(value, axis, pairs)


def exchange(value):
    return lax.all_to_all(
        lax.all_to_all(value, "dp", split_axis=0, concat_axis=0, tiled=True),
        "expert",
        split_axis=1,
        concat_axis=1,
        tiled=True,
    )


def sparse(tokens, expert_ids, route_weight, slot_of, swap_flag, w_gate, w_up, w_down):
    dp_count = lax.axis_size("dp")
    ex_count = lax.axis_size("expert")
    slot_count = dp_count * ex_count
    tok_rows, model_width = tokens.shape
    top_count = expert_ids.shape[1]
    experts = slot_of.shape[0]
    capacity = 2 * tok_rows * top_count // experts
    moved_shards = partner((w_gate, w_up, w_down), "dp", 0)
    taking = swap_flag[0] == 1
    gate_w = jnp.where(taking, moved_shards[0][0], w_gate[0])
    up_w = jnp.where(taking, moved_shards[1][0], w_up[0])
    down_w = jnp.where(taking, moved_shards[2][0], w_down[0])
    pair_count = tok_rows * top_count
    flat_ids = expert_ids.reshape(pair_count)
    onehot = (flat_ids[:, None] == jnp.arange(experts, dtype=jnp.int32)).astype(jnp.int32)
    order_rank = jnp.sum((jnp.cumsum(onehot, axis=0) - onehot) * onehot, axis=1)
    dest_slot = jnp.sum(onehot[:, :, None] * slot_of[None, :, :], axis=1)
    position = dest_slot * capacity + order_rank[:, None]
    pair_ids = jnp.broadcast_to(jnp.arange(pair_count, dtype=jnp.int32)[:, None], (pair_count, 2))
    owner = (
        jnp.full((slot_count * capacity,), -1, jnp.int32)
        .at[position.reshape(-1)]
        .set(pair_ids.reshape(-1))
    )
    token_row = jnp.maximum(owner, 0) // top_count
    outbox = jnp.where((owner >= 0)[:, None], tokens[token_row], jnp.zeros((), tokens.dtype))
    outbox = outbox.reshape(dp_count, ex_count, capacity, model_width)
    arrived = exchange(outbox).reshape(slot_count * capacity, model_width)
    gate_sum = jnp.dot(arrived, gate_w, preferred_element_type=jnp.float32)
    up_sum = jnp.dot(arrived, up_w, preferred_element_type=jnp.float32)
    hidden = (jax.nn.silu(gate_sum) * up_sum).astype(jnp.bfloat16)
    partial_out = jnp.dot(hidden, down_w, preferred_element_type=jnp.float32).astype(jnp.bfloat16)
    partial_out = partial_out.reshape(dp_count, ex_count, capacity, model_width)
    returned = exchange(partial_out).reshape(slot_count * capacity, model_width)
    picked = returned[position].astype(jnp.float32)
    scaled = jnp.sum(picked, axis=1) * route_weight.reshape(pair_count)[:, None]
    return jnp.sum(scaled.reshape(tok_rows, top_count, model_width), axis=1).astype(jnp.bfloat16)


def permute(value, move):
    ex_count = lax.axis_size("expert")
    pairs = []
    for source in range(lax.axis_size("dp") * ex_count):
        d, e = move(*divmod(source, ex_count))
        pairs.append((source, d * ex_count + e))
    return lax.ppermute(value, AXES, pairs)


def to_sibling(d, e):
    return d ^ 1, e


def over_first(d, e):
    return (d ^ 2, e) if d % 2 else (d, e ^ 1)


def over_second(d, e):
    return (d, e ^ 1) if d % 2 else (d ^ 2, e)


def along_line(distance):
    return lambda d, e: (d, e ^ (2 * distance))


def pack_kernel(slots, flag, tokens_hbm, ids_hbm, weights_hbm, mine, *outs_and_scratch):
    *outs, square, tokens, ids, weights, sems = outs_and_scratch
    loads = [
        pltpu.make_async_copy(source, target, sems.at[k])
        for k, (source, target) in enumerate(((ids_hbm, ids), (weights_hbm, weights), (tokens_hbm, tokens)))
    ]
    for load in loads:
        load.start()
    d = lax.axis_index("dp")
    serving = jnp.where(flag[0] == 1, d ^ 1, d) * lax.axis_size("expert") + lax.axis_index("expert")
    expert = jnp.int32(0)
    for half in range(slots.shape[0]):
        for number in range(slots.shape[1]):
            expert += jnp.where(slots[half, number] == serving, number, 0)
    mine[0] = expert
    top_count, tok_rows = ids.shape
    square[...] = jnp.zeros_like(square)
    loads[0].wait()
    loads[1].wait()
    square[:top_count, :tok_rows] = ids[...].astype(jnp.float32)
    rest = weights[...]
    for k in range(1, 4):
        part = rest.astype(jnp.bfloat16).astype(jnp.float32)
        square[k * top_count : (k + 1) * top_count, :tok_rows] = part
        rest = rest - part
    extra = square[...].T.astype(jnp.bfloat16)
    loads[2].wait()
    at = 0
    for out in outs:
        rows, packed_width = out.shape
        out[...] = jnp.concatenate([tokens[at : at + rows], extra[at : at + rows]], axis=1)
        at += rows


def in_hbm(*arrays):
    return [pltpu.with_memory_space_constraint(array, pltpu.HBM) for array in arrays]


def packed(tokens, expert_ids, route_weight, slot_of, swap_flag, rows):
    tok_rows, width = tokens.shape
    side = -(-max(tok_rows, 4 * expert_ids.shape[1]) // LANES) * LANES
    scalars = pl.BlockSpec(memory_space=pltpu.SMEM)
    whole = pl.BlockSpec(memory_space=pltpu.VMEM)
    count = tok_rows // rows
    mine, *owns = pl.pallas_call(
        pack_kernel,
        out_shape=(jax.ShapeDtypeStruct((1,), jnp.int32),) + (pltpu.VMEM((rows, width + side), tokens.dtype),) * count,
        in_specs=[scalars] * 2 + [pl.BlockSpec(memory_space=pl.ANY)] * 3,
        out_specs=(scalars,) + (whole,) * count,
        scratch_shapes=[
            pltpu.VMEM((side, side), jnp.float32),
            pltpu.VMEM(tokens.shape, tokens.dtype),
            pltpu.VMEM(expert_ids.shape[::-1], expert_ids.dtype),
            pltpu.VMEM(route_weight.shape[::-1], route_weight.dtype),
            pltpu.SemaphoreType.DMA((3,)),
        ],
        compiler_params=pltpu.CompilerParams(vmem_limit_bytes=VMEM_MIB * 2**20),
        cost_estimate=pl.CostEstimate(flops=10**10, bytes_accessed=4 * tok_rows * width, transcendentals=0),
        name="pack_rows",
    )(*in_hbm(slot_of.T), swap_flag, *in_hbm(tokens, expert_ids.T, route_weight.T))
    return mine, owns


def scale_of(extra, mine, top_count):
    extra = extra.astype(jnp.float32)
    ids, hi, mid, lo = (extra[:, k * top_count : (k + 1) * top_count] for k in range(4))
    return jnp.sum(jnp.where(ids == mine, hi + mid + lo, 0.0), axis=1, keepdims=True)


def serve_kernel(top_count, mine, own, sib, w_gate, w_up, w_down, out_own, out_sib):
    rows = own.shape[0]
    width, hidden_width = w_gate.shape
    depth = width // PARTS
    gate_sum = jnp.zeros((2 * rows, hidden_width), jnp.float32)
    up_sum = jnp.zeros((2 * rows, hidden_width), jnp.float32)
    for k in range(PARTS):
        part = pl.ds(k * depth, depth)
        x = jnp.concatenate([own[:, part], sib[:, part]])
        gate_sum += jnp.dot(x, w_gate[part], preferred_element_type=jnp.float32)
        up_sum += jnp.dot(x, w_up[part], preferred_element_type=jnp.float32)
    hidden = (gate_sum / (1.0 + jnp.exp(-gate_sum)) * up_sum).astype(jnp.bfloat16)
    extra = jnp.concatenate([own[:, width:], sib[:, width:]])
    scale = scale_of(extra, mine[0].astype(jnp.float32), top_count)
    for k in range(PARTS):
        part = pl.ds(k * depth, depth)
        served = jnp.dot(hidden, w_down[:, part], preferred_element_type=jnp.float32) * scale
        out_own[:, part] = served[:rows].astype(jnp.bfloat16)
        out_sib[:, part] = served[rows:].astype(jnp.bfloat16)


def serve_rows(own, sib, mine, top_count, w_gate, w_up, w_down):
    rows, packed_width = own.shape
    width, hidden_width = w_gate.shape
    whole = pl.BlockSpec(memory_space=pltpu.VMEM)
    out = jax.ShapeDtypeStruct((rows, width), jnp.bfloat16)
    moved = 2 * (4 * rows * width + 3 * width * hidden_width)
    return pl.pallas_call(
        functools.partial(serve_kernel, top_count),
        out_shape=(out, out),
        in_specs=[pl.BlockSpec(memory_space=pltpu.SMEM)] + [whole] * 5,
        out_specs=(whole, whole),
        compiler_params=pltpu.CompilerParams(vmem_limit_bytes=VMEM_MIB * 2**20),
        cost_estimate=pl.CostEstimate(
            flops=12 * rows * width * hidden_width, bytes_accessed=moved, transcendentals=2 * rows * hidden_width
        ),
        name="serve_rows",
    )(mine, own, sib, w_gate, w_up, w_down)


def total(*terms):
    return sum(term.astype(jnp.float32) for term in terms).astype(jnp.bfloat16)


def chunk_steps(own, moves, serve):
    rows = own.shape[0]
    (held,) = yield (own,)
    for move in moves:
        (got,) = yield (permute(held, move),)
        held = jnp.concatenate([held, got])
    (sib,) = yield (permute(held, to_sibling),)
    out, out_sib = serve(held, sib)
    (out_sib,) = yield (out_sib,)
    (got,) = yield (permute(out_sib, to_sibling),)
    terms = [out]
    for move in moves[::-1]:
        terms.append(got)
        half = got.shape[0] // 2
        sent = total(*[term[half : 2 * half] for term in terms])
        (got,) = yield (permute(sent, move),)
    terms.append(got)
    return total(*[term[:rows] for term in terms])


def run_steps(chunks):
    waits = [next(chunk) for chunk in chunks]
    results = [None] * len(chunks)
    while any(result is None for result in results):
        for i, chunk in enumerate(chunks):
            try:
                waits[i] = chunk.send(waits[i]) if results[i] is None else None
            except StopIteration as end:
                results[i] = end.value
    return results


def dense(tokens, expert_ids, route_weight, slot_of, swap_flag, w_gate, w_up, w_down):
    tok_rows = tokens.shape[0]
    top_count = expert_ids.shape[1]
    line_bits = (lax.axis_size("expert") // 2).bit_length() - 1
    along = [along_line(2**bit) for bit in range(line_bits)][::-1]
    across = [over_first, over_second]
    routes = [along + across, along[:1] + across + along[1:]]
    step = ROWS_AT_ONCE if tok_rows % ROWS_AT_ONCE == 0 else tok_rows
    mine, owns = packed(tokens, expert_ids, route_weight, slot_of, swap_flag, step)
    serve = lambda held, sib: serve_rows(held, sib, mine, top_count, w_gate[0], w_up[0], w_down[0])
    chunks = [chunk_steps(own, routes[i % len(routes)], serve) for i, own in enumerate(owns)]
    return jnp.concatenate(run_steps(chunks))


def on_device(tokens, expert_ids, *rest):
    slot_of = rest[1]
    ex_count = lax.axis_size("expert")
    capacity = 2 * tokens.shape[0] * expert_ids.shape[1] // slot_of.shape[0]
    paired = lax.axis_size("dp") == 4 and ex_count >= 2 and ex_count & (ex_count - 1) == 0
    serve = dense if capacity >= tokens.shape[0] and paired else sparse
    return serve(tokens, expert_ids, *rest)


def solution(mesh):
    return jax.shard_map(
        on_device,
        mesh=mesh,
        in_specs=(
            P(AXES, None),
            P(AXES, None),
            P(AXES, None),
            P(),
            P(AXES),
            P(AXES, None, None),
            P(AXES, None, None),
            P(AXES, None, None),
        ),
        out_specs=P(AXES, None),
        check_vma=False,
    )
```

```python
import functools

import jax
import jax.numpy as jnp
from jax import lax
from jax.experimental import pallas as pl
from jax.experimental.pallas import tpu as pltpu
from jax.sharding import PartitionSpec as P

AXES = ("dp", "expert")
LANES = 128
COLUMNS = 256
VMEM_MIB = 10
ROWS_AT_ONCE = 8


def partner(value, axis, distance):
    mask = 2**distance
    pairs = [(source, source ^ mask) for source in range(lax.axis_size(axis))]
    return lax.ppermute(value, axis, pairs)


def exchange(value):
    return lax.all_to_all(
        lax.all_to_all(value, "dp", split_axis=0, concat_axis=0, tiled=True),
        "expert",
        split_axis=1,
        concat_axis=1,
        tiled=True,
    )


def sparse(tokens, expert_ids, route_weight, slot_of, swap_flag, w_gate, w_up, w_down):
    dp_count = lax.axis_size("dp")
    ex_count = lax.axis_size("expert")
    slot_count = dp_count * ex_count
    tok_rows, model_width = tokens.shape
    top_count = expert_ids.shape[1]
    experts = slot_of.shape[0]
    capacity = 2 * tok_rows * top_count // experts
    moved_shards = partner((w_gate, w_up, w_down), "dp", 0)
    taking = swap_flag[0] == 1
    gate_w = jnp.where(taking, moved_shards[0][0], w_gate[0])
    up_w = jnp.where(taking, moved_shards[1][0], w_up[0])
    down_w = jnp.where(taking, moved_shards[2][0], w_down[0])
    pair_count = tok_rows * top_count
    flat_ids = expert_ids.reshape(pair_count)
    onehot = (flat_ids[:, None] == jnp.arange(experts, dtype=jnp.int32)).astype(jnp.int32)
    order_rank = jnp.sum((jnp.cumsum(onehot, axis=0) - onehot) * onehot, axis=1)
    dest_slot = jnp.sum(onehot[:, :, None] * slot_of[None, :, :], axis=1)
    position = dest_slot * capacity + order_rank[:, None]
    pair_ids = jnp.broadcast_to(jnp.arange(pair_count, dtype=jnp.int32)[:, None], (pair_count, 2))
    owner = (
        jnp.full((slot_count * capacity,), -1, jnp.int32)
        .at[position.reshape(-1)]
        .set(pair_ids.reshape(-1))
    )
    token_row = jnp.maximum(owner, 0) // top_count
    outbox = jnp.where((owner >= 0)[:, None], tokens[token_row], jnp.zeros((), tokens.dtype))
    outbox = outbox.reshape(dp_count, ex_count, capacity, model_width)
    arrived = exchange(outbox).reshape(slot_count * capacity, model_width)
    gate_sum = jnp.dot(arrived, gate_w, preferred_element_type=jnp.float32)
    up_sum = jnp.dot(arrived, up_w, preferred_element_type=jnp.float32)
    hidden = (jax.nn.silu(gate_sum) * up_sum).astype(jnp.bfloat16)
    partial_out = jnp.dot(hidden, down_w, preferred_element_type=jnp.float32).astype(jnp.bfloat16)
    partial_out = partial_out.reshape(dp_count, ex_count, capacity, model_width)
    returned = exchange(partial_out).reshape(slot_count * capacity, model_width)
    picked = returned[position].astype(jnp.float32)
    scaled = jnp.sum(picked, axis=1) * route_weight.reshape(pair_count)[:, None]
    return jnp.sum(scaled.reshape(tok_rows, top_count, model_width), axis=1).astype(jnp.bfloat16)


def permute(value, move):
    ex_count = lax.axis_size("expert")
    pairs = []
    for source in range(lax.axis_size("dp") * ex_count):
        d, e = move(*divmod(source, ex_count))
        pairs.append((source, d * ex_count + e))
    return lax.ppermute(value, AXES, pairs)


def to_sibling(d, e):
    return d ^ 1, e


def over_first(d, e):
    return (d ^ 2, e) if d % 2 else (d, e ^ 1)


def over_second(d, e):
    return (d, e ^ 1) if d % 2 else (d ^ 2, e)


def along_line(distance):
    return lambda d, e: (d, e ^ (2 * distance))


def expert_kernel(slots, flag, mine):
    d = lax.axis_index("dp")
    serving = jnp.where(flag[0] == 1, d ^ 1, d) * lax.axis_size("expert") + lax.axis_index("expert")
    expert = jnp.int32(0)
    for half in range(slots.shape[0]):
        for number in range(slots.shape[1]):
            expert += jnp.where(slots[half, number] == serving, number, 0)
    mine[0] = expert


def served_expert(slot_of, swap_flag):
    scalars = pl.BlockSpec(memory_space=pltpu.SMEM)
    return pl.pallas_call(
        expert_kernel,
        out_shape=jax.ShapeDtypeStruct((1,), jnp.int32),
        in_specs=[scalars] * 2,
        out_specs=scalars,
        compiler_params=pltpu.CompilerParams(vmem_limit_bytes=2**20),
        cost_estimate=pl.CostEstimate(flops=10**10, bytes_accessed=0, transcendentals=0),
        name="served_expert",
    )(*in_hbm(slot_of.T), swap_flag)


def pack_kernel(tokens_hbm, ids_hbm, weights_hbm, *outs_and_scratch):
    *outs, square, tokens, ids, weights, sems = outs_and_scratch
    loads = [
        pltpu.make_async_copy(source, target, sems.at[k])
        for k, (source, target) in enumerate(((ids_hbm, ids), (weights_hbm, weights), (tokens_hbm, tokens)))
    ]
    for load in loads:
        load.start()
    top_count, tok_rows = ids.shape
    square[...] = jnp.zeros_like(square)
    loads[0].wait()
    loads[1].wait()
    square[:top_count, :tok_rows] = ids[...].astype(jnp.float32)
    rest = weights[...]
    for k in range(1, 4):
        part = rest.astype(jnp.bfloat16).astype(jnp.float32)
        square[k * top_count : (k + 1) * top_count, :tok_rows] = part
        rest = rest - part
    extra = square[...].T.astype(jnp.bfloat16)
    loads[2].wait()
    at = 0
    for out in outs:
        rows, packed_width = out.shape
        out[...] = jnp.concatenate([tokens[at : at + rows], extra[at : at + rows]], axis=1)
        at += rows


def in_hbm(*arrays):
    return [pltpu.with_memory_space_constraint(array, pltpu.HBM) for array in arrays]


def packed(tokens, expert_ids, route_weight, rows):
    tok_rows, width = tokens.shape
    side = -(-max(tok_rows, 4 * expert_ids.shape[1]) // LANES) * LANES
    whole = pl.BlockSpec(memory_space=pltpu.VMEM)
    count = tok_rows // rows
    return pl.pallas_call(
        pack_kernel,
        out_shape=(pltpu.VMEM((rows, width + side), tokens.dtype),) * count,
        in_specs=[pl.BlockSpec(memory_space=pl.ANY)] * 3,
        out_specs=(whole,) * count,
        scratch_shapes=[
            pltpu.VMEM((side, side), jnp.float32),
            pltpu.VMEM(tokens.shape, tokens.dtype),
            pltpu.VMEM(expert_ids.shape[::-1], expert_ids.dtype),
            pltpu.VMEM(route_weight.shape[::-1], route_weight.dtype),
            pltpu.SemaphoreType.DMA((3,)),
        ],
        compiler_params=pltpu.CompilerParams(vmem_limit_bytes=VMEM_MIB * 2**20),
        cost_estimate=pl.CostEstimate(flops=0, bytes_accessed=4 * tok_rows * width, transcendentals=0),
        name="pack_rows",
    )(*in_hbm(tokens, expert_ids.T, route_weight.T))


def scale_of(extra, mine, top_count):
    extra = extra.astype(jnp.float32)
    ids, hi, mid, lo = (extra[:, k * top_count : (k + 1) * top_count] for k in range(4))
    return jnp.sum(jnp.where(ids == mine, hi + mid + lo, 0.0), axis=1, keepdims=True)


def serve_kernel(top_count, mine, own, sib, w_gate, w_up, w_down, out_own, out_sib, x, hidden):
    rows = own.shape[0]
    width, hidden_width = w_gate.shape
    x[:rows] = own[:, :width]
    x[rows:] = sib[:, :width]
    for at in range(0, hidden_width, COLUMNS):
        part = pl.ds(at, COLUMNS)
        gate_sum = jnp.dot(x[...], w_gate[:, part], preferred_element_type=jnp.float32)
        up_sum = jnp.dot(x[...], w_up[:, part], preferred_element_type=jnp.float32)
        hidden[:, part] = (gate_sum / (1.0 + jnp.exp(-gate_sum)) * up_sum).astype(jnp.bfloat16)
    extra = jnp.concatenate([own[:, width:], sib[:, width:]])
    scale = scale_of(extra, mine[0].astype(jnp.float32), top_count)
    for at in range(0, width, COLUMNS):
        part = pl.ds(at, COLUMNS)
        served = jnp.dot(hidden[...], w_down[:, part], preferred_element_type=jnp.float32) * scale
        out_own[:, part] = served[:rows].astype(jnp.bfloat16)
        out_sib[:, part] = served[rows:].astype(jnp.bfloat16)


def serve_rows(own, sib, mine, top_count, w_gate, w_up, w_down):
    rows, packed_width = own.shape
    width, hidden_width = w_gate.shape
    whole = pl.BlockSpec(memory_space=pltpu.VMEM)
    out = jax.ShapeDtypeStruct((rows, width), jnp.bfloat16)
    moved = 2 * (4 * rows * width + 3 * width * hidden_width)
    return pl.pallas_call(
        functools.partial(serve_kernel, top_count),
        out_shape=(out, out),
        in_specs=[pl.BlockSpec(memory_space=pltpu.SMEM)] + [whole] * 5,
        out_specs=(whole, whole),
        scratch_shapes=[
            pltpu.VMEM((2 * rows, width), jnp.bfloat16),
            pltpu.VMEM((2 * rows, hidden_width), jnp.bfloat16),
        ],
        compiler_params=pltpu.CompilerParams(vmem_limit_bytes=VMEM_MIB * 2**20),
        cost_estimate=pl.CostEstimate(
            flops=12 * rows * width * hidden_width, bytes_accessed=moved, transcendentals=2 * rows * hidden_width
        ),
        name="serve_rows",
    )(mine, own, sib, w_gate, w_up, w_down)


def total(*terms):
    return sum(term.astype(jnp.float32) for term in terms).astype(jnp.bfloat16)


def chunk_steps(own, moves, serve, beside):
    rows = own.shape[0]
    (held,) = yield (own,)
    for move in moves:
        (got,) = yield (permute(held, move),)
        if move is moves[0] and beside:
            got = lax.optimization_barrier((got, *beside))[0]
        held = jnp.concatenate([held, got])
    (sib,) = yield (permute(held, to_sibling),)
    out, out_sib = serve(held, sib)
    (out_sib,) = yield (out_sib,)
    (got,) = yield (permute(out_sib, to_sibling),)
    terms = [out]
    for move in moves[::-1]:
        terms.append(got)
        half = got.shape[0] // 2
        sent = total(*[term[half : 2 * half] for term in terms])
        (got,) = yield (permute(sent, move),)
    terms.append(got)
    return total(*[term[:rows] for term in terms])


def run_steps(chunks):
    waits = [next(chunk) for chunk in chunks]
    results = [None] * len(chunks)
    while any(result is None for result in results):
        for i, chunk in enumerate(chunks):
            try:
                waits[i] = chunk.send(waits[i]) if results[i] is None else None
            except StopIteration as end:
                results[i] = end.value
    return results


def dense(tokens, expert_ids, route_weight, slot_of, swap_flag, w_gate, w_up, w_down):
    tok_rows = tokens.shape[0]
    top_count = expert_ids.shape[1]
    line_bits = (lax.axis_size("expert") // 2).bit_length() - 1
    along = [along_line(2**bit) for bit in range(line_bits)][::-1]
    across = [over_first, over_second]
    routes = [along + across, along[:1] + across + along[1:]]
    step = ROWS_AT_ONCE if tok_rows % ROWS_AT_ONCE == 0 else tok_rows
    owns = packed(tokens, expert_ids, route_weight, step)
    mine = served_expert(slot_of, lax.optimization_barrier((swap_flag, owns[0]))[0])
    serve = lambda held, sib: serve_rows(held, sib, mine, top_count, w_gate[0], w_up[0], w_down[0])
    chunks = [chunk_steps(own, routes[i % len(routes)], serve, (mine,) if i == 1 else ()) for i, own in enumerate(owns)]
    return jnp.concatenate(run_steps(chunks))


def on_device(tokens, expert_ids, *rest):
    slot_of = rest[1]
    ex_count = lax.axis_size("expert")
    capacity = 2 * tokens.shape[0] * expert_ids.shape[1] // slot_of.shape[0]
    paired = lax.axis_size("dp") == 4 and ex_count >= 2 and ex_count & (ex_count - 1) == 0
    serve = dense if capacity >= tokens.shape[0] and paired else sparse
    return serve(tokens, expert_ids, *rest)


def solution(mesh):
    return jax.shard_map(
        on_device,
        mesh=mesh,
        in_specs=(
            P(AXES, None),
            P(AXES, None),
            P(AXES, None),
            P(),
            P(AXES),
            P(AXES, None, None),
            P(AXES, None, None),
            P(AXES, None, None),
        ),
        out_specs=P(AXES, None),
        check_vma=False,
    )
```

```python
import functools

import jax
import jax.numpy as jnp
from jax import lax
from jax.experimental import pallas as pl
from jax.experimental.pallas import tpu as pltpu
from jax.sharding import PartitionSpec as P

AXES = ("dp", "expert")
LANES = 128
COLUMNS = 256
VMEM_MIB = 10
ROWS_AT_ONCE = 8
GUARDS = [(2, 5, 0, 7), (1, 5, 2, 4), (1, 4, 0, 6), (0, 8, 2, 7), (0, 9, 2, 8), (0, 10, 2, 9)]


def partner(value, axis, distance):
    mask = 2**distance
    pairs = [(source, source ^ mask) for source in range(lax.axis_size(axis))]
    return lax.ppermute(value, axis, pairs)


def exchange(value):
    return lax.all_to_all(
        lax.all_to_all(value, "dp", split_axis=0, concat_axis=0, tiled=True),
        "expert",
        split_axis=1,
        concat_axis=1,
        tiled=True,
    )


def sparse(tokens, expert_ids, route_weight, slot_of, swap_flag, w_gate, w_up, w_down):
    dp_count = lax.axis_size("dp")
    ex_count = lax.axis_size("expert")
    slot_count = dp_count * ex_count
    tok_rows, model_width = tokens.shape
    top_count = expert_ids.shape[1]
    experts = slot_of.shape[0]
    capacity = 2 * tok_rows * top_count // experts
    moved_shards = partner((w_gate, w_up, w_down), "dp", 0)
    taking = swap_flag[0] == 1
    gate_w = jnp.where(taking, moved_shards[0][0], w_gate[0])
    up_w = jnp.where(taking, moved_shards[1][0], w_up[0])
    down_w = jnp.where(taking, moved_shards[2][0], w_down[0])
    pair_count = tok_rows * top_count
    flat_ids = expert_ids.reshape(pair_count)
    onehot = (flat_ids[:, None] == jnp.arange(experts, dtype=jnp.int32)).astype(jnp.int32)
    order_rank = jnp.sum((jnp.cumsum(onehot, axis=0) - onehot) * onehot, axis=1)
    dest_slot = jnp.sum(onehot[:, :, None] * slot_of[None, :, :], axis=1)
    position = dest_slot * capacity + order_rank[:, None]
    pair_ids = jnp.broadcast_to(jnp.arange(pair_count, dtype=jnp.int32)[:, None], (pair_count, 2))
    owner = (
        jnp.full((slot_count * capacity,), -1, jnp.int32)
        .at[position.reshape(-1)]
        .set(pair_ids.reshape(-1))
    )
    token_row = jnp.maximum(owner, 0) // top_count
    outbox = jnp.where((owner >= 0)[:, None], tokens[token_row], jnp.zeros((), tokens.dtype))
    outbox = outbox.reshape(dp_count, ex_count, capacity, model_width)
    arrived = exchange(outbox).reshape(slot_count * capacity, model_width)
    gate_sum = jnp.dot(arrived, gate_w, preferred_element_type=jnp.float32)
    up_sum = jnp.dot(arrived, up_w, preferred_element_type=jnp.float32)
    hidden = (jax.nn.silu(gate_sum) * up_sum).astype(jnp.bfloat16)
    partial_out = jnp.dot(hidden, down_w, preferred_element_type=jnp.float32).astype(jnp.bfloat16)
    partial_out = partial_out.reshape(dp_count, ex_count, capacity, model_width)
    returned = exchange(partial_out).reshape(slot_count * capacity, model_width)
    picked = returned[position].astype(jnp.float32)
    scaled = jnp.sum(picked, axis=1) * route_weight.reshape(pair_count)[:, None]
    return jnp.sum(scaled.reshape(tok_rows, top_count, model_width), axis=1).astype(jnp.bfloat16)


def permute(value, move):
    ex_count = lax.axis_size("expert")
    pairs = []
    for source in range(lax.axis_size("dp") * ex_count):
        d, e = move(*divmod(source, ex_count))
        pairs.append((source, d * ex_count + e))
    return lax.ppermute(value, AXES, pairs)


def to_sibling(d, e):
    return d ^ 1, e


def over_first(d, e):
    return (d ^ 2, e) if d % 2 else (d, e ^ 1)


def over_second(d, e):
    return (d, e ^ 1) if d % 2 else (d ^ 2, e)


def along_line(distance):
    return lambda d, e: (d, e ^ (2 * distance))


def expert_kernel(slots, flag, mine):
    d = lax.axis_index("dp")
    serving = jnp.where(flag[0] == 1, d ^ 1, d) * lax.axis_size("expert") + lax.axis_index("expert")
    expert = jnp.int32(0)
    for half in range(slots.shape[0]):
        for number in range(slots.shape[1]):
            expert += jnp.where(slots[half, number] == serving, number, 0)
    mine[0] = expert


def served_expert(slot_of, swap_flag):
    scalars = pl.BlockSpec(memory_space=pltpu.SMEM)
    return pl.pallas_call(
        expert_kernel,
        out_shape=jax.ShapeDtypeStruct((1,), jnp.int32),
        in_specs=[scalars] * 2,
        out_specs=scalars,
        compiler_params=pltpu.CompilerParams(vmem_limit_bytes=2**20),
        cost_estimate=pl.CostEstimate(flops=10**10, bytes_accessed=0, transcendentals=0),
        name="served_expert",
    )(*in_hbm(slot_of.T), swap_flag)


def pack_kernel(tokens_hbm, ids_hbm, weights_hbm, *outs_and_scratch):
    *outs, square, tokens, ids, weights, sems = outs_and_scratch
    loads = [
        pltpu.make_async_copy(source, target, sems.at[k])
        for k, (source, target) in enumerate(((ids_hbm, ids), (weights_hbm, weights), (tokens_hbm, tokens)))
    ]
    for load in loads:
        load.start()
    top_count, tok_rows = ids.shape
    square[...] = jnp.zeros_like(square)
    loads[0].wait()
    loads[1].wait()
    square[:top_count, :tok_rows] = ids[...].astype(jnp.float32)
    rest = weights[...]
    for k in range(1, 4):
        part = rest.astype(jnp.bfloat16).astype(jnp.float32)
        square[k * top_count : (k + 1) * top_count, :tok_rows] = part
        rest = rest - part
    extra = square[...].T.astype(jnp.bfloat16)
    loads[2].wait()
    at = 0
    for out in outs:
        rows, packed_width = out.shape
        out[...] = jnp.concatenate([tokens[at : at + rows], extra[at : at + rows]], axis=1)
        at += rows


def in_hbm(*arrays):
    return [pltpu.with_memory_space_constraint(array, pltpu.HBM) for array in arrays]


def packed(tokens, expert_ids, route_weight, rows):
    tok_rows, width = tokens.shape
    side = -(-max(tok_rows, 4 * expert_ids.shape[1]) // LANES) * LANES
    whole = pl.BlockSpec(memory_space=pltpu.VMEM)
    count = tok_rows // rows
    return pl.pallas_call(
        pack_kernel,
        out_shape=(pltpu.VMEM((rows, width + side), tokens.dtype),) * count,
        in_specs=[pl.BlockSpec(memory_space=pl.ANY)] * 3,
        out_specs=(whole,) * count,
        scratch_shapes=[
            pltpu.VMEM((side, side), jnp.float32),
            pltpu.VMEM(tokens.shape, tokens.dtype),
            pltpu.VMEM(expert_ids.shape[::-1], expert_ids.dtype),
            pltpu.VMEM(route_weight.shape[::-1], route_weight.dtype),
            pltpu.SemaphoreType.DMA((3,)),
        ],
        compiler_params=pltpu.CompilerParams(vmem_limit_bytes=VMEM_MIB * 2**20),
        cost_estimate=pl.CostEstimate(flops=0, bytes_accessed=4 * tok_rows * width, transcendentals=0),
        name="pack_rows",
    )(*in_hbm(tokens, expert_ids.T, route_weight.T))


def scale_of(extra, mine, top_count):
    extra = extra.astype(jnp.float32)
    ids, hi, mid, lo = (extra[:, k * top_count : (k + 1) * top_count] for k in range(4))
    return jnp.sum(jnp.where(ids == mine, hi + mid + lo, 0.0), axis=1, keepdims=True)


def serve_kernel(top_count, mine, own, sib, w_gate, w_up, w_down, out_own, out_sib, x, hidden):
    rows = own.shape[0]
    width, hidden_width = w_gate.shape
    x[:rows] = own[:, :width]
    x[rows:] = sib[:, :width]
    for at in range(0, hidden_width, COLUMNS):
        part = pl.ds(at, COLUMNS)
        gate_sum = jnp.dot(x[...], w_gate[:, part], preferred_element_type=jnp.float32)
        up_sum = jnp.dot(x[...], w_up[:, part], preferred_element_type=jnp.float32)
        hidden[:, part] = (gate_sum / (1.0 + jnp.exp(-gate_sum)) * up_sum).astype(jnp.bfloat16)
    extra = jnp.concatenate([own[:, width:], sib[:, width:]])
    scale = scale_of(extra, mine[0].astype(jnp.float32), top_count)
    for at in range(0, width, COLUMNS):
        part = pl.ds(at, COLUMNS)
        served = jnp.dot(hidden[...], w_down[:, part], preferred_element_type=jnp.float32) * scale
        out_own[:, part] = served[:rows].astype(jnp.bfloat16)
        out_sib[:, part] = served[rows:].astype(jnp.bfloat16)


def serve_rows(own, sib, mine, top_count, w_gate, w_up, w_down):
    rows, packed_width = own.shape
    width, hidden_width = w_gate.shape
    whole = pl.BlockSpec(memory_space=pltpu.VMEM)
    out = jax.ShapeDtypeStruct((rows, width), jnp.bfloat16)
    moved = 2 * (4 * rows * width + 3 * width * hidden_width)
    return pl.pallas_call(
        functools.partial(serve_kernel, top_count),
        out_shape=(out, out),
        in_specs=[pl.BlockSpec(memory_space=pltpu.SMEM)] + [whole] * 5,
        out_specs=(whole, whole),
        scratch_shapes=[
            pltpu.VMEM((2 * rows, width), jnp.bfloat16),
            pltpu.VMEM((2 * rows, hidden_width), jnp.bfloat16),
        ],
        compiler_params=pltpu.CompilerParams(vmem_limit_bytes=VMEM_MIB * 2**20),
        cost_estimate=pl.CostEstimate(
            flops=12 * rows * width * hidden_width, bytes_accessed=moved, transcendentals=2 * rows * hidden_width
        ),
        name="serve_rows",
    )(mine, own, sib, w_gate, w_up, w_down)


def total(*terms):
    return sum(term.astype(jnp.float32) for term in terms).astype(jnp.bfloat16)


def chunk_steps(own, moves, back, serve, beside):
    rows, packed_width = own.shape
    (held,) = yield (own,)
    for move in moves:
        (got,) = yield (permute(held, move),)
        if move is moves[0] and beside:
            got = lax.optimization_barrier((got, *beside))[0]
        held = jnp.concatenate([held, got])
    (sib,) = yield (permute(held, to_sibling),)
    out, out_sib = serve(held, sib)
    (out_sib,) = yield (out_sib,)
    (got,) = yield (permute(out_sib, to_sibling),)
    left = list(range(len(moves)))[::-1]
    terms = [out.reshape((2,) * len(left) + (rows, -1)), got.reshape((2,) * len(left) + (rows, -1))]
    for number in back:
        at = left.index(number)
        left.remove(number)
        kept, sent = ([lax.index_in_dim(term, k, at, keepdims=False) for term in terms] for k in (0, 1))
        sent = total(*sent).reshape(-1, out.shape[1])
        (got,) = yield (permute(sent, moves[number]),)
        terms = kept + [got.reshape((2,) * len(left) + (rows, -1))]
    return total(*terms)


def run_steps(chunks, guards):
    waits = [[next(chunk)[0]] for chunk in chunks]
    results = [None] * len(chunks)
    while any(result is None for result in results):
        for i, chunk in enumerate(chunks):
            at = len(waits[i]) - 1
            asked = [(j, t) for k, s, j, t in guards if (k, s) == (i, at)]
            if results[i] is not None or any(len(waits[j]) <= t for j, t in asked):
                continue
            ready = tuple(waits[i][-1:])
            if asked:
                ready = lax.optimization_barrier(ready + tuple(waits[j][t] for j, t in asked))[:1]
            try:
                waits[i].append(chunk.send(ready)[0])
            except StopIteration as end:
                results[i] = end.value
    return results


def dense(tokens, expert_ids, route_weight, slot_of, swap_flag, w_gate, w_up, w_down):
    tok_rows = tokens.shape[0]
    top_count = expert_ids.shape[1]
    line_bits = (lax.axis_size("expert") // 2).bit_length() - 1
    along = [along_line(2**bit) for bit in range(line_bits)][::-1]
    across = [over_first, over_second]
    routes = [along + across, along + across, along[:1] + across + along[1:]]
    backs = [[3, 2, 1, 0], [3, 2, 1, 0], [2, 3, 1, 0]] if line_bits == 2 else [range(len(along + across))[::-1]]
    step = ROWS_AT_ONCE if tok_rows % ROWS_AT_ONCE == 0 else tok_rows
    owns = packed(tokens, expert_ids, route_weight, step)
    mine = served_expert(slot_of, lax.optimization_barrier((swap_flag, owns[0]))[0])
    serve = lambda held, sib: serve_rows(held, sib, mine, top_count, w_gate[0], w_up[0], w_down[0])
    chunks = [chunk_steps(own, routes[i % len(routes)], backs[i % len(backs)], serve, (mine,) if i == 1 else ()) for i, own in enumerate(owns)]
    guards = GUARDS if len(chunks) == 3 and line_bits == 2 else []
    return jnp.concatenate(run_steps(chunks, guards))


def on_device(tokens, expert_ids, *rest):
    slot_of = rest[1]
    ex_count = lax.axis_size("expert")
    capacity = 2 * tokens.shape[0] * expert_ids.shape[1] // slot_of.shape[0]
    paired = lax.axis_size("dp") == 4 and ex_count >= 2 and ex_count & (ex_count - 1) == 0
    serve = dense if capacity >= tokens.shape[0] and paired else sparse
    return serve(tokens, expert_ids, *rest)


def solution(mesh):
    return jax.shard_map(
        on_device,
        mesh=mesh,
        in_specs=(
            P(AXES, None),
            P(AXES, None),
            P(AXES, None),
            P(),
            P(AXES),
            P(AXES, None, None),
            P(AXES, None, None),
            P(AXES, None, None),
        ),
        out_specs=P(AXES, None),
        check_vma=False,
    )
```

```python
import functools

import jax
import jax.numpy as jnp
from jax import lax
from jax.experimental import pallas as pl
from jax.experimental.pallas import tpu as pltpu
from jax.sharding import PartitionSpec as P

AXES = ("dp", "expert")
LANES = 128
COLUMNS = 256
VMEM_MIB = 10
ROWS_AT_ONCE = 8
GUARDS = [(2, 6, 0, 7), (1, 5, 2, 4), (1, 4, 0, 6), (1, 7, 0, 5), (0, 9, 2, 8), (0, 10, 2, 9), (0, 8, 2, 8)]


def partner(value, axis, distance):
    mask = 2**distance
    pairs = [(source, source ^ mask) for source in range(lax.axis_size(axis))]
    return lax.ppermute(value, axis, pairs)


def exchange(value):
    return lax.all_to_all(
        lax.all_to_all(value, "dp", split_axis=0, concat_axis=0, tiled=True),
        "expert",
        split_axis=1,
        concat_axis=1,
        tiled=True,
    )


def sparse(tokens, expert_ids, route_weight, slot_of, swap_flag, w_gate, w_up, w_down):
    dp_count = lax.axis_size("dp")
    ex_count = lax.axis_size("expert")
    slot_count = dp_count * ex_count
    tok_rows, model_width = tokens.shape
    top_count = expert_ids.shape[1]
    experts = slot_of.shape[0]
    capacity = 2 * tok_rows * top_count // experts
    moved_shards = partner((w_gate, w_up, w_down), "dp", 0)
    taking = swap_flag[0] == 1
    gate_w = jnp.where(taking, moved_shards[0][0], w_gate[0])
    up_w = jnp.where(taking, moved_shards[1][0], w_up[0])
    down_w = jnp.where(taking, moved_shards[2][0], w_down[0])
    pair_count = tok_rows * top_count
    flat_ids = expert_ids.reshape(pair_count)
    onehot = (flat_ids[:, None] == jnp.arange(experts, dtype=jnp.int32)).astype(jnp.int32)
    order_rank = jnp.sum((jnp.cumsum(onehot, axis=0) - onehot) * onehot, axis=1)
    dest_slot = jnp.sum(onehot[:, :, None] * slot_of[None, :, :], axis=1)
    position = dest_slot * capacity + order_rank[:, None]
    pair_ids = jnp.broadcast_to(jnp.arange(pair_count, dtype=jnp.int32)[:, None], (pair_count, 2))
    owner = (
        jnp.full((slot_count * capacity,), -1, jnp.int32)
        .at[position.reshape(-1)]
        .set(pair_ids.reshape(-1))
    )
    token_row = jnp.maximum(owner, 0) // top_count
    outbox = jnp.where((owner >= 0)[:, None], tokens[token_row], jnp.zeros((), tokens.dtype))
    outbox = outbox.reshape(dp_count, ex_count, capacity, model_width)
    arrived = exchange(outbox).reshape(slot_count * capacity, model_width)
    gate_sum = jnp.dot(arrived, gate_w, preferred_element_type=jnp.float32)
    up_sum = jnp.dot(arrived, up_w, preferred_element_type=jnp.float32)
    hidden = (jax.nn.silu(gate_sum) * up_sum).astype(jnp.bfloat16)
    partial_out = jnp.dot(hidden, down_w, preferred_element_type=jnp.float32).astype(jnp.bfloat16)
    partial_out = partial_out.reshape(dp_count, ex_count, capacity, model_width)
    returned = exchange(partial_out).reshape(slot_count * capacity, model_width)
    picked = returned[position].astype(jnp.float32)
    scaled = jnp.sum(picked, axis=1) * route_weight.reshape(pair_count)[:, None]
    return jnp.sum(scaled.reshape(tok_rows, top_count, model_width), axis=1).astype(jnp.bfloat16)


def permute(value, move):
    ex_count = lax.axis_size("expert")
    pairs = []
    for source in range(lax.axis_size("dp") * ex_count):
        d, e = move(*divmod(source, ex_count))
        pairs.append((source, d * ex_count + e))
    return lax.ppermute(value, AXES, pairs)


def to_sibling(d, e):
    return d ^ 1, e


def over_first(d, e):
    return (d ^ 2, e) if d % 2 else (d, e ^ 1)


def over_second(d, e):
    return (d, e ^ 1) if d % 2 else (d ^ 2, e)


def along_line(distance):
    return lambda d, e: (d, e ^ (2 * distance))


def expert_kernel(slots, flag, mine):
    d = lax.axis_index("dp")
    serving = jnp.where(flag[0] == 1, d ^ 1, d) * lax.axis_size("expert") + lax.axis_index("expert")
    expert = jnp.int32(0)
    for half in range(slots.shape[0]):
        for number in range(slots.shape[1]):
            expert += jnp.where(slots[half, number] == serving, number, 0)
    mine[0] = expert


def served_expert(slot_of, swap_flag):
    scalars = pl.BlockSpec(memory_space=pltpu.SMEM)
    return pl.pallas_call(
        expert_kernel,
        out_shape=jax.ShapeDtypeStruct((1,), jnp.int32),
        in_specs=[scalars] * 2,
        out_specs=scalars,
        compiler_params=pltpu.CompilerParams(vmem_limit_bytes=2**20),
        cost_estimate=pl.CostEstimate(flops=10**10, bytes_accessed=0, transcendentals=0),
        name="served_expert",
    )(*in_hbm(slot_of.T), swap_flag)


def pack_kernel(tokens_hbm, ids_hbm, weights_hbm, *outs_and_scratch):
    *outs, square, tokens, ids, weights, sems = outs_and_scratch
    loads = [
        pltpu.make_async_copy(source, target, sems.at[k])
        for k, (source, target) in enumerate(((ids_hbm, ids), (weights_hbm, weights), (tokens_hbm, tokens)))
    ]
    for load in loads:
        load.start()
    top_count, tok_rows = ids.shape
    square[...] = jnp.zeros_like(square)
    loads[0].wait()
    loads[1].wait()
    square[:top_count, :tok_rows] = ids[...].astype(jnp.float32)
    rest = weights[...]
    for k in range(1, 4):
        part = rest.astype(jnp.bfloat16).astype(jnp.float32)
        square[k * top_count : (k + 1) * top_count, :tok_rows] = part
        rest = rest - part
    extra = square[...].T.astype(jnp.bfloat16)
    loads[2].wait()
    at = 0
    for out in outs:
        rows, packed_width = out.shape
        out[...] = jnp.concatenate([tokens[at : at + rows], extra[at : at + rows]], axis=1)
        at += rows


def in_hbm(*arrays):
    return [pltpu.with_memory_space_constraint(array, pltpu.HBM) for array in arrays]


def packed(tokens, expert_ids, route_weight, rows):
    tok_rows, width = tokens.shape
    side = -(-max(tok_rows, 4 * expert_ids.shape[1]) // LANES) * LANES
    whole = pl.BlockSpec(memory_space=pltpu.VMEM)
    count = tok_rows // rows
    return pl.pallas_call(
        pack_kernel,
        out_shape=(pltpu.VMEM((rows, width + side), tokens.dtype),) * count,
        in_specs=[pl.BlockSpec(memory_space=pl.ANY)] * 3,
        out_specs=(whole,) * count,
        scratch_shapes=[
            pltpu.VMEM((side, side), jnp.float32),
            pltpu.VMEM(tokens.shape, tokens.dtype),
            pltpu.VMEM(expert_ids.shape[::-1], expert_ids.dtype),
            pltpu.VMEM(route_weight.shape[::-1], route_weight.dtype),
            pltpu.SemaphoreType.DMA((3,)),
        ],
        compiler_params=pltpu.CompilerParams(vmem_limit_bytes=VMEM_MIB * 2**20),
        cost_estimate=pl.CostEstimate(flops=0, bytes_accessed=4 * tok_rows * width, transcendentals=0),
        name="pack_rows",
    )(*in_hbm(tokens, expert_ids.T, route_weight.T))


def scale_of(extra, mine, top_count):
    extra = extra.astype(jnp.float32)
    ids, hi, mid, lo = (extra[:, k * top_count : (k + 1) * top_count] for k in range(4))
    return jnp.sum(jnp.where(ids == mine, hi + mid + lo, 0.0), axis=1, keepdims=True)


def serve_kernel(top_count, mine, own, sib, w_gate, w_up, w_down, out_own, out_sib, x, hidden):
    rows = own.shape[0]
    width, hidden_width = w_gate.shape
    x[:rows] = own[:, :width]
    x[rows:] = sib[:, :width]
    for at in range(0, hidden_width, COLUMNS):
        part = pl.ds(at, COLUMNS)
        gate_sum = jnp.dot(x[...], w_gate[:, part], preferred_element_type=jnp.float32)
        up_sum = jnp.dot(x[...], w_up[:, part], preferred_element_type=jnp.float32)
        hidden[:, part] = (gate_sum / (1.0 + jnp.exp(-gate_sum)) * up_sum).astype(jnp.bfloat16)
    extra = jnp.concatenate([own[:, width:], sib[:, width:]])
    scale = scale_of(extra, mine[0].astype(jnp.float32), top_count)
    for at in range(0, width, COLUMNS):
        part = pl.ds(at, COLUMNS)
        served = jnp.dot(hidden[...], w_down[:, part], preferred_element_type=jnp.float32) * scale
        out_own[:, part] = served[:rows].astype(jnp.bfloat16)
        out_sib[:, part] = served[rows:].astype(jnp.bfloat16)


def serve_rows(own, sib, mine, top_count, w_gate, w_up, w_down):
    rows, packed_width = own.shape
    width, hidden_width = w_gate.shape
    whole = pl.BlockSpec(memory_space=pltpu.VMEM)
    out = jax.ShapeDtypeStruct((rows, width), jnp.bfloat16)
    moved = 2 * (4 * rows * width + 3 * width * hidden_width)
    return pl.pallas_call(
        functools.partial(serve_kernel, top_count),
        out_shape=(out, out),
        in_specs=[pl.BlockSpec(memory_space=pltpu.SMEM)] + [whole] * 5,
        out_specs=(whole, whole),
        scratch_shapes=[
            pltpu.VMEM((2 * rows, width), jnp.bfloat16),
            pltpu.VMEM((2 * rows, hidden_width), jnp.bfloat16),
        ],
        compiler_params=pltpu.CompilerParams(vmem_limit_bytes=VMEM_MIB * 2**20),
        cost_estimate=pl.CostEstimate(
            flops=12 * rows * width * hidden_width, bytes_accessed=moved, transcendentals=2 * rows * hidden_width
        ),
        name="serve_rows",
    )(mine, own, sib, w_gate, w_up, w_down)


def total(*terms):
    return sum(term.astype(jnp.float32) for term in terms).astype(jnp.bfloat16)


def chunk_steps(own, moves, back, serve, beside):
    rows, packed_width = own.shape
    (held,) = yield (own,)
    for move in moves:
        (got,) = yield (permute(held, move),)
        if move is moves[0] and beside:
            got = lax.optimization_barrier((got, *beside))[0]
        held = jnp.concatenate([held, got])
    (sib,) = yield (permute(held, to_sibling),)
    out, out_sib = serve(held, sib)
    (out_sib,) = yield (out_sib,)
    (got,) = yield (permute(out_sib, to_sibling),)
    left = list(range(len(moves)))[::-1]
    terms = [out.reshape((2,) * len(left) + (rows, -1)), got.reshape((2,) * len(left) + (rows, -1))]
    for number in back:
        at = left.index(number)
        left.remove(number)
        kept, sent = ([lax.index_in_dim(term, k, at, keepdims=False) for term in terms] for k in (0, 1))
        sent = total(*sent).reshape(-1, out.shape[1])
        (got,) = yield (permute(sent, moves[number]),)
        terms = kept + [got.reshape((2,) * len(left) + (rows, -1))]
    return total(*terms)


def run_steps(chunks, guards):
    waits = [[next(chunk)[0]] for chunk in chunks]
    results = [None] * len(chunks)
    while any(result is None for result in results):
        for i, chunk in enumerate(chunks):
            at = len(waits[i]) - 1
            asked = [(j, t) for k, s, j, t in guards if (k, s) == (i, at)]
            if results[i] is not None or any(len(waits[j]) <= t for j, t in asked):
                continue
            ready = tuple(waits[i][-1:])
            if asked:
                ready = lax.optimization_barrier(ready + tuple(waits[j][t] for j, t in asked))[:1]
            try:
                waits[i].append(chunk.send(ready)[0])
            except StopIteration as end:
                results[i] = end.value
    return results


def dense(tokens, expert_ids, route_weight, slot_of, swap_flag, w_gate, w_up, w_down):
    tok_rows = tokens.shape[0]
    top_count = expert_ids.shape[1]
    line_bits = (lax.axis_size("expert") // 2).bit_length() - 1
    along = [along_line(2**bit) for bit in range(line_bits)][::-1]
    across = [over_first, over_second]
    routes = [along + across, along + across, along[:1] + across + along[1:]]
    backs = [[3, 2, 1, 0], [3, 2, 1, 0], [2, 3, 1, 0]] if line_bits == 2 else [range(len(along + across))[::-1]]
    step = ROWS_AT_ONCE if tok_rows % ROWS_AT_ONCE == 0 else tok_rows
    owns = packed(tokens, expert_ids, route_weight, step)
    mine = served_expert(slot_of, lax.optimization_barrier((swap_flag, owns[0]))[0])
    serve = lambda held, sib: serve_rows(held, sib, mine, top_count, w_gate[0], w_up[0], w_down[0])
    chunks = [chunk_steps(own, routes[i % len(routes)], backs[i % len(backs)], serve, (mine,) if i == 1 else ()) for i, own in enumerate(owns)]
    guards = GUARDS if len(chunks) == 3 and line_bits == 2 else []
    return jnp.concatenate(run_steps(chunks, guards))


def on_device(tokens, expert_ids, *rest):
    slot_of = rest[1]
    ex_count = lax.axis_size("expert")
    capacity = 2 * tokens.shape[0] * expert_ids.shape[1] // slot_of.shape[0]
    paired = lax.axis_size("dp") == 4 and ex_count >= 2 and ex_count & (ex_count - 1) == 0
    serve = dense if capacity >= tokens.shape[0] and paired else sparse
    return serve(tokens, expert_ids, *rest)


def solution(mesh):
    return jax.shard_map(
        on_device,
        mesh=mesh,
        in_specs=(
            P(AXES, None),
            P(AXES, None),
            P(AXES, None),
            P(),
            P(AXES),
            P(AXES, None, None),
            P(AXES, None, None),
            P(AXES, None, None),
        ),
        out_specs=P(AXES, None),
        check_vma=False,
    )
```

```python
import functools

import jax
import jax.numpy as jnp
from jax import lax
from jax.experimental import pallas as pl
from jax.experimental.pallas import tpu as pltpu
from jax.sharding import PartitionSpec as P

AXES = ("dp", "expert")
LANES = 128
COLUMNS = 256
VMEM_MIB = 10
ROWS_AT_ONCE = 8
GUARDS = [(2, 6, 0, 7), (1, 5, 2, 4), (1, 4, 0, 6), (1, 7, 0, 5), (0, 9, 2, 8), (0, 10, 2, 9), (0, 8, 2, 8)]


def partner(value, axis, distance):
    mask = 2**distance
    pairs = [(source, source ^ mask) for source in range(lax.axis_size(axis))]
    return lax.ppermute(value, axis, pairs)


def exchange(value):
    return lax.all_to_all(
        lax.all_to_all(value, "dp", split_axis=0, concat_axis=0, tiled=True),
        "expert",
        split_axis=1,
        concat_axis=1,
        tiled=True,
    )


def sparse(tokens, expert_ids, route_weight, slot_of, swap_flag, w_gate, w_up, w_down):
    dp_count = lax.axis_size("dp")
    ex_count = lax.axis_size("expert")
    slot_count = dp_count * ex_count
    tok_rows, model_width = tokens.shape
    top_count = expert_ids.shape[1]
    experts = slot_of.shape[0]
    capacity = 2 * tok_rows * top_count // experts
    moved_shards = partner((w_gate, w_up, w_down), "dp", 0)
    taking = swap_flag[0] == 1
    gate_w = jnp.where(taking, moved_shards[0][0], w_gate[0])
    up_w = jnp.where(taking, moved_shards[1][0], w_up[0])
    down_w = jnp.where(taking, moved_shards[2][0], w_down[0])
    pair_count = tok_rows * top_count
    flat_ids = expert_ids.reshape(pair_count)
    onehot = (flat_ids[:, None] == jnp.arange(experts, dtype=jnp.int32)).astype(jnp.int32)
    order_rank = jnp.sum((jnp.cumsum(onehot, axis=0) - onehot) * onehot, axis=1)
    dest_slot = jnp.sum(onehot[:, :, None] * slot_of[None, :, :], axis=1)
    position = dest_slot * capacity + order_rank[:, None]
    pair_ids = jnp.broadcast_to(jnp.arange(pair_count, dtype=jnp.int32)[:, None], (pair_count, 2))
    owner = (
        jnp.full((slot_count * capacity,), -1, jnp.int32)
        .at[position.reshape(-1)]
        .set(pair_ids.reshape(-1))
    )
    token_row = jnp.maximum(owner, 0) // top_count
    outbox = jnp.where((owner >= 0)[:, None], tokens[token_row], jnp.zeros((), tokens.dtype))
    outbox = outbox.reshape(dp_count, ex_count, capacity, model_width)
    arrived = exchange(outbox).reshape(slot_count * capacity, model_width)
    gate_sum = jnp.dot(arrived, gate_w, preferred_element_type=jnp.float32)
    up_sum = jnp.dot(arrived, up_w, preferred_element_type=jnp.float32)
    hidden = (jax.nn.silu(gate_sum) * up_sum).astype(jnp.bfloat16)
    partial_out = jnp.dot(hidden, down_w, preferred_element_type=jnp.float32).astype(jnp.bfloat16)
    partial_out = partial_out.reshape(dp_count, ex_count, capacity, model_width)
    returned = exchange(partial_out).reshape(slot_count * capacity, model_width)
    picked = returned[position].astype(jnp.float32)
    scaled = jnp.sum(picked, axis=1) * route_weight.reshape(pair_count)[:, None]
    return jnp.sum(scaled.reshape(tok_rows, top_count, model_width), axis=1).astype(jnp.bfloat16)


def permute(value, move):
    ex_count = lax.axis_size("expert")
    pairs = []
    for source in range(lax.axis_size("dp") * ex_count):
        d, e = move(*divmod(source, ex_count))
        pairs.append((source, d * ex_count + e))
    return lax.ppermute(value, AXES, pairs)


def to_sibling(d, e):
    return d ^ 1, e


def over_first(d, e):
    return (d ^ 2, e) if d % 2 else (d, e ^ 1)


def over_second(d, e):
    return (d, e ^ 1) if d % 2 else (d ^ 2, e)


def along_line(distance):
    return lambda d, e: (d, e ^ (2 * distance))


def expert_kernel(slots, flag, mine):
    d = lax.axis_index("dp")
    serving = jnp.where(flag[0] == 1, d ^ 1, d) * lax.axis_size("expert") + lax.axis_index("expert")
    expert = jnp.int32(0)
    for half in range(slots.shape[0]):
        for number in range(slots.shape[1]):
            expert += jnp.where(slots[half, number] == serving, number, 0)
    mine[0] = expert


def served_expert(slot_of, swap_flag):
    scalars = pl.BlockSpec(memory_space=pltpu.SMEM)
    return pl.pallas_call(
        expert_kernel,
        out_shape=jax.ShapeDtypeStruct((1,), jnp.int32),
        in_specs=[scalars] * 2,
        out_specs=scalars,
        compiler_params=pltpu.CompilerParams(vmem_limit_bytes=2**20),
        cost_estimate=pl.CostEstimate(flops=10**10, bytes_accessed=0, transcendentals=0),
        name="served_expert",
    )(*in_hbm(slot_of.T), swap_flag)


def pack_kernel(tokens_hbm, ids_hbm, weights_hbm, *outs_and_scratch):
    *outs, square, tokens, ids, weights, sems = outs_and_scratch
    loads = [
        pltpu.make_async_copy(source, target, sems.at[k])
        for k, (source, target) in enumerate(((ids_hbm, ids), (weights_hbm, weights), (tokens_hbm, tokens)))
    ]
    for load in loads:
        load.start()
    top_count, tok_rows = ids.shape
    square[...] = jnp.zeros_like(square)
    loads[0].wait()
    loads[1].wait()
    square[:top_count, :tok_rows] = ids[...].astype(jnp.float32)
    rest = weights[...]
    for k in range(1, 4):
        part = rest.astype(jnp.bfloat16).astype(jnp.float32)
        square[k * top_count : (k + 1) * top_count, :tok_rows] = part
        rest = rest - part
    extra = square[...].T.astype(jnp.bfloat16)
    loads[2].wait()
    at = 0
    for out in outs:
        rows, packed_width = out.shape
        out[...] = jnp.concatenate([tokens[at : at + rows], extra[at : at + rows]], axis=1)
        at += rows


def in_hbm(*arrays):
    return [pltpu.with_memory_space_constraint(array, pltpu.HBM) for array in arrays]


def packed(tokens, expert_ids, route_weight, rows):
    tok_rows, width = tokens.shape
    side = -(-max(tok_rows, 4 * expert_ids.shape[1]) // LANES) * LANES
    whole = pl.BlockSpec(memory_space=pltpu.VMEM)
    count = tok_rows // rows
    return pl.pallas_call(
        pack_kernel,
        out_shape=(pltpu.VMEM((rows, width + side), tokens.dtype),) * count,
        in_specs=[pl.BlockSpec(memory_space=pl.ANY)] * 3,
        out_specs=(whole,) * count,
        scratch_shapes=[
            pltpu.VMEM((side, side), jnp.float32),
            pltpu.VMEM(tokens.shape, tokens.dtype),
            pltpu.VMEM(expert_ids.shape[::-1], expert_ids.dtype),
            pltpu.VMEM(route_weight.shape[::-1], route_weight.dtype),
            pltpu.SemaphoreType.DMA((3,)),
        ],
        compiler_params=pltpu.CompilerParams(vmem_limit_bytes=VMEM_MIB * 2**20),
        cost_estimate=pl.CostEstimate(flops=0, bytes_accessed=4 * tok_rows * width, transcendentals=0),
        name="pack_rows",
    )(*in_hbm(tokens, expert_ids.T, route_weight.T))


def scale_of(extra, mine, top_count):
    extra = extra.astype(jnp.float32)
    ids, hi, mid, lo = (extra[:, k * top_count : (k + 1) * top_count] for k in range(4))
    return jnp.sum(jnp.where(ids == mine, hi + mid + lo, 0.0), axis=1, keepdims=True)


def serve_kernel(top_count, mine, own, sib, w_gate, w_up, w_down, out_own, out_sib, x, hidden):
    rows = own.shape[0]
    width, hidden_width = w_gate.shape
    x[:rows] = own[:, :width]
    x[rows:] = sib[:, :width]
    for at in range(0, hidden_width, COLUMNS):
        part = pl.ds(at, COLUMNS)
        gate_sum = jnp.dot(x[...], w_gate[:, part], preferred_element_type=jnp.float32)
        up_sum = jnp.dot(x[...], w_up[:, part], preferred_element_type=jnp.float32)
        hidden[:, part] = (gate_sum / (1.0 + jnp.exp(-gate_sum)) * up_sum).astype(jnp.bfloat16)
    extra = jnp.concatenate([own[:, width:], sib[:, width:]])
    scale = scale_of(extra, mine[0].astype(jnp.float32), top_count)
    for at in range(0, width, COLUMNS):
        part = pl.ds(at, COLUMNS)
        served = jnp.dot(hidden[...], w_down[:, part], preferred_element_type=jnp.float32) * scale
        out_own[:, part] = served[:rows].astype(jnp.bfloat16)
        out_sib[:, part] = served[rows:].astype(jnp.bfloat16)


def serve_rows(own, sib, mine, top_count, w_gate, w_up, w_down):
    rows, packed_width = own.shape
    width, hidden_width = w_gate.shape
    whole = pl.BlockSpec(memory_space=pltpu.VMEM)
    out = jax.ShapeDtypeStruct((rows, width), jnp.bfloat16)
    moved = 2 * (4 * rows * width + 3 * width * hidden_width)
    return pl.pallas_call(
        functools.partial(serve_kernel, top_count),
        out_shape=(out, out),
        in_specs=[pl.BlockSpec(memory_space=pltpu.SMEM)] + [whole] * 5,
        out_specs=(whole, whole),
        scratch_shapes=[
            pltpu.VMEM((2 * rows, width), jnp.bfloat16),
            pltpu.VMEM((2 * rows, hidden_width), jnp.bfloat16),
        ],
        compiler_params=pltpu.CompilerParams(vmem_limit_bytes=VMEM_MIB * 2**20),
        cost_estimate=pl.CostEstimate(
            flops=12 * rows * width * hidden_width, bytes_accessed=moved, transcendentals=2 * rows * hidden_width
        ),
        name="serve_rows",
    )(mine, own, sib, w_gate, w_up, w_down)


def total(*terms):
    return sum(term.astype(jnp.float32) for term in terms).astype(jnp.bfloat16)


def chunk_steps(own, moves, back, serve, beside):
    rows, packed_width = own.shape
    (held,) = yield (own,)
    for move in moves:
        (got,) = yield (permute(held, move),)
        if move is moves[2] and beside:
            got = lax.optimization_barrier((got, *beside))[0]
        held = jnp.concatenate([held, got])
    (sib,) = yield (permute(held, to_sibling),)
    out, out_sib = serve(held, sib)
    (out_sib,) = yield (out_sib,)
    (got,) = yield (permute(out_sib, to_sibling),)
    left = list(range(len(moves)))[::-1]
    terms = [out.reshape((2,) * len(left) + (rows, -1)), got.reshape((2,) * len(left) + (rows, -1))]
    for number in back:
        at = left.index(number)
        left.remove(number)
        kept, sent = ([lax.index_in_dim(term, k, at, keepdims=False) for term in terms] for k in (0, 1))
        sent = total(*sent).reshape(-1, out.shape[1])
        (got,) = yield (permute(sent, moves[number]),)
        terms = kept + [got.reshape((2,) * len(left) + (rows, -1))]
    return total(*terms)


def run_steps(chunks, guards):
    waits = [[next(chunk)[0]] for chunk in chunks]
    results = [None] * len(chunks)
    while any(result is None for result in results):
        for i, chunk in enumerate(chunks):
            at = len(waits[i]) - 1
            asked = [(j, t) for k, s, j, t in guards if (k, s) == (i, at)]
            if results[i] is not None or any(len(waits[j]) <= t for j, t in asked):
                continue
            ready = tuple(waits[i][-1:])
            if asked:
                ready = lax.optimization_barrier(ready + tuple(waits[j][t] for j, t in asked))[:1]
            try:
                waits[i].append(chunk.send(ready)[0])
            except StopIteration as end:
                results[i] = end.value
    return results


def dense(tokens, expert_ids, route_weight, slot_of, swap_flag, w_gate, w_up, w_down):
    tok_rows = tokens.shape[0]
    top_count = expert_ids.shape[1]
    line_bits = (lax.axis_size("expert") // 2).bit_length() - 1
    along = [along_line(2**bit) for bit in range(line_bits)][::-1]
    across = [over_first, over_second]
    routes = [along + across, along + across, along[:1] + across + along[1:]]
    backs = [[3, 2, 1, 0], [3, 2, 1, 0], [2, 1, 3, 0]] if line_bits == 2 else [range(len(along + across))[::-1]]
    step = ROWS_AT_ONCE if tok_rows % ROWS_AT_ONCE == 0 else tok_rows
    owns = packed(tokens, expert_ids, route_weight, step)
    mine = served_expert(slot_of, lax.optimization_barrier((swap_flag, owns[0]))[0])
    serve = lambda held, sib: serve_rows(held, sib, mine, top_count, w_gate[0], w_up[0], w_down[0])
    chunks = [chunk_steps(own, routes[i % len(routes)], backs[i % len(backs)], serve, (mine,) if i == 1 else ()) for i, own in enumerate(owns)]
    guards = GUARDS if len(chunks) == 3 and line_bits == 2 else []
    return jnp.concatenate(run_steps(chunks, guards))


def on_device(tokens, expert_ids, *rest):
    slot_of = rest[1]
    ex_count = lax.axis_size("expert")
    capacity = 2 * tokens.shape[0] * expert_ids.shape[1] // slot_of.shape[0]
    paired = lax.axis_size("dp") == 4 and ex_count >= 2 and ex_count & (ex_count - 1) == 0
    serve = dense if capacity >= tokens.shape[0] and paired else sparse
    return serve(tokens, expert_ids, *rest)


def solution(mesh):
    return jax.shard_map(
        on_device,
        mesh=mesh,
        in_specs=(
            P(AXES, None),
            P(AXES, None),
            P(AXES, None),
            P(),
            P(AXES),
            P(AXES, None, None),
            P(AXES, None, None),
            P(AXES, None, None),
        ),
        out_specs=P(AXES, None),
        check_vma=False,
    )
```

```python
import functools

import jax
import jax.numpy as jnp
from jax import lax
from jax.experimental import pallas as pl
from jax.experimental.pallas import tpu as pltpu
from jax.sharding import PartitionSpec as P

AXES = ("dp", "expert")
LANES = 128
COLUMNS = 256
VMEM_MIB = 10
ROWS_AT_ONCE = 8
GUARDS = [(2, 6, 0, 7), (1, 5, 2, 4), (1, 4, 0, 6), (1, 7, 0, 5), (0, 9, 2, 8), (0, 10, 2, 9), (0, 8, 2, 8)]


def partner(value, axis, distance):
    mask = 2**distance
    pairs = [(source, source ^ mask) for source in range(lax.axis_size(axis))]
    return lax.ppermute(value, axis, pairs)


def exchange(value):
    return lax.all_to_all(
        lax.all_to_all(value, "dp", split_axis=0, concat_axis=0, tiled=True),
        "expert",
        split_axis=1,
        concat_axis=1,
        tiled=True,
    )


def sparse(tokens, expert_ids, route_weight, slot_of, swap_flag, w_gate, w_up, w_down):
    dp_count = lax.axis_size("dp")
    ex_count = lax.axis_size("expert")
    slot_count = dp_count * ex_count
    tok_rows, model_width = tokens.shape
    top_count = expert_ids.shape[1]
    experts = slot_of.shape[0]
    capacity = 2 * tok_rows * top_count // experts
    moved_shards = partner((w_gate, w_up, w_down), "dp", 0)
    taking = swap_flag[0] == 1
    gate_w = jnp.where(taking, moved_shards[0][0], w_gate[0])
    up_w = jnp.where(taking, moved_shards[1][0], w_up[0])
    down_w = jnp.where(taking, moved_shards[2][0], w_down[0])
    pair_count = tok_rows * top_count
    flat_ids = expert_ids.reshape(pair_count)
    onehot = (flat_ids[:, None] == jnp.arange(experts, dtype=jnp.int32)).astype(jnp.int32)
    order_rank = jnp.sum((jnp.cumsum(onehot, axis=0) - onehot) * onehot, axis=1)
    dest_slot = jnp.sum(onehot[:, :, None] * slot_of[None, :, :], axis=1)
    position = dest_slot * capacity + order_rank[:, None]
    pair_ids = jnp.broadcast_to(jnp.arange(pair_count, dtype=jnp.int32)[:, None], (pair_count, 2))
    owner = (
        jnp.full((slot_count * capacity,), -1, jnp.int32)
        .at[position.reshape(-1)]
        .set(pair_ids.reshape(-1))
    )
    token_row = jnp.maximum(owner, 0) // top_count
    outbox = jnp.where((owner >= 0)[:, None], tokens[token_row], jnp.zeros((), tokens.dtype))
    outbox = outbox.reshape(dp_count, ex_count, capacity, model_width)
    arrived = exchange(outbox).reshape(slot_count * capacity, model_width)
    gate_sum = jnp.dot(arrived, gate_w, preferred_element_type=jnp.float32)
    up_sum = jnp.dot(arrived, up_w, preferred_element_type=jnp.float32)
    hidden = (jax.nn.silu(gate_sum) * up_sum).astype(jnp.bfloat16)
    partial_out = jnp.dot(hidden, down_w, preferred_element_type=jnp.float32).astype(jnp.bfloat16)
    partial_out = partial_out.reshape(dp_count, ex_count, capacity, model_width)
    returned = exchange(partial_out).reshape(slot_count * capacity, model_width)
    picked = returned[position].astype(jnp.float32)
    scaled = jnp.sum(picked, axis=1) * route_weight.reshape(pair_count)[:, None]
    return jnp.sum(scaled.reshape(tok_rows, top_count, model_width), axis=1).astype(jnp.bfloat16)


def permute(value, move):
    ex_count = lax.axis_size("expert")
    pairs = []
    for source in range(lax.axis_size("dp") * ex_count):
        d, e = move(*divmod(source, ex_count))
        pairs.append((source, d * ex_count + e))
    return lax.ppermute(value, AXES, pairs)


def to_sibling(d, e):
    return d ^ 1, e


def over_first(d, e):
    return (d ^ 2, e) if d % 2 else (d, e ^ 1)


def over_second(d, e):
    return (d, e ^ 1) if d % 2 else (d ^ 2, e)


def along_line(distance):
    return lambda d, e: (d, e ^ (2 * distance))


def expert_kernel(slots, flag, after, mine):
    d = lax.axis_index("dp")
    serving = jnp.where(flag[0] == 1, d ^ 1, d) * lax.axis_size("expert") + lax.axis_index("expert")
    expert = jnp.int32(0)
    for half in range(slots.shape[0]):
        for number in range(slots.shape[1]):
            expert += jnp.where(slots[half, number] == serving, number, 0)
    mine[0] = expert


def served_expert(slot_of, swap_flag, after):
    scalars = pl.BlockSpec(memory_space=pltpu.SMEM)
    return pl.pallas_call(
        expert_kernel,
        out_shape=jax.ShapeDtypeStruct((1,), jnp.int32),
        in_specs=[scalars] * 2 + [pl.BlockSpec(memory_space=pl.ANY)],
        out_specs=scalars,
        compiler_params=pltpu.CompilerParams(vmem_limit_bytes=2**20),
        cost_estimate=pl.CostEstimate(flops=10**10, bytes_accessed=0, transcendentals=0),
        name="served_expert",
    )(*in_hbm(slot_of.T), swap_flag, after)


def pack_kernel(tokens_hbm, ids_hbm, weights_hbm, *outs_and_scratch):
    *outs, square, tokens, ids, weights, sems = outs_and_scratch
    loads = [
        pltpu.make_async_copy(source, target, sems.at[k])
        for k, (source, target) in enumerate(((ids_hbm, ids), (weights_hbm, weights), (tokens_hbm, tokens)))
    ]
    for load in loads:
        load.start()
    top_count, tok_rows = ids.shape
    square[...] = jnp.zeros_like(square)
    loads[0].wait()
    loads[1].wait()
    square[:top_count, :tok_rows] = ids[...].astype(jnp.float32)
    rest = weights[...]
    for k in range(1, 4):
        part = rest.astype(jnp.bfloat16).astype(jnp.float32)
        square[k * top_count : (k + 1) * top_count, :tok_rows] = part
        rest = rest - part
    extra = square[...].T.astype(jnp.bfloat16)
    loads[2].wait()
    at = 0
    for out in outs:
        rows, packed_width = out.shape
        out[...] = jnp.concatenate([tokens[at : at + rows], extra[at : at + rows]], axis=1)
        at += rows


def in_hbm(*arrays):
    return [pltpu.with_memory_space_constraint(array, pltpu.HBM) for array in arrays]


def packed(tokens, expert_ids, route_weight, rows):
    tok_rows, width = tokens.shape
    side = -(-max(tok_rows, 4 * expert_ids.shape[1]) // LANES) * LANES
    whole = pl.BlockSpec(memory_space=pltpu.VMEM)
    count = tok_rows // rows
    return pl.pallas_call(
        pack_kernel,
        out_shape=(pltpu.VMEM((rows, width + side), tokens.dtype),) * count,
        in_specs=[pl.BlockSpec(memory_space=pl.ANY)] * 3,
        out_specs=(whole,) * count,
        scratch_shapes=[
            pltpu.VMEM((side, side), jnp.float32),
            pltpu.VMEM(tokens.shape, tokens.dtype),
            pltpu.VMEM(expert_ids.shape[::-1], expert_ids.dtype),
            pltpu.VMEM(route_weight.shape[::-1], route_weight.dtype),
            pltpu.SemaphoreType.DMA((3,)),
        ],
        compiler_params=pltpu.CompilerParams(vmem_limit_bytes=VMEM_MIB * 2**20),
        cost_estimate=pl.CostEstimate(flops=0, bytes_accessed=4 * tok_rows * width, transcendentals=0),
        name="pack_rows",
    )(*in_hbm(tokens, expert_ids.T, route_weight.T))


def scale_of(extra, mine, top_count):
    extra = extra.astype(jnp.float32)
    ids, hi, mid, lo = (extra[:, k * top_count : (k + 1) * top_count] for k in range(4))
    return jnp.sum(jnp.where(ids == mine, hi + mid + lo, 0.0), axis=1, keepdims=True)


def serve_kernel(top_count, mine, own, sib, w_gate, w_up, w_down, out_own, out_sib, x, hidden):
    rows = own.shape[0]
    width, hidden_width = w_gate.shape
    x[:rows] = own[:, :width]
    x[rows:] = sib[:, :width]
    for at in range(0, hidden_width, COLUMNS):
        part = pl.ds(at, COLUMNS)
        gate_sum = jnp.dot(x[...], w_gate[:, part], preferred_element_type=jnp.float32)
        up_sum = jnp.dot(x[...], w_up[:, part], preferred_element_type=jnp.float32)
        hidden[:, part] = (gate_sum / (1.0 + jnp.exp(-gate_sum)) * up_sum).astype(jnp.bfloat16)
    extra = jnp.concatenate([own[:, width:], sib[:, width:]])
    scale = scale_of(extra, mine[0].astype(jnp.float32), top_count)
    for at in range(0, width, COLUMNS):
        part = pl.ds(at, COLUMNS)
        served = jnp.dot(hidden[...], w_down[:, part], preferred_element_type=jnp.float32) * scale
        out_own[:, part] = served[:rows].astype(jnp.bfloat16)
        out_sib[:, part] = served[rows:].astype(jnp.bfloat16)


def serve_rows(own, sib, mine, top_count, w_gate, w_up, w_down):
    rows, packed_width = own.shape
    width, hidden_width = w_gate.shape
    whole = pl.BlockSpec(memory_space=pltpu.VMEM)
    out = jax.ShapeDtypeStruct((rows, width), jnp.bfloat16)
    moved = 2 * (4 * rows * width + 3 * width * hidden_width)
    return pl.pallas_call(
        functools.partial(serve_kernel, top_count),
        out_shape=(out, out),
        in_specs=[pl.BlockSpec(memory_space=pltpu.SMEM)] + [whole] * 5,
        out_specs=(whole, whole),
        scratch_shapes=[
            pltpu.VMEM((2 * rows, width), jnp.bfloat16),
            pltpu.VMEM((2 * rows, hidden_width), jnp.bfloat16),
        ],
        compiler_params=pltpu.CompilerParams(vmem_limit_bytes=VMEM_MIB * 2**20),
        cost_estimate=pl.CostEstimate(
            flops=12 * rows * width * hidden_width, bytes_accessed=moved, transcendentals=2 * rows * hidden_width
        ),
        name="serve_rows",
    )(mine, own, sib, w_gate, w_up, w_down)


def total(*terms):
    return sum(term.astype(jnp.float32) for term in terms).astype(jnp.bfloat16)


def chunk_steps(own, moves, back, serve, beside):
    rows, packed_width = own.shape
    (held,) = yield (own,)
    for move in moves:
        (got,) = yield (permute(held, move),)
        if move is moves[2] and beside:
            got = lax.optimization_barrier((got, beside(before)))[0]
        before = got
        held = jnp.concatenate([held, got])
    (sib,) = yield (permute(held, to_sibling),)
    out, out_sib = serve(held, sib)
    (out_sib,) = yield (out_sib,)
    (got,) = yield (permute(out_sib, to_sibling),)
    left = list(range(len(moves)))[::-1]
    terms = [out.reshape((2,) * len(left) + (rows, -1)), got.reshape((2,) * len(left) + (rows, -1))]
    for number in back:
        at = left.index(number)
        left.remove(number)
        kept, sent = ([lax.index_in_dim(term, k, at, keepdims=False) for term in terms] for k in (0, 1))
        sent = total(*sent).reshape(-1, out.shape[1])
        (got,) = yield (permute(sent, moves[number]),)
        terms = kept + [got.reshape((2,) * len(left) + (rows, -1))]
    return total(*terms)


def run_steps(chunks, guards):
    waits = [[next(chunk)[0]] for chunk in chunks]
    results = [None] * len(chunks)
    while any(result is None for result in results):
        for i, chunk in enumerate(chunks):
            at = len(waits[i]) - 1
            asked = [(j, t) for k, s, j, t in guards if (k, s) == (i, at)]
            if results[i] is not None or any(len(waits[j]) <= t for j, t in asked):
                continue
            ready = tuple(waits[i][-1:])
            if asked:
                ready = lax.optimization_barrier(ready + tuple(waits[j][t] for j, t in asked))[:1]
            try:
                waits[i].append(chunk.send(ready)[0])
            except StopIteration as end:
                results[i] = end.value
    return results


def dense(tokens, expert_ids, route_weight, slot_of, swap_flag, w_gate, w_up, w_down):
    tok_rows = tokens.shape[0]
    top_count = expert_ids.shape[1]
    line_bits = (lax.axis_size("expert") // 2).bit_length() - 1
    along = [along_line(2**bit) for bit in range(line_bits)][::-1]
    across = [over_first, over_second]
    routes = [along + across, along + across, along[:1] + across + along[1:]]
    backs = [[3, 2, 1, 0], [3, 2, 1, 0], [2, 3, 1, 0]] if line_bits == 2 else [range(len(along + across))[::-1]]
    step = ROWS_AT_ONCE if tok_rows % ROWS_AT_ONCE == 0 else tok_rows
    owns = packed(tokens, expert_ids, route_weight, step)
    found = []

    def find(after):
        found.append(served_expert(slot_of, swap_flag, after))
        return found[0]

    serve = lambda held, sib: serve_rows(held, sib, found[0], top_count, w_gate[0], w_up[0], w_down[0])
    chunks = [
        chunk_steps(own, routes[i % len(routes)], backs[i % len(backs)], serve, find if i == 0 else None)
        for i, own in enumerate(owns)
    ]
    guards = GUARDS if len(chunks) == 3 and line_bits == 2 else []
    return jnp.concatenate(run_steps(chunks, guards))


def on_device(tokens, expert_ids, *rest):
    slot_of = rest[1]
    ex_count = lax.axis_size("expert")
    capacity = 2 * tokens.shape[0] * expert_ids.shape[1] // slot_of.shape[0]
    paired = lax.axis_size("dp") == 4 and ex_count >= 2 and ex_count & (ex_count - 1) == 0
    serve = dense if capacity >= tokens.shape[0] and paired else sparse
    return serve(tokens, expert_ids, *rest)


def solution(mesh):
    return jax.shard_map(
        on_device,
        mesh=mesh,
        in_specs=(
            P(AXES, None),
            P(AXES, None),
            P(AXES, None),
            P(),
            P(AXES),
            P(AXES, None, None),
            P(AXES, None, None),
            P(AXES, None, None),
        ),
        out_specs=P(AXES, None),
        check_vma=False,
    )
```

```python
import functools

import jax
import jax.numpy as jnp
from jax import lax
from jax.experimental import pallas as pl
from jax.experimental.pallas import tpu as pltpu
from jax.sharding import PartitionSpec as P

AXES = ("dp", "expert")
LANES = 128
COLUMNS = 256
VMEM_MIB = 10
ROWS_AT_ONCE = 8
GUARDS = [(2, 6, 0, 7), (1, 5, 2, 4), (1, 4, 0, 6), (1, 7, 0, 5), (0, 9, 2, 8), (0, 10, 2, 9), (0, 8, 2, 8)]


def partner(value, axis, distance):
    mask = 2**distance
    pairs = [(source, source ^ mask) for source in range(lax.axis_size(axis))]
    return lax.ppermute(value, axis, pairs)


def exchange(value):
    return lax.all_to_all(
        lax.all_to_all(value, "dp", split_axis=0, concat_axis=0, tiled=True),
        "expert",
        split_axis=1,
        concat_axis=1,
        tiled=True,
    )


def sparse(tokens, expert_ids, route_weight, slot_of, swap_flag, w_gate, w_up, w_down):
    dp_count = lax.axis_size("dp")
    ex_count = lax.axis_size("expert")
    slot_count = dp_count * ex_count
    tok_rows, model_width = tokens.shape
    top_count = expert_ids.shape[1]
    experts = slot_of.shape[0]
    capacity = 2 * tok_rows * top_count // experts
    moved_shards = partner((w_gate, w_up, w_down), "dp", 0)
    taking = swap_flag[0] == 1
    gate_w = jnp.where(taking, moved_shards[0][0], w_gate[0])
    up_w = jnp.where(taking, moved_shards[1][0], w_up[0])
    down_w = jnp.where(taking, moved_shards[2][0], w_down[0])
    pair_count = tok_rows * top_count
    flat_ids = expert_ids.reshape(pair_count)
    onehot = (flat_ids[:, None] == jnp.arange(experts, dtype=jnp.int32)).astype(jnp.int32)
    order_rank = jnp.sum((jnp.cumsum(onehot, axis=0) - onehot) * onehot, axis=1)
    dest_slot = jnp.sum(onehot[:, :, None] * slot_of[None, :, :], axis=1)
    position = dest_slot * capacity + order_rank[:, None]
    pair_ids = jnp.broadcast_to(jnp.arange(pair_count, dtype=jnp.int32)[:, None], (pair_count, 2))
    owner = (
        jnp.full((slot_count * capacity,), -1, jnp.int32)
        .at[position.reshape(-1)]
        .set(pair_ids.reshape(-1))
    )
    token_row = jnp.maximum(owner, 0) // top_count
    outbox = jnp.where((owner >= 0)[:, None], tokens[token_row], jnp.zeros((), tokens.dtype))
    outbox = outbox.reshape(dp_count, ex_count, capacity, model_width)
    arrived = exchange(outbox).reshape(slot_count * capacity, model_width)
    gate_sum = jnp.dot(arrived, gate_w, preferred_element_type=jnp.float32)
    up_sum = jnp.dot(arrived, up_w, preferred_element_type=jnp.float32)
    hidden = (jax.nn.silu(gate_sum) * up_sum).astype(jnp.bfloat16)
    partial_out = jnp.dot(hidden, down_w, preferred_element_type=jnp.float32).astype(jnp.bfloat16)
    partial_out = partial_out.reshape(dp_count, ex_count, capacity, model_width)
    returned = exchange(partial_out).reshape(slot_count * capacity, model_width)
    picked = returned[position].astype(jnp.float32)
    scaled = jnp.sum(picked, axis=1) * route_weight.reshape(pair_count)[:, None]
    return jnp.sum(scaled.reshape(tok_rows, top_count, model_width), axis=1).astype(jnp.bfloat16)


def permute(value, move):
    ex_count = lax.axis_size("expert")
    pairs = []
    for source in range(lax.axis_size("dp") * ex_count):
        d, e = move(*divmod(source, ex_count))
        pairs.append((source, d * ex_count + e))
    return lax.ppermute(value, AXES, pairs)


def to_sibling(d, e):
    return d ^ 1, e


def over_first(d, e):
    return (d ^ 2, e) if d % 2 else (d, e ^ 1)


def over_second(d, e):
    return (d, e ^ 1) if d % 2 else (d ^ 2, e)


def along_line(distance):
    return lambda d, e: (d, e ^ (2 * distance))


def expert_kernel(slots, flag, after, mine):
    d = lax.axis_index("dp")
    serving = jnp.where(flag[0] == 1, d ^ 1, d) * lax.axis_size("expert") + lax.axis_index("expert")
    expert = jnp.int32(0)
    for half in range(slots.shape[0]):
        for number in range(slots.shape[1]):
            expert += jnp.where(slots[half, number] == serving, number, 0)
    mine[0] = expert


def served_expert(slot_of, swap_flag, after):
    scalars = pl.BlockSpec(memory_space=pltpu.SMEM)
    return pl.pallas_call(
        expert_kernel,
        out_shape=jax.ShapeDtypeStruct((1,), jnp.int32),
        in_specs=[scalars] * 2 + [pl.BlockSpec(memory_space=pl.ANY)],
        out_specs=scalars,
        compiler_params=pltpu.CompilerParams(vmem_limit_bytes=2**20),
        cost_estimate=pl.CostEstimate(flops=10**10, bytes_accessed=0, transcendentals=0),
        name="served_expert",
    )(*in_hbm(slot_of.T), swap_flag, after)


def pack_kernel(tokens_hbm, ids_hbm, weights_hbm, *outs_and_scratch):
    *outs, square, tokens, ids, weights, sems = outs_and_scratch
    loads = [
        pltpu.make_async_copy(source, target, sems.at[k])
        for k, (source, target) in enumerate(((ids_hbm, ids), (weights_hbm, weights), (tokens_hbm, tokens)))
    ]
    for load in loads:
        load.start()
    top_count, tok_rows = ids.shape
    square[...] = jnp.zeros_like(square)
    loads[0].wait()
    loads[1].wait()
    square[:top_count, :tok_rows] = ids[...].astype(jnp.float32)
    rest = weights[...]
    for k in range(1, 4):
        part = rest.astype(jnp.bfloat16).astype(jnp.float32)
        square[k * top_count : (k + 1) * top_count, :tok_rows] = part
        rest = rest - part
    extra = square[...].T.astype(jnp.bfloat16)
    loads[2].wait()
    at = 0
    for out in outs:
        rows, packed_width = out.shape
        out[...] = jnp.concatenate([tokens[at : at + rows], extra[at : at + rows]], axis=1)
        at += rows


def in_hbm(*arrays):
    return [pltpu.with_memory_space_constraint(array, pltpu.HBM) for array in arrays]


def packed(tokens, expert_ids, route_weight, rows):
    tok_rows, width = tokens.shape
    side = -(-max(tok_rows, 4 * expert_ids.shape[1]) // LANES) * LANES
    whole = pl.BlockSpec(memory_space=pltpu.VMEM)
    count = tok_rows // rows
    return pl.pallas_call(
        pack_kernel,
        out_shape=(pltpu.VMEM((rows, width + side), tokens.dtype),) * count,
        in_specs=[pl.BlockSpec(memory_space=pl.ANY)] * 3,
        out_specs=(whole,) * count,
        scratch_shapes=[
            pltpu.VMEM((side, side), jnp.float32),
            pltpu.VMEM(tokens.shape, tokens.dtype),
            pltpu.VMEM(expert_ids.shape[::-1], expert_ids.dtype),
            pltpu.VMEM(route_weight.shape[::-1], route_weight.dtype),
            pltpu.SemaphoreType.DMA((3,)),
        ],
        compiler_params=pltpu.CompilerParams(vmem_limit_bytes=VMEM_MIB * 2**20),
        cost_estimate=pl.CostEstimate(flops=0, bytes_accessed=4 * tok_rows * width, transcendentals=0),
        name="pack_rows",
    )(*in_hbm(tokens, expert_ids.T, route_weight.T))


def scale_of(extra, mine, top_count):
    extra = extra.astype(jnp.float32)
    ids, hi, mid, lo = (extra[:, k * top_count : (k + 1) * top_count] for k in range(4))
    return jnp.sum(jnp.where(ids == mine, hi + mid + lo, 0.0), axis=1, keepdims=True)


def serve_kernel(top_count, mine, own, sib, w_gate, w_up, w_down, out_own, out_sib, x, hidden):
    rows = own.shape[0]
    width, hidden_width = w_gate.shape
    x[:rows] = own[:, :width]
    x[rows:] = sib[:, :width]
    for at in range(0, hidden_width, COLUMNS):
        part = pl.ds(at, COLUMNS)
        gate_sum = jnp.dot(x[...], w_gate[:, part], preferred_element_type=jnp.float32)
        up_sum = jnp.dot(x[...], w_up[:, part], preferred_element_type=jnp.float32)
        hidden[:, part] = (gate_sum / (1.0 + jnp.exp(-gate_sum)) * up_sum).astype(jnp.bfloat16)
    extra = jnp.concatenate([own[:, width:], sib[:, width:]])
    scale = scale_of(extra, mine[0].astype(jnp.float32), top_count)
    for at in range(0, width, COLUMNS):
        part = pl.ds(at, COLUMNS)
        served = jnp.dot(hidden[...], w_down[:, part], preferred_element_type=jnp.float32) * scale
        out_own[:, part] = served[:rows].astype(jnp.bfloat16)
        out_sib[:, part] = served[rows:].astype(jnp.bfloat16)


def serve_rows(own, sib, mine, top_count, w_gate, w_up, w_down):
    rows, packed_width = own.shape
    width, hidden_width = w_gate.shape
    whole = pl.BlockSpec(memory_space=pltpu.VMEM)
    out = jax.ShapeDtypeStruct((rows, width), jnp.bfloat16)
    moved = 2 * (4 * rows * width + 3 * width * hidden_width)
    return pl.pallas_call(
        functools.partial(serve_kernel, top_count),
        out_shape=(out, out),
        in_specs=[pl.BlockSpec(memory_space=pltpu.SMEM)] + [whole] * 5,
        out_specs=(whole, whole),
        scratch_shapes=[
            pltpu.VMEM((2 * rows, width), jnp.bfloat16),
            pltpu.VMEM((2 * rows, hidden_width), jnp.bfloat16),
        ],
        compiler_params=pltpu.CompilerParams(vmem_limit_bytes=VMEM_MIB * 2**20),
        cost_estimate=pl.CostEstimate(
            flops=12 * rows * width * hidden_width, bytes_accessed=moved, transcendentals=2 * rows * hidden_width
        ),
        name="serve_rows",
    )(mine, own, sib, w_gate, w_up, w_down)


def total(*terms):
    return sum(term.astype(jnp.float32) for term in terms).astype(jnp.bfloat16)


def chunk_steps(own, moves, back, serve, beside):
    rows, packed_width = own.shape
    (held,) = yield (own,)
    for move in moves:
        (got,) = yield (permute(held, move),)
        if move is moves[3] and beside:
            got = lax.optimization_barrier((got, beside(before)))[0]
        before = got
        held = jnp.concatenate([held, got])
    (sib,) = yield (permute(held, to_sibling),)
    out, out_sib = serve(held, sib)
    (out_sib,) = yield (out_sib,)
    (got,) = yield (permute(out_sib, to_sibling),)
    left = list(range(len(moves)))[::-1]
    terms = [out.reshape((2,) * len(left) + (rows, -1)), got.reshape((2,) * len(left) + (rows, -1))]
    for number in back:
        at = left.index(number)
        left.remove(number)
        kept, sent = ([lax.index_in_dim(term, k, at, keepdims=False) for term in terms] for k in (0, 1))
        sent = total(*sent).reshape(-1, out.shape[1])
        (got,) = yield (permute(sent, moves[number]),)
        terms = kept + [got.reshape((2,) * len(left) + (rows, -1))]
    return total(*terms)


def run_steps(chunks, guards):
    waits = [[next(chunk)[0]] for chunk in chunks]
    results = [None] * len(chunks)
    while any(result is None for result in results):
        for i, chunk in enumerate(chunks):
            at = len(waits[i]) - 1
            asked = [(j, t) for k, s, j, t in guards if (k, s) == (i, at)]
            if results[i] is not None or any(len(waits[j]) <= t for j, t in asked):
                continue
            ready = tuple(waits[i][-1:])
            if asked:
                ready = lax.optimization_barrier(ready + tuple(waits[j][t] for j, t in asked))[:1]
            try:
                waits[i].append(chunk.send(ready)[0])
            except StopIteration as end:
                results[i] = end.value
    return results


def dense(tokens, expert_ids, route_weight, slot_of, swap_flag, w_gate, w_up, w_down):
    tok_rows = tokens.shape[0]
    top_count = expert_ids.shape[1]
    line_bits = (lax.axis_size("expert") // 2).bit_length() - 1
    along = [along_line(2**bit) for bit in range(line_bits)][::-1]
    across = [over_first, over_second]
    routes = [along + across, along + across, along[:1] + across + along[1:]]
    backs = [[3, 2, 1, 0], [3, 2, 1, 0], [2, 3, 1, 0]] if line_bits == 2 else [range(len(along + across))[::-1]]
    step = ROWS_AT_ONCE if tok_rows % ROWS_AT_ONCE == 0 else tok_rows
    owns = packed(tokens, expert_ids, route_weight, step)
    found = []

    def find(after):
        found.append(served_expert(slot_of, swap_flag, after))
        return found[0]

    serve = lambda held, sib: serve_rows(held, sib, found[0], top_count, w_gate[0], w_up[0], w_down[0])
    chunks = [
        chunk_steps(own, routes[i % len(routes)], backs[i % len(backs)], serve, find if i == 2 else None)
        for i, own in enumerate(owns)
    ]
    guards = GUARDS if len(chunks) == 3 and line_bits == 2 else []
    return jnp.concatenate(run_steps(chunks, guards))


def on_device(tokens, expert_ids, *rest):
    slot_of = rest[1]
    ex_count = lax.axis_size("expert")
    capacity = 2 * tokens.shape[0] * expert_ids.shape[1] // slot_of.shape[0]
    paired = lax.axis_size("dp") == 4 and ex_count >= 2 and ex_count & (ex_count - 1) == 0
    serve = dense if capacity >= tokens.shape[0] and paired else sparse
    return serve(tokens, expert_ids, *rest)


def solution(mesh):
    return jax.shard_map(
        on_device,
        mesh=mesh,
        in_specs=(
            P(AXES, None),
            P(AXES, None),
            P(AXES, None),
            P(),
            P(AXES),
            P(AXES, None, None),
            P(AXES, None, None),
            P(AXES, None, None),
        ),
        out_specs=P(AXES, None),
        check_vma=False,
    )
```
